32 devices in a mesh: member: 2 (over y), tile: 4 (over z), nest: 2 (over x), lev: 2 (over core).
Axes of the slice: x: 2, y: 2, z: 4, core: 2. Of those that a mesh axis runs over, the one named last changes fastest.
Arguments:
- parent_field: float32 [10, 2, 256, 512], P('member', None, 'tile', ('nest', 'lev')), parts along dimension 0, may hold values from -6 to 6
- nest_fields: float32 [12, 5, 2, 384, 384], P(('member', 'nest'), None, None, 'tile', 'lev'), parts along dimension 0, may hold values from -6 to 6
- lateral_rate: float32 [5], replicated, may hold values from 0.02 to 0.12
- vertical_rate: float32 [5], replicated, may hold values from 0.02 to 0.12
- centres: int32 [6, 6, 2], P('member'), parts along dimension 0, may hold values from 64 to 448, as said below
- slot_storm: int32 [12], P('member'), parts along dimension 0, may hold values from 0 to 5, each once
Outputs:
- parent_final: float32 [10, 2, 256, 512], P('member', None, 'tile', ('nest', 'lev')), parts along dimension 0
- nest_final: float32 [12, 5, 2, 384, 384], P(('member', 'nest'), None, None, 'tile', 'lev'), parts along dimension 0
The draws below stay inside these ranges and needn't reach their ends.
There are 2 independent parts, one for each index of `member`. The reference program is written for one: setup_inputs(seed, part) draws one part's arguments, and reference() takes and returns one part's arrays. A program takes and returns all parts, laid end to end along the dimension named above; an argument that names none is the same for every part. Nothing has to cross between parts.
Inputs may be any that keep to these rules, and one draw needn't show every extreme that they name: `centres`: from one step to the next the row of a centre changes by 1 to 2 cells in either direction and the column by at most 2 cells; rows stay within 64 to 192 and columns within 64 to 448. `slot_storm`: every storm occupies exactly one nest position.
All inputs are finite; a program needn't handle non-finite values.
Results may differ from the reference program's by a relative error of at most 0.0003.
Values sent between devices are 32-bit elements; how exact they have to be, the bound alone decides.
No kernel may reach another device: no remote copies, remote signals or barrier semaphores. Data moves between devices by JAX's collectives and lax.ppermute only.
A program may use at most 128 MiB of HBM per device.

```python
import math
import jax
import jax.numpy as jnp
from jax import lax

F = 5
LEV = 2
NXP = 256
NYP = 512
FP = 128
NXN = 384
NESTS = 6
BWP = 2
MOVE = 2
STEPS = 2


def draw_centres(key, part):
    half_span = FP // 2
    travel = MOVE * STEPS
    key_rows = jax.random.fold_in(key, 11)
    key_cols = jax.random.fold_in(key, 12)
    key_size = jax.random.fold_in(key, 13)
    key_sign = jax.random.fold_in(key, 14)
    key_drift = jax.random.fold_in(key, 15)
    first_rows = jax.random.randint(key_rows, (NESTS,), half_span + travel, NXP - half_span - travel + 1, dtype=jnp.int32)
    first_cols = jax.random.randint(key_cols, (NESTS,), half_span + travel, NYP - half_span - travel + 1, dtype=jnp.int32)
    row_size = jax.random.randint(key_size, (STEPS, NESTS), 1, MOVE + 1, dtype=jnp.int32)
    row_sign = 2 * jax.random.randint(key_sign, (STEPS, NESTS), 0, 2, dtype=jnp.int32) - 1
    row_moves = row_size * row_sign
    col_moves = jax.random.randint(key_drift, (STEPS, NESTS), -MOVE, MOVE + 1, dtype=jnp.int32)
    first_rows = first_rows.at[0].set(half_span + travel)
    row_moves = row_moves.at[:, 0].set(-MOVE)
    if NXP >= NYP:
        first_rows = first_rows.at[1].set(NXP - half_span - travel)
        row_moves = row_moves.at[:, 1].set(MOVE)
    else:
        first_cols = first_cols.at[1].set(NYP - half_span - travel)
        col_moves = col_moves.at[:, 1].set(MOVE)
    row_track = jnp.concatenate([first_rows[None, :], first_rows[None, :] + jnp.cumsum(row_moves, axis=0)], axis=0)
    col_track = jnp.concatenate([first_cols[None, :], first_cols[None, :] + jnp.cumsum(col_moves, axis=0)], axis=0)
    return jnp.stack([row_track, col_track], axis=-1).astype(jnp.int32)


def block_scale(stream_key, dims, shards, smallest, high):
    loudness = 1.0
    for position, parts in shards:
        steps = jax.random.uniform(jax.random.fold_in(jax.random.fold_in(stream_key, 6), position), (parts,), jnp.float32, smallest / len(shards), high / len(shards))
        loudness = loudness * jnp.repeat(jnp.exp(steps), dims[position] // parts).reshape((-1,) + (1,) * (len(dims) - 1 - position))
    return loudness


def normal_values(stream_key, dims, spread, bound, shards=(), held_as=jnp.bfloat16):
    values = jax.random.normal(stream_key, dims, jnp.float32) * spread
    if len(shards) > 0:
        values = block_scale(stream_key, dims, shards, -0.22, 0.18) * values
    return jnp.clip(values, min=-bound, max=bound).astype(held_as)


def setup_inputs(seed: int = 0, part: int = 0) -> dict:
    seeds = jax.random.split(jax.random.key(seed), 7)
    own_keys = jax.random.split(jax.random.fold_in(seeds[6], part), 7)
    parent_field = normal_values(own_keys[0], (F, LEV, NXP, NYP), 1.0, 6.0, ((2, 4), (3, 4)), jnp.float32)
    nest_fields = normal_values(own_keys[1], (NESTS, F, LEV, NXN, NXN), 1.0, 6.0, ((0, 2), (3, 4), (4, 2)), jnp.float32)
    lateral_rate = jnp.clip(jnp.exp(jax.random.uniform(seeds[2], (F,), jnp.float32, math.log(0.02), math.log(0.12))), 0.02, 0.12)
    vertical_rate = jnp.clip(jnp.exp(jax.random.uniform(seeds[3], (F,), jnp.float32, math.log(0.02), math.log(0.12))), 0.02, 0.12)
    centres = draw_centres(jax.random.fold_in(jax.random.fold_in(seeds[6], part), 71), part)
    slot_storm = jax.random.permutation(own_keys[5], NESTS).astype(jnp.int32)
    return dict(parent_field=parent_field, nest_fields=nest_fields, lateral_rate=lateral_rate, vertical_rate=vertical_rate, centres=centres, slot_storm=slot_storm)


def tendency(field, lateral_rate, vertical_rate):
    padded = jnp.pad(field, ((0, 0), (1, 1), (1, 1), (1, 1)))
    centre = padded[:, 1:-1, 1:-1, 1:-1]
    lateral = padded[:, 1:-1, 2:, 1:-1] + padded[:, 1:-1, :-2, 1:-1] + padded[:, 1:-1, 1:-1, 2:] + padded[:, 1:-1, 1:-1, :-2] - 4.0 * centre
    upright = padded[:, 2:, 1:-1, 1:-1] + padded[:, :-2, 1:-1, 1:-1] - 2.0 * centre
    return lateral_rate[:, None, None, None] * lateral + vertical_rate[:, None, None, None] * upright


def zone_weights():
    nest_span = 3 * FP
    indices = jnp.arange(nest_span, dtype=jnp.int32)
    edge_gap = jnp.minimum(indices, nest_span - 1 - indices)
    distance = jnp.minimum(edge_gap[:, None], edge_gap[None, :])
    weight = jnp.maximum(3 * BWP - distance, 0).astype(jnp.float32) / jnp.float32(3 * BWP)
    inside = (distance >= 1).astype(jnp.float32)
    return weight, inside


def reference(parent_field, nest_fields, lateral_rate, vertical_rate, centres, slot_storm):
    weight, inside = zone_weights()
    nest_span = 3 * FP
    margin = 3 * MOVE
    zero_index = jnp.zeros((), jnp.int32)
    parent_now = parent_field
    nests_now = nest_fields
    for step_index in range(STEPS):
        parent_now = parent_now + tendency(parent_now, lateral_rate, vertical_rate)
        later_pos = centres[step_index + 1][slot_storm]
        before = centres[step_index][slot_storm]
        anchor = (later_pos - FP // 2).astype(jnp.int32)
        offsets = (3 * (later_pos - before)).astype(jnp.int32)
        current = parent_now

        def advance(inputs):
            nest_state, corner, offset = inputs
            window = lax.dynamic_slice(current, (zero_index, zero_index, corner[0], corner[1]), (F, LEV, FP, FP))
            fine_values = jnp.repeat(jnp.repeat(window, 3, axis=2), 3, axis=3)
            padded = jnp.pad(nest_state, ((0, 0), (0, 0), (margin, margin), (margin, margin)))
            shifted = lax.dynamic_slice(padded, (zero_index, zero_index, margin + offset[0], margin + offset[1]), (F, LEV, nest_span, nest_span))
            indices = jnp.arange(nest_span, dtype=jnp.int32)
            row_source = indices + offset[0]
            col_source = indices + offset[1]
            keep_mask = ((row_source >= 0) & (row_source < nest_span))[:, None] & ((col_source >= 0) & (col_source < nest_span))[None, :]
            retained = jnp.where(keep_mask, shifted, fine_values)
            relaxed = retained + weight * (fine_values - retained)
            return relaxed + inside * tendency(relaxed, lateral_rate, vertical_rate)

        nests_now = lax.map(advance, (nests_now, anchor, offsets))
    return parent_now, nests_now
```

```python
import jax
import jax.numpy as jnp
from jax import lax
from jax.experimental import pallas as pl
from jax.experimental.pallas import tpu as pltpu
from jax.sharding import PartitionSpec as P

FP = 128
BWP = 2
MOVE = 2
STEPS = 2
BORDER = 3 * BWP
SPAN = 3 * FP
HALO = STEPS * (3 * MOVE + 1)
PAD = 16
LANES = 128
RING = STEPS
ROW_AT = 32
ZONE_AT = 72
SPLIT = -(FP // 4)
VMEM_LIMIT = 40 * 1024 * 1024

SMEM_SPEC = pl.BlockSpec(memory_space=pltpu.SMEM)
VMEM_SPEC = pl.BlockSpec(memory_space=pltpu.VMEM)


def params(**more):
    return pltpu.CompilerParams(vmem_limit_bytes=VMEM_LIMIT, **more)


def lane_iota(rows=1, lanes=LANES):
    return lax.broadcasted_iota(jnp.int32, (rows, lanes), 1)


def row_iota(rows, lanes=LANES):
    return lax.broadcasted_iota(jnp.int32, (rows, lanes), 0)


def beside(x, first_lane, last_lane):
    left = [pltpu.roll(v, 1, 1) for v in x]
    right = [pltpu.roll(v, LANES - 1, 1) for v in x]
    return [
        jnp.where(first_lane, left[1 - a], left[a]) + jnp.where(last_lane, right[1 - a], right[a])
        for a in range(2)
    ]


def third(values):
    return (values * 21846) >> 16


def strips_kernel(
    fields, rows, cols, storms, centres, slots, lateral, vertical, parent,
    send, keep, ring_out, plain0, plain1, plain2, turned0, turned1, turned2, block, gather,
):
    planes = 2 * fields
    tile_at, tiles = lax.axis_index("tile"), lax.axis_size("tile")
    lev_at, levs = lax.axis_index("lev"), lax.axis_size("lev")
    col_at = lax.axis_index("nest") * levs + lev_at
    col_blocks = lax.axis_size("nest") * levs
    top = 8
    height = rows + 16
    width = cols + 16

    lane = lane_iota()
    first_lane, last_lane = lane == 0, lane == LANES - 1
    row = tile_at * rows + row_iota(height) - top
    tile_cols = (lane, jnp.where(lane < LANES // 2, lane + LANES, lane - LANES))
    within = [
        (
            (row >= 0) & (row < tiles * rows)
            & (col_at * cols + c >= 0) & (col_at * cols + c < col_blocks * cols)
        ).astype(jnp.float32)
        for c in tile_cols
    ]
    plain0[...] = jnp.zeros_like(plain0)
    turned0[...] = jnp.zeros_like(turned0)
    block[...] = jnp.zeros_like(block)
    for p in range(planes):
        plain0[p, 0, top : top + rows, :] = parent[p // 2, p % 2]
        block[ROW_AT : ROW_AT + rows, :] = parent[p // 2, p % 2]
        turned0[p, top : top + cols, :] = block[...].T

    inner = slice(1, height - 1)

    def plain_step(source, target, mask):
        for f in range(fields):
            lat, ver = lateral[f], vertical[f]
            for v in range(2):
                x = [source[2 * f + v, a, inner, :] for a in range(2)]
                sideways = beside(x, first_lane, last_lane)
                for a in range(2):
                    near = (
                        sideways[a]
                        + source[2 * f + v, a, 2:height, :]
                        + source[2 * f + v, a, 0 : height - 2, :]
                    )
                    other = source[2 * f + 1 - v, a, inner, :]
                    new = x[a] + lat * (near - 4.0 * x[a]) + ver * (other - 2.0 * x[a])
                    if mask is not None:
                        new = new * mask[a][inner, :]
                    target[2 * f + v, a, inner, :] = new
                    for edge in (0, height - 1):
                        target[2 * f + v, a, edge : edge + 1, :] = jnp.zeros(
                            (1, LANES), jnp.float32
                        )

    plain_step(plain0, plain1, within)
    plain_step(plain1, plain2, None)

    row_t = tile_at * rows + lane_iota() - ROW_AT
    col_t = col_at * cols + row_iota(width) - top
    within_t = (
        (row_t >= 0) & (row_t < tiles * rows) & (col_t >= 0) & (col_t < col_blocks * cols)
    ).astype(jnp.float32)

    def turned_step(source, target, mask):
        for f in range(fields):
            lat, ver = lateral[f], vertical[f]
            for v in range(2):
                x = source[2 * f + v, 1 : width - 1, :]
                near = (
                    source[2 * f + v, 2:width, :]
                    + source[2 * f + v, 0 : width - 2, :]
                    + pltpu.roll(x, 1, 1)
                    + pltpu.roll(x, LANES - 1, 1)
                )
                other = source[2 * f + 1 - v, 1 : width - 1, :]
                new = x + lat * (near - 4.0 * x) + ver * (other - 2.0 * x)
                if mask is not None:
                    new = new * mask[1 : width - 1, :]
                target[2 * f + v, 1 : width - 1, :] = new
                target[2 * f + v, 0:1, :] = jnp.zeros((1, LANES), jnp.float32)
                target[2 * f + v, width - 1 : width, :] = jnp.zeros((1, LANES), jnp.float32)

    turned_step(turned0, turned1, within_t)
    turned_step(turned1, turned2, None)

    share = storms * STEPS * planes * BWP
    for j in range(storms):
        storm = slots[j]
        for s in range(STEPS):
            at = (j * STEPS + s) * planes * BWP
            corner_row = centres[s + 1, storm, 0] - FP // 2 - tile_at * rows
            corner_col = centres[s + 1, storm, 1] - FP // 2 - col_at * cols
            plain = (plain1, plain2)[s]
            turned = (turned1, turned2)[s]
            first = jnp.where(corner_row >= SPLIT, corner_row, corner_row + FP - BWP)
            first = jnp.clip(first + top, 0, height - BWP)
            for p in range(planes):
                for a in range(2):
                    gather[a, BWP * p : BWP * (p + 1), :] = plain[p, a, pl.ds(first, BWP), :]
            shift = (64 * LANES - corner_col) % LANES
            window = [pltpu.roll(gather[a], shift, 1) for a in range(2)]
            place = lane + corner_col
            main = (place >= 0) & (place < cols)
            rim = (place >= -RING) & (place < cols + RING)
            window = jnp.where(main, window[0], jnp.where(rim, window[1], 0.0))[: planes * BWP]
            send[at : at + planes * BWP, :] = window
            keep[at : at + planes * BWP, :] = window
            mine = corner_col + (FP - BWP) * lev_at
            theirs = corner_col + (FP - BWP) * (levs - 1 - lev_at)
            for target, start in ((keep, mine), (send, theirs)):
                start = jnp.clip(start + top, 0, width - BWP)
                for p in range(planes):
                    target[share + at + BWP * p : share + at + BWP * (p + 1), :] = turned[
                        p, pl.ds(start, BWP), :
                    ]
    for p in range(planes):
        send[2 * share + BWP * p : 2 * share + BWP * (p + 1), :] = turned2[p, top - RING : top, :]
        at = 2 * share + planes * BWP + BWP * p
        send[at : at + BWP, :] = turned2[p, top + cols : top + cols + RING, :]
        ring_out[p] = turned2[p, top : top + cols, :]


def pair_up_kernel(own, share, rim, keep, got, kept, *sends):
    nest_at = lax.axis_index("nest")
    lev_at = lax.axis_index("lev")
    for k in range(len(sends) + 1):
        group = lax.bitwise_xor(nest_at, k)
        target = kept if k == 0 else sends[k - 1]
        for part in range(2):
            rows = pl.ds(pl.multiple_of(part * share + group * own, 8), own)
            target[part * own : (part + 1) * own, :] = keep[rows, :] + got[rows, :]
        if k > 0:
            west = got[2 * share : 2 * share + rim, :]
            east = got[2 * share + rim : 2 * share + 2 * rim, :]
            target[2 * own : 2 * own + rim, :] = jnp.where(lev_at == 0, east, west)


def aim_kernel(
    fields, rows, cols, strip_rows, strip_cols, slot_count, moves, share, touching,
    centres, slots, ring, first_got, kept, *refs,
):
    crossing = lax.axis_size("nest") - 1
    nest_gots, rest = refs[:crossing], refs[crossing:]
    partial, zone_self, zone_sends, total = rest[0], rest[1], rest[2:-1], rest[-1]
    planes = 2 * fields
    rim = planes * BWP
    own = slot_count * STEPS * rim
    tile_at, tiles = lax.axis_index("tile"), lax.axis_size("tile")
    nest_at = lax.axis_index("nest")
    lev_at = lax.axis_index("lev")

    sums = kept[...]
    for got in nest_gots:
        sums = sums + got[0 : 2 * own, :]
    total[...] = sums

    lane = lane_iota()
    col_base = lev_at * (strip_cols // 3 - 3)
    for j in range(slot_count):
        storm = slots[nest_at * slot_count + j]
        at = j * STEPS * rim
        both = STEPS * rim
        strip = pltpu.roll(total[at : at + both, :], (LANES - col_base) % LANES, 1)
        side = total[own + at : own + at + both, :]
        second = row_iota(both) >= rim
        origins = [centres[s + 1, storm, 0] - FP // 2 - tile_at * rows for s in range(STEPS)]
        for k in moves:
            dest = lax.bitwise_xor(tile_at, k)
            parts = []
            for s in range(STEPS):
                south = origins[s] >= SPLIT
                wanted = ((dest == 0) & south) | ((dest == tiles - 1) & jnp.logical_not(south))
                offset = ROW_AT + origins[s] + (strip_rows // 3) * dest - 3 - ZONE_AT
                source = lane + offset
                fits = (source >= ROW_AT - RING) & (source < ROW_AT + rows + RING)
                turned = pltpu.roll(side, (64 * LANES - offset) % LANES, 1)
                turned = jnp.where(fits, turned, 0.0)
                parts.append(
                    jnp.where(lane < ZONE_AT, strip * wanted.astype(jnp.float32), turned)
                )
            target = zone_self if k == 0 else zone_sends[moves.index(k) - 1]
            target[at : at + both, :] = jnp.where(second, parts[1], parts[0])

    from_west = first_got[2 * share + rim : 2 * share + 2 * rim, :]
    from_east = first_got[2 * share : 2 * share + rim, :]
    far_west = jnp.zeros((rim, LANES), jnp.float32)
    far_east = jnp.zeros((rim, LANES), jnp.float32)
    for i, got in enumerate(nest_gots):
        other = lax.bitwise_xor(nest_at, i + 1)
        edge = got[2 * own : 2 * own + rim, :]
        far_west = far_west + jnp.where(other == nest_at - 1, edge, 0.0)
        far_east = far_east + jnp.where(other == nest_at + 1, edge, 0.0)
    from_west = jnp.where(lev_at == 0, far_west, from_west)
    from_east = jnp.where(lev_at == 0, from_east, far_east)
    for p in range(planes):
        two = slice(BWP * p, BWP * (p + 1))
        total[0:cols, :] = ring[p]
        total[0:RING, :] = total[0:RING, :] + from_west[two]
        total[cols - RING : cols, :] = total[cols - RING : cols, :] + from_east[two]
        total[0:LANES, :] = total[0:cols, :].T
        partial[p // 2, p % 2] = total[ROW_AT : ROW_AT + rows, :]
        below = total[ROW_AT - RING : ROW_AT, :]
        above = total[ROW_AT + rows : ROW_AT + rows + RING, :]
        for i, k in enumerate(moves[1:]):
            if k in touching:
                dest = lax.bitwise_xor(tile_at, k)
                zone_sends[i][own + BWP * p : own + BWP * (p + 1), :] = jnp.where(
                    dest > tile_at, above, below
                )


def edge_rows_kernel(fields, strip_rows, nests, to_pair, to_cross):
    even = lax.rem(lax.axis_index("tile"), 2) == 0
    for f in range(fields):
        for v in range(2):
            low = nests[0, f, v, 0:HALO, 0:LANES]
            high = nests[0, f, v, strip_rows - HALO : strip_rows, 0:LANES]
            at = (2 * f + v) * HALO
            to_pair[0, at : at + HALO, :] = jnp.where(even, high, low)
            to_cross[0, at : at + HALO, :] = jnp.where(even, low, high)
        half = nests.shape[4] - LANES
        low = jnp.concatenate([nests[0, f, v, 0:HALO, LANES : LANES + half] for v in range(2)], 1)
        high = jnp.concatenate(
            [nests[0, f, v, strip_rows - HALO : strip_rows, LANES : LANES + half] for v in range(2)],
            1,
        )
        at = (2 * fields + f) * HALO
        to_pair[0, at : at + HALO, :] = jnp.where(even, high, low)
        to_cross[0, at : at + HALO, :] = jnp.where(even, low, high)


def edge_cols_kernel(fields, strip_rows, slot_count, nests, pair, cross, packed, wide):
    even = lax.rem(lax.axis_index("tile"), 2) == 0
    west_most = lax.axis_index("lev") == 0
    planes = 2 * fields
    half = nests.shape[4] - LANES
    packed[...] = jnp.zeros_like(packed)
    wide[...] = jnp.zeros_like(wide)
    lane = lane_iota()
    for q in range(slot_count * planes):
        j, f, v = q // planes, (q % planes) // 2, q % 2
        spot = (q % 8) * 16
        mask = (lane >= spot) & (lane < spot + HALO)
        wide[:, 0:half] = nests[j, f, v, :, LANES : LANES + half]
        cells = jnp.where(west_most, wide[...], nests[j, f, v, :, 0:LANES])
        shift = jnp.where(west_most, spot + 2 * LANES - (half - HALO), spot + 2 * LANES) % LANES
        cells = pltpu.roll(cells, shift, 1)
        rows = slice(PAD, PAD + strip_rows)
        packed[q // 8, rows, :] = jnp.where(mask, cells, packed[q // 8, rows, :])
        at, rest = (2 * f + v) * HALO, (2 * fields + f) * HALO
        shift = (
            jnp.where(west_most, spot + 2 * LANES - (half - HALO) - half * v, spot + 2 * LANES) % LANES
        )
        halos = []
        for got in (pair, cross):
            cells = jnp.where(west_most, got[j, rest : rest + HALO, :], got[j, at : at + HALO, :])
            halos.append(pltpu.roll(cells, shift, 1))
        high = jnp.where(even, halos[0], halos[1])
        low = jnp.where(even, halos[1], halos[0])
        rows = slice(PAD - HALO, PAD)
        packed[q // 8, rows, :] = jnp.where(mask, low, packed[q // 8, rows, :])
        rows = slice(PAD + strip_rows, PAD + strip_rows + HALO)
        packed[q // 8, rows, :] = jnp.where(mask, high, packed[q // 8, rows, :])


def nests_kernel(
    fields, strip_rows, strip_cols, rows, moves, touching,
    centres, slots, lateral, vertical, nests, pair, cross, packed, partial, zone_self, *refs,
):
    count = len(moves) - 1
    zone_gots = refs[:count]
    nest_out, parent_out = refs[count : count + 2]
    cells, mixed, weight, inner, strips, sides = refs[count + 2 :]
    planes = 2 * fields
    rim = planes * BWP
    both = STEPS * rim
    half = strip_cols - LANES
    height = strip_rows + 2 * PAD
    tile_at, tiles = lax.axis_index("tile"), lax.axis_size("tile")
    nest_at = lax.axis_index("nest")
    lev_at = lax.axis_index("lev")
    even = lax.rem(tile_at, 2) == 0
    j = pl.program_id(0)
    own = pl.num_programs(0) * both

    @pl.when(j == 0)
    def _():
        below = jnp.zeros((rim, LANES), jnp.float32)
        above = jnp.zeros((rim, LANES), jnp.float32)
        for i, k in enumerate(moves[1:]):
            if k in touching:
                other = lax.bitwise_xor(tile_at, k)
                edge = zone_gots[i][zone_self.shape[0] : zone_self.shape[0] + rim, :]
                below = below + jnp.where(other == tile_at - 1, edge, 0.0)
                above = above + jnp.where(other == tile_at + 1, edge, 0.0)
        for p in range(planes):
            f, v = p // 2, p % 2
            two = slice(BWP * p, BWP * (p + 1))
            parent_out[f, v] = partial[f, v]
            parent_out[f, v, 0:RING, :] = partial[f, v, 0:RING, :] + below[two]
            parent_out[f, v, rows - RING : rows, :] = partial[f, v, rows - RING : rows, :] + above[two]

    storm = slots[nest_at * pl.num_programs(0) + j]
    spots = [[centres[n, storm, d] for d in range(2)] for n in range(STEPS + 1)]
    down = [3 * (spots[n + 1][0] - spots[0][0]) for n in range(STEPS)]
    right = [3 * (spots[n + 1][1] - spots[0][1]) for n in range(STEPS)]

    lane = lane_iota()
    row_from = tile_at * strip_rows - PAD
    col_from = lev_at * strip_cols
    gap = (half + LANES) // 2
    lane_cols = (lane, jnp.where(lane < gap, lane + LANES, lane - LANES))

    at = pl.multiple_of(j * both, 8)
    zone = zone_self[pl.ds(at, both), :]
    for got in zone_gots:
        zone = zone + got[pl.ds(at, both), :]
    second = row_iota(both) >= rim
    col_base = lev_at * (strip_cols // 3 - 3)
    for a in range(2):
        picks = []
        for s in range(STEPS):
            fine = jnp.clip(lane_cols[a] + col_from - right[s], 0, SPAN - 1)
            picks.append(jnp.clip(third(fine) - col_base, 0, ZONE_AT - 1))
        pick = jnp.where(second, picks[1], picks[0])
        strips[a] = jnp.take_along_axis(zone, pick, axis=1)
    picks = []
    for s in range(STEPS):
        fine = jnp.clip(lane + row_from - down[s], 0, SPAN - 1)
        picks.append(
            jnp.clip(third(fine) - ((strip_rows // 3) * tile_at - 3) + ZONE_AT, ZONE_AT, LANES - 1)
        )
    pick = jnp.where(second, picks[1], picks[0])
    sides[:, 0:both] = jnp.take_along_axis(zone, pick, axis=1).T

    i_rows = row_iota(height) + row_from
    keep = [None, None]
    for s in range(STEPS):
        for a in range(2):
            i = i_rows - down[s]
            c = lane_cols[a] + col_from - right[s]
            distance = jnp.minimum(jnp.minimum(i, SPAN - 1 - i), jnp.minimum(c, SPAN - 1 - c))
            if s == 0:
                i0, c0 = i_rows, lane_cols[a] + col_from
                stays = (
                    (i0 >= 0) & (i0 < SPAN) & (c0 >= 0) & (c0 < SPAN)
                )
            else:
                stays = keep[a]
            share = jnp.clip(BORDER - distance, 0, BORDER).astype(jnp.float32) / jnp.float32(BORDER)
            weight[s, a] = jnp.where(stays, share, 1.0)
            inner[s, a] = (distance >= 1).astype(jnp.float32)
            keep[a] = distance >= 0

    chunk = 32 if height % 32 == 0 else 8
    first_lane, last_lane = lane == 0, lane == LANES - 1
    cells[...] = jnp.zeros_like(cells)

    for f in range(fields):
        lat, ver = lateral[f], vertical[f]
        for v in range(2):
            q = j * planes + 2 * f + v
            a_row, rest = (2 * f + v) * HALO, (2 * fields + f) * HALO
            cells[v, 0, PAD : PAD + strip_rows, :] = nests[0, f, v, :, 0:LANES]
            cells[v, 1, PAD : PAD + strip_rows, 0:half] = nests[0, f, v, :, LANES : LANES + half]
            ends = []
            for got in (pair, cross):
                tail = got[0, rest : rest + HALO, :]
                if v == 1:
                    tail = pltpu.roll(tail, LANES - half, 1)
                ends.append((got[0, a_row : a_row + HALO, :], tail))
            for a in range(2):
                low = jnp.where(even, ends[1][a], ends[0][a])
                high = jnp.where(even, ends[0][a], ends[1][a])
                lanes = slice(0, LANES if a == 0 else half)
                cells[v, a, PAD - HALO : PAD, lanes] = low[:, lanes]
                cells[v, a, PAD + strip_rows : PAD + strip_rows + HALO, lanes] = high[:, lanes]
            spot = lax.rem(q, 8) * 16
            goal = jnp.where(lev_at == 0, half, LANES - HALO)
            got = pltpu.roll(packed[lax.div(q, 8)], (goal - spot + 2 * LANES) % LANES, 1)
            got = jnp.where((lane >= goal) & (lane < goal + HALO), got, 0.0)
            cells[v, 1, :, half:LANES] = got[:, half:LANES]

        for s in range(STEPS):
            edge_cols = [
                (lane_cols[a] + col_from - right[s] < 3)
                | ((lane_cols[a] + col_from - right[s] >= SPAN // 2)
                   & (lane_cols[a] + col_from - right[s] < SPAN - 3))
                for a in range(2)
            ]
            for c in range(0, height, chunk):
                i = row_iota(chunk) + (row_from + c - down[s])
                in_rows = (i < BORDER) | (i >= SPAN - BORDER)
                early = (i < 3) | ((i >= SPAN // 2) & (i < SPAN - 3))
                for v in range(2):
                    n = s * rim + (2 * f + v) * BWP
                    near = jnp.broadcast_to(sides[c : c + chunk, n : n + 1], (chunk, LANES))
                    far = jnp.broadcast_to(sides[c : c + chunk, n + 1 : n + 2], (chunk, LANES))
                    for a in range(2):
                        side = jnp.where(edge_cols[a], near, far)
                        strip = jnp.where(early, strips[a, n : n + 1, :], strips[a, n + 1 : n + 2, :])
                        driving = jnp.where(in_rows, strip, side)
                        w = weight[s, a, c : c + chunk, :]
                        x = cells[v, a, c : c + chunk, :]
                        mixed[v, a, 8 + c : 8 + c + chunk, :] = (1.0 - w) * x + w * driving
            for c in range(0, height, chunk):
                x = [[mixed[v, a, 8 + c : 8 + c + chunk, :] for a in range(2)] for v in range(2)]
                for v in range(2):
                    sideways = beside(x[v], first_lane, last_lane)
                    for a in range(2):
                        near = (
                            sideways[a]
                            + mixed[v, a, 7 + c : 7 + c + chunk, :]
                            + mixed[v, a, 9 + c : 9 + c + chunk, :]
                        )
                        change = lat * (near - 4.0 * x[v][a]) + ver * (x[1 - v][a] - 2.0 * x[v][a])
                        cells[v, a, c : c + chunk, :] = (
                            x[v][a] + inner[s, a, c : c + chunk, :] * change
                        )

        start = PAD + down[STEPS - 1]
        slide = right[STEPS - 1]
        for v in range(2):
            moved = [
                pltpu.roll(cells[v, a, pl.ds(start, strip_rows), :], (LANES - slide) % LANES, 1)
                for a in range(2)
            ]
            same = (lane + slide >= 0) & (lane + slide < LANES)
            nest_out[0, f, v, :, 0:LANES] = jnp.where(same, moved[0], moved[1])
            nest_out[0, f, v, :, LANES : LANES + half] = jnp.where(same, moved[1], moved[0])[:, :half]


def per_device(parent_field, nest_fields, lateral_rate, vertical_rate, centres, slot_storm):
    fields, _, rows, cols = parent_field.shape
    slot_count, _, _, strip_rows, strip_cols = nest_fields.shape
    storms = slot_storm.shape[0]
    tiles, groups, levs = lax.axis_size("tile"), lax.axis_size("nest"), lax.axis_size("lev")
    planes = 2 * fields
    rim = planes * BWP
    share = storms * STEPS * rim
    own = slot_count * STEPS * rim
    height = strip_rows + 2 * PAD
    half = strip_cols - LANES
    f32 = jnp.float32

    def shaped(*dims):
        return jax.ShapeDtypeStruct(dims, f32)

    pair_list = [(t, t ^ 1) for t in range(tiles) if t ^ 1 < tiles]
    cross_list = [(t, t - 1 if t % 2 == 0 else t + 1) for t in range(1, tiles - 1)]
    edge_block = pl.BlockSpec((1, 3 * fields * HALO, LANES), lambda j: (j, 0, 0))
    nest_block = pl.BlockSpec((1, fields, 2, strip_rows, strip_cols), lambda j: (j, 0, 0, 0, 0))
    to_pair, to_cross = pl.pallas_call(
        lambda *refs: edge_rows_kernel(fields, strip_rows, *refs),
        grid=(slot_count,),
        in_specs=[nest_block],
        out_specs=[edge_block, edge_block],
        out_shape=[shaped(slot_count, 3 * fields * HALO, LANES)] * 2,
        compiler_params=params(),
        name="edge_rows",
    )(nest_fields)
    pair = lax.ppermute(to_pair, "tile", pair_list)
    cross = lax.ppermute(to_cross, "tile", cross_list)

    send, keep, ring = pl.pallas_call(
        lambda *refs: strips_kernel(fields, rows, cols, storms, *refs),
        in_specs=[SMEM_SPEC] * 4 + [VMEM_SPEC],
        out_specs=[VMEM_SPEC] * 3,
        out_shape=[shaped(2 * share + 2 * rim, LANES), shaped(2 * share, LANES), shaped(planes, cols, LANES)],
        scratch_shapes=[pltpu.VMEM((planes, 2, rows + 16, LANES), f32)] * 3
        + [pltpu.VMEM((planes, cols + 16, LANES), f32)] * 3
        + [pltpu.VMEM((LANES, LANES), f32), pltpu.VMEM((2, 24, LANES), f32)],
        compiler_params=params(),
        name="strips",
    )(centres, slot_storm, lateral_rate, vertical_rate, parent_field)
    got = lax.ppermute(send, "lev", [(l, l ^ 1) for l in range(levs)])

    kept, *sends = pl.pallas_call(
        lambda *refs: pair_up_kernel(own, share, rim, *refs),
        in_specs=[VMEM_SPEC] * 2,
        out_specs=[VMEM_SPEC] * groups,
        out_shape=[shaped(2 * own, LANES)] + [shaped(2 * own + rim, LANES)] * (groups - 1),
        compiler_params=params(),
        name="pair_up",
    )(keep, got)
    nest_gots = [
        lax.ppermute(x, "nest", [(n, n ^ (i + 1)) for n in range(groups)])
        for i, x in enumerate(sends)
    ]

    def holds(source, dest):
        low = max((strip_rows // 3) * dest - 3, 0)
        high = tiles * rows - FP + min((strip_rows // 3) * (dest + 1) + 3, FP)
        return rows * source - RING < high and rows * (source + 1) + RING > low

    routes = {}
    for k in range(1, tiles):
        pairs = [
            (t, t ^ k)
            for t in range(tiles)
            if t ^ k < tiles and (holds(t, t ^ k) or holds(t ^ k, t) or abs(t - (t ^ k)) == 1)
        ]
        if pairs:
            routes[k] = pairs
    touching = tuple(k for k in routes if any(abs(a - b) == 1 for a, b in routes[k]))
    moves = (0, *routes)
    zone_shapes = [shaped(own + (rim if k in touching else 0), LANES) for k in moves]
    partial, zone_self, *zone_sends = pl.pallas_call(
        lambda *refs: aim_kernel(
            fields, rows, cols, strip_rows, strip_cols, slot_count, moves, share, touching, *refs
        ),
        in_specs=[SMEM_SPEC] * 2 + [VMEM_SPEC] * (2 + groups),
        out_specs=[VMEM_SPEC] * (1 + len(moves)),
        out_shape=[shaped(fields, 2, rows, cols), *zone_shapes],
        scratch_shapes=[pltpu.VMEM((2 * own, LANES), f32)],
        compiler_params=params(),
        name="aim",
    )(centres, slot_storm, ring, got, kept, *nest_gots)
    zone_gots = [lax.ppermute(x, "tile", routes[k]) for k, x in zip(moves[1:], zone_sends)]

    bundles = -(-slot_count * planes // 8)
    packed = pl.pallas_call(
        lambda *refs: edge_cols_kernel(fields, strip_rows, slot_count, *refs),
        in_specs=[VMEM_SPEC] * 3,
        out_specs=VMEM_SPEC,
        out_shape=shaped(bundles, height, LANES),
        scratch_shapes=[pltpu.VMEM((strip_rows, LANES), f32)],
        compiler_params=params(),
        name="edge_cols",
    )(nest_fields, pair, cross)
    packed = lax.ppermute(packed, "lev", [(l, l ^ 1) for l in range(levs)])

    whole = lambda *dims: pl.BlockSpec(dims, lambda j: (0,) * len(dims))
    nest_final, parent_final = pl.pallas_call(
        lambda *refs: nests_kernel(fields, strip_rows, strip_cols, rows, moves, touching, *refs),
        grid=(slot_count,),
        in_specs=[SMEM_SPEC] * 4
        + [nest_block, edge_block, edge_block, whole(bundles, height, LANES), whole(fields, 2, rows, cols)]
        + [whole(*s.shape) for s in zone_shapes],
        out_specs=[nest_block, whole(fields, 2, rows, cols)],
        out_shape=[
            jax.ShapeDtypeStruct(nest_fields.shape, f32),
            jax.ShapeDtypeStruct(parent_field.shape, f32),
        ],
        scratch_shapes=[
            pltpu.VMEM((2, 2, height, LANES), f32),
            pltpu.VMEM((2, 2, height + 16, LANES), f32),
            pltpu.VMEM((STEPS, 2, height, LANES), f32),
            pltpu.VMEM((STEPS, 2, height, LANES), f32),
            pltpu.VMEM((2, STEPS * rim, LANES), f32),
            pltpu.VMEM((LANES, LANES), f32),
        ],
        compiler_params=params(dimension_semantics=("arbitrary",)),
        name="nests",
    )(
        centres, slot_storm, lateral_rate, vertical_rate,
        nest_fields, pair, cross, packed, partial, zone_self, *zone_gots,
    )
    return (parent_final, nest_final)


def solution(mesh):
    placed = (
        P("member", None, "tile", ("nest", "lev")),
        P(("member", "nest"), None, None, "tile", "lev"),
        P(),
        P(),
        P("member", None, None),
        P("member"),
    )
    return jax.shard_map(
        per_device,
        mesh=mesh,
        in_specs=placed,
        out_specs=(
            P("member", None, "tile", ("nest", "lev")),
            P(("member", "nest"), None, None, "tile", "lev"),
        ),
        check_vma=False,
    )
```

```python
import jax
import jax.numpy as jnp
from jax import lax
from jax.experimental import pallas as pl
from jax.experimental.pallas import tpu as pltpu
from jax.sharding import PartitionSpec as P

FP = 128
BWP = 2
MOVE = 2
STEPS = 2
BORDER = 3 * BWP
SPAN = 3 * FP
HALO = STEPS * (3 * MOVE + 1)
PAD = 16
LANES = 128
PLAN = 8
RING = STEPS
ROW_AT = 32
ZONE_AT = 72
SPLIT = -(FP // 4)
SLOT = 24
VMEM_LIMIT = 40 * 1024 * 1024

SMEM_SPEC = pl.BlockSpec(memory_space=pltpu.SMEM)
VMEM_SPEC = pl.BlockSpec(memory_space=pltpu.VMEM)
HBM_SPEC = pl.BlockSpec(memory_space=pltpu.HBM)
ANY_SPEC = pl.BlockSpec(memory_space=pl.ANY)


def params(**more):
    return pltpu.CompilerParams(vmem_limit_bytes=VMEM_LIMIT, **more)


def lane_iota(rows=1, lanes=LANES):
    return lax.broadcasted_iota(jnp.int32, (rows, lanes), 1)


def row_iota(rows, lanes=LANES):
    return lax.broadcasted_iota(jnp.int32, (rows, lanes), 0)


def beside(x, first_lane, last_lane):
    left = [pltpu.roll(v, 1, 1) for v in x]
    right = [pltpu.roll(v, LANES - 1, 1) for v in x]
    return [
        jnp.where(first_lane, left[1 - a], left[a]) + jnp.where(last_lane, right[1 - a], right[a])
        for a in range(2)
    ]


def third(values):
    return (values * 21846) >> 16


def strips_kernel(
    fields, rows, cols, storms, slot_count, strip_rows,
    centres_in, slots_in, lateral_in, vertical_in, parent_in, nests,
    send, keep, ring_out, to_pair, to_cross, plan, rates,
    plain0, plain1, plain2, turned0, turned1, turned2, block, gather,
    centres, slots, lateral, vertical, parent, low_rows, high_rows, arrived,
):
    sources = (
        (centres_in, centres),
        (slots_in, slots),
        (lateral_in, lateral),
        (vertical_in, vertical),
        (parent_in, parent),
        (nests.at[:, :, :, pl.ds(0, PAD), :], low_rows),
        (nests.at[:, :, :, pl.ds(strip_rows - PAD, PAD), :], high_rows),
    )
    copies = [
        pltpu.make_async_copy(source, target, arrived.at[i])
        for i, (source, target) in enumerate(sources)
    ]
    for copy in copies:
        copy.start()
    planes = 2 * fields
    tile_at, tiles = lax.axis_index("tile"), lax.axis_size("tile")
    lev_at, levs = lax.axis_index("lev"), lax.axis_size("lev")
    col_at = lax.axis_index("nest") * levs + lev_at
    col_blocks = lax.axis_size("nest") * levs
    top = 8
    height = rows + 16
    width = cols + 16

    lane = lane_iota()
    first_lane, last_lane = lane == 0, lane == LANES - 1
    row = tile_at * rows + row_iota(height) - top
    tile_cols = (lane, jnp.where(lane < LANES // 2, lane + LANES, lane - LANES))
    within = [
        (
            (row >= 0) & (row < tiles * rows)
            & (col_at * cols + c >= 0) & (col_at * cols + c < col_blocks * cols)
        ).astype(jnp.float32)
        for c in tile_cols
    ]
    plain0[...] = jnp.zeros_like(plain0)
    turned0[...] = jnp.zeros_like(turned0)
    block[...] = jnp.zeros_like(block)
    for copy in copies[:5]:
        copy.wait()
    for f in range(fields):
        rates[f : f + 1, :] = jnp.full((1, LANES), lateral[f], jnp.float32)
        rates[fields + f : fields + f + 1, :] = jnp.full((1, LANES), vertical[f], jnp.float32)
    for j in range(slot_count):
        storm = slots[lax.axis_index("nest") * slot_count + j]
        at = [[centres[n, d, storm] for d in range(2)] for n in range(STEPS + 1)]
        for d in range(2):
            plan[j * PLAN + d] = at[d + 1][0] - FP // 2
            plan[j * PLAN + 2 + d] = 3 * (at[STEPS][d] - at[0][d])
            plan[j * PLAN + 4 + d] = 3 * (at[STEPS][d] - at[STEPS - 1][d])
    for p in range(planes):
        plain0[p, 0, top : top + rows, :] = parent[p // 2, p % 2]
        block[ROW_AT : ROW_AT + rows, :] = parent[p // 2, p % 2]
        turned0[p, top : top + cols, :] = block[...].T

    inner = slice(1, height - 1)

    def plain_step(source, target, mask):
        for f in range(fields):
            lat, ver = lateral[f], vertical[f]
            for v in range(2):
                x = [source[2 * f + v, a, inner, :] for a in range(2)]
                sideways = beside(x, first_lane, last_lane)
                for a in range(2):
                    near = (
                        sideways[a]
                        + source[2 * f + v, a, 2:height, :]
                        + source[2 * f + v, a, 0 : height - 2, :]
                    )
                    other = source[2 * f + 1 - v, a, inner, :]
                    new = x[a] + lat * (near - 4.0 * x[a]) + ver * (other - 2.0 * x[a])
                    if mask is not None:
                        new = new * mask[a][inner, :]
                    target[2 * f + v, a, inner, :] = new
                    for edge in (0, height - 1):
                        target[2 * f + v, a, edge : edge + 1, :] = jnp.zeros(
                            (1, LANES), jnp.float32
                        )

    plain_step(plain0, plain1, within)
    plain_step(plain1, plain2, None)

    row_t = tile_at * rows + lane_iota() - ROW_AT
    col_t = col_at * cols + row_iota(width) - top
    within_t = (
        (row_t >= 0) & (row_t < tiles * rows) & (col_t >= 0) & (col_t < col_blocks * cols)
    ).astype(jnp.float32)

    def turned_step(source, target, mask):
        for f in range(fields):
            lat, ver = lateral[f], vertical[f]
            for v in range(2):
                x = source[2 * f + v, 1 : width - 1, :]
                near = (
                    source[2 * f + v, 2:width, :]
                    + source[2 * f + v, 0 : width - 2, :]
                    + pltpu.roll(x, 1, 1)
                    + pltpu.roll(x, LANES - 1, 1)
                )
                other = source[2 * f + 1 - v, 1 : width - 1, :]
                new = x + lat * (near - 4.0 * x) + ver * (other - 2.0 * x)
                if mask is not None:
                    new = new * mask[1 : width - 1, :]
                target[2 * f + v, 1 : width - 1, :] = new
                target[2 * f + v, 0:1, :] = jnp.zeros((1, LANES), jnp.float32)
                target[2 * f + v, width - 1 : width, :] = jnp.zeros((1, LANES), jnp.float32)

    turned_step(turned0, turned1, within_t)
    turned_step(turned1, turned2, None)

    share = storms * STEPS * planes * BWP
    for j in range(storms):
        storm = slots[j]
        for s in range(STEPS):
            at = (j * STEPS + s) * planes * BWP
            corner_row = centres[s + 1, 0, storm] - FP // 2 - tile_at * rows
            corner_col = centres[s + 1, 1, storm] - FP // 2 - col_at * cols
            plain = (plain1, plain2)[s]
            turned = (turned1, turned2)[s]
            first = jnp.where(corner_row >= SPLIT, corner_row, corner_row + FP - BWP)
            first = jnp.clip(first + top, 0, height - BWP)
            for p in range(planes):
                for a in range(2):
                    gather[a, BWP * p : BWP * (p + 1), :] = plain[p, a, pl.ds(first, BWP), :]
            shift = (64 * LANES - corner_col) % LANES
            window = [pltpu.roll(gather[a], shift, 1) for a in range(2)]
            place = lane + corner_col
            main = (place >= 0) & (place < cols)
            rim = (place >= -RING) & (place < cols + RING)
            window = jnp.where(main, window[0], jnp.where(rim, window[1], 0.0))[: planes * BWP]
            send[at : at + planes * BWP, :] = window
            keep[at : at + planes * BWP, :] = window
            mine = corner_col + (FP - BWP) * lev_at
            theirs = corner_col + (FP - BWP) * (levs - 1 - lev_at)
            for target, start in ((keep, mine), (send, theirs)):
                start = jnp.clip(start + top, 0, width - BWP)
                for p in range(planes):
                    target[share + at + BWP * p : share + at + BWP * (p + 1), :] = turned[
                        p, pl.ds(start, BWP), :
                    ]
    for p in range(planes):
        send[2 * share + BWP * p : 2 * share + BWP * (p + 1), :] = turned2[p, top - RING : top, :]
        at = 2 * share + planes * BWP + BWP * p
        send[at : at + BWP, :] = turned2[p, top + cols : top + cols + RING, :]
        ring_out[p] = turned2[p, top : top + cols, :]

    for copy in copies[5:]:
        copy.wait()
    even = lax.rem(tile_at, 2) == 0
    half = nests.shape[4] - LANES
    lows, highs, tail = slice(0, HALO), slice(PAD - HALO, PAD), slice(LANES, LANES + half)
    for j in range(slot_count):
        for f in range(fields):
            for v in range(2):
                low, high = low_rows[j, f, v, lows, 0:LANES], high_rows[j, f, v, highs, 0:LANES]
                at = (2 * f + v) * HALO
                to_pair[j, at : at + HALO, :] = jnp.where(even, high, low)
                to_cross[j, at : at + HALO, :] = jnp.where(even, low, high)
            low = jnp.concatenate([low_rows[j, f, v, lows, tail] for v in range(2)], 1)
            high = jnp.concatenate([high_rows[j, f, v, highs, tail] for v in range(2)], 1)
            at = (2 * fields + f) * HALO
            to_pair[j, at : at + HALO, :] = jnp.where(even, high, low)
            to_cross[j, at : at + HALO, :] = jnp.where(even, low, high)


def pair_up_kernel(own, share, rim, keep, got, kept, *sends):
    nest_at = lax.axis_index("nest")
    lev_at = lax.axis_index("lev")
    for k in range(len(sends) + 1):
        group = lax.bitwise_xor(nest_at, k)
        target = kept if k == 0 else sends[k - 1]
        for part in range(2):
            rows = pl.ds(pl.multiple_of(part * share + group * own, 8), own)
            target[part * own : (part + 1) * own, :] = keep[rows, :] + got[rows, :]
        if k > 0:
            west = got[2 * share : 2 * share + rim, :]
            east = got[2 * share + rim : 2 * share + 2 * rim, :]
            target[2 * own : 2 * own + rim, :] = jnp.where(lev_at == 0, east, west)


def aim_kernel(
    fields, rows, cols, strip_rows, strip_cols, slot_count, moves, share, touching,
    plan, ring, first_got, kept, *refs,
):
    crossing = lax.axis_size("nest") - 1
    nest_gots, rest = refs[:crossing], refs[crossing:]
    partial, zone_self, zone_sends, total = rest[0], rest[1], rest[2:-1], rest[-1]
    planes = 2 * fields
    rim = planes * BWP
    own = slot_count * STEPS * rim
    tile_at, tiles = lax.axis_index("tile"), lax.axis_size("tile")
    nest_at = lax.axis_index("nest")
    lev_at = lax.axis_index("lev")

    sums = kept[...]
    for got in nest_gots:
        sums = sums + got[0 : 2 * own, :]
    total[...] = sums

    lane = lane_iota()
    col_base = lev_at * (strip_cols // 3 - 3)
    for j in range(slot_count):
        at = j * STEPS * rim
        both = STEPS * rim
        strip = pltpu.roll(total[at : at + both, :], (LANES - col_base) % LANES, 1)
        side = total[own + at : own + at + both, :]
        second = row_iota(both) >= rim
        origins = [plan[j * PLAN + s] - tile_at * rows for s in range(STEPS)]
        for k in moves:
            dest = lax.bitwise_xor(tile_at, k)
            parts = []
            for s in range(STEPS):
                south = origins[s] >= SPLIT
                wanted = ((dest == 0) & south) | ((dest == tiles - 1) & jnp.logical_not(south))
                offset = ROW_AT + origins[s] + (strip_rows // 3) * dest - 3 - ZONE_AT
                source = lane + offset
                fits = (source >= ROW_AT - RING) & (source < ROW_AT + rows + RING)
                turned = pltpu.roll(side, (64 * LANES - offset) % LANES, 1)
                turned = jnp.where(fits, turned, 0.0)
                parts.append(
                    jnp.where(lane < ZONE_AT, strip * wanted.astype(jnp.float32), turned)
                )
            target = zone_self if k == 0 else zone_sends[moves.index(k) - 1]
            target[at : at + both, :] = jnp.where(second, parts[1], parts[0])

    from_west = first_got[2 * share + rim : 2 * share + 2 * rim, :]
    from_east = first_got[2 * share : 2 * share + rim, :]
    far_west = jnp.zeros((rim, LANES), jnp.float32)
    far_east = jnp.zeros((rim, LANES), jnp.float32)
    for i, got in enumerate(nest_gots):
        other = lax.bitwise_xor(nest_at, i + 1)
        edge = got[2 * own : 2 * own + rim, :]
        far_west = far_west + jnp.where(other == nest_at - 1, edge, 0.0)
        far_east = far_east + jnp.where(other == nest_at + 1, edge, 0.0)
    from_west = jnp.where(lev_at == 0, far_west, from_west)
    from_east = jnp.where(lev_at == 0, from_east, far_east)
    for p in range(planes):
        two = slice(BWP * p, BWP * (p + 1))
        total[0:cols, :] = ring[p]
        total[0:RING, :] = total[0:RING, :] + from_west[two]
        total[cols - RING : cols, :] = total[cols - RING : cols, :] + from_east[two]
        total[0:LANES, :] = total[0:cols, :].T
        partial[p // 2, p % 2] = total[ROW_AT : ROW_AT + rows, :]
        below = total[ROW_AT - RING : ROW_AT, :]
        above = total[ROW_AT + rows : ROW_AT + rows + RING, :]
        for i, k in enumerate(moves[1:]):
            if k in touching:
                dest = lax.bitwise_xor(tile_at, k)
                zone_sends[i][own + BWP * p : own + BWP * (p + 1), :] = jnp.where(
                    dest > tile_at, above, below
                )


def edge_cols_kernel(fields, strip_rows, slot_count, nests, pair, cross, after, packed, wide):
    del after
    even = lax.rem(lax.axis_index("tile"), 2) == 0
    west_most = lax.axis_index("lev") == 0
    planes = 2 * fields
    half = nests.shape[4] - LANES
    packed[...] = jnp.zeros_like(packed)
    wide[...] = jnp.zeros_like(wide)
    lane = lane_iota()
    for q in range(slot_count * planes):
        j, f, v = q // planes, (q % planes) // 2, q % 2
        spot = (q % 8) * 16
        mask = (lane >= spot) & (lane < spot + HALO)
        wide[:, 0:half] = nests[j, f, v, :, LANES : LANES + half]
        cells = jnp.where(west_most, wide[...], nests[j, f, v, :, 0:LANES])
        shift = jnp.where(west_most, spot + 2 * LANES - (half - HALO), spot + 2 * LANES) % LANES
        cells = pltpu.roll(cells, shift, 1)
        rows = slice(PAD, PAD + strip_rows)
        packed[q // 8, rows, :] = jnp.where(mask, cells, packed[q // 8, rows, :])
        at, rest = (2 * f + v) * HALO, (2 * fields + f) * HALO
        shift = (
            jnp.where(west_most, spot + 2 * LANES - (half - HALO) - half * v, spot + 2 * LANES) % LANES
        )
        halos = []
        for got in (pair, cross):
            cells = jnp.where(west_most, got[j, rest : rest + HALO, :], got[j, at : at + HALO, :])
            halos.append(pltpu.roll(cells, shift, 1))
        high = jnp.where(even, halos[0], halos[1])
        low = jnp.where(even, halos[1], halos[0])
        rows = slice(PAD - HALO, PAD)
        packed[q // 8, rows, :] = jnp.where(mask, low, packed[q // 8, rows, :])
        rows = slice(PAD + strip_rows, PAD + strip_rows + HALO)
        packed[q // 8, rows, :] = jnp.where(mask, high, packed[q // 8, rows, :])


def advance_kernel(
    fields, strip_rows, strip_cols, slot_count,
    plan, rates, nests, pair, cross, packed,
    inner_out, side_out, row_out, cells, first, second,
):
    planes = 2 * fields
    half = strip_cols - LANES
    room = PAD + 8
    height = strip_rows + 16
    tile_at, tiles = lax.axis_index("tile"), lax.axis_size("tile")
    nest_at = lax.axis_index("nest")
    lev_at = lax.axis_index("lev")
    even = lax.rem(tile_at, 2) == 0
    lane = lane_iota()
    first_lane, last_lane = lane == 0, lane == LANES - 1
    chunk = 16 if height % 16 == 0 and strip_rows % 16 == 0 else 8
    row_start = pl.multiple_of(jnp.where(tile_at == 0, 0, strip_rows - 16), 8)
    west_lanes = lane < jnp.where(lev_at == 0, LANES // 2, 0)

    cells[...] = jnp.zeros_like(cells)

    lats = [rates[f : f + 1, :] for f in range(fields)]
    vers = [rates[fields + f : fields + f + 1, :] for f in range(fields)]
    stays = [1.0 - 4.0 * lats[f] - 2.0 * vers[f] for f in range(fields)]

    def stencil(f, source, at, size):
        x = [[source[f, v, a, at : at + size, :] for a in range(2)] for v in range(2)]
        new = [[None] * 2, [None] * 2]
        for v in range(2):
            sideways = beside(x[v], first_lane, last_lane)
            for a in range(2):
                near = (
                    sideways[a]
                    + source[f, v, a, at - 1 : at + size - 1, :]
                    + source[f, v, a, at + 1 : at + size + 1, :]
                )
                new[v][a] = stays[f] * x[v][a] + lats[f] * near + vers[f] * x[1 - v][a]
        return new

    def one(j, _):
        down, right = plan[j * PLAN + 2], plan[j * PLAN + 3]
        shift = (LANES - right) % LANES
        same = (lane + right >= 0) & (lane + right < LANES)
        start = room - 8 + down
        goal = jnp.where(lev_at == 0, half, LANES - HALO)
        in_goal = (lane >= goal) & (lane < goal + HALO)
        for f in range(fields):
            for v in range(2):
                cells[f, v, 0, room : room + strip_rows, :] = nests[j, f, v, :, 0:LANES]
                cells[f, v, 1, room : room + strip_rows, 0:half] = nests[j, f, v, :, LANES : LANES + half]
                ends = []
                for got in (pair, cross):
                    tail = got[j, (planes + f) * HALO : (planes + f + 1) * HALO, :]
                    if v == 1:
                        tail = pltpu.roll(tail, LANES - half, 1)
                    ends.append((got[j, (2 * f + v) * HALO : (2 * f + v + 1) * HALO, :], tail))
                for a in range(2):
                    low = jnp.where(even, ends[1][a], ends[0][a])
                    high = jnp.where(even, ends[0][a], ends[1][a])
                    lanes = slice(0, LANES if a == 0 else half)
                    cells[f, v, a, room - HALO : room, lanes] = low[:, lanes]
                    cells[f, v, a, room + strip_rows : room + strip_rows + HALO, lanes] = high[:, lanes]
                n = j * planes + 2 * f + v
                got = pltpu.roll(
                    packed[lax.div(n, 8)], (goal - lax.rem(n, 8) * 16 + 2 * LANES) % LANES, 1
                )
                got = jnp.where(in_goal, got, 0.0)
                cells[f, v, 1, room - PAD : room + strip_rows + PAD, half:LANES] = got[:, half:LANES]

        sides = [None, None]
        for f in range(fields):
            for v in range(2):
                both = [
                    pltpu.roll(cells[f, v, a, pl.ds(start, height), :], shift, 1) for a in range(2)
                ]
                both = [jnp.where(same, both[a], both[1 - a]) for a in range(2)]
                for a in range(2):
                    first[f, v, a, 8 : 8 + height, :] = both[a]
                near = jnp.where(west_lanes, both[0], both[1])
                turn = jnp.where(lev_at == 0, 8, LANES + 16 - half) + f * SLOT
                near = pltpu.roll(near, turn % LANES, 1)
                sides[v] = near if f == 0 else jnp.where(lane >= f * SLOT, near, sides[v])
        for v in range(2):
            side_out[v, j] = sides[v]
        for f in range(fields):
            for v in range(2):
                for a in range(2):
                    row_out[j, f, v, a] = first[f, v, a, pl.ds(8 + row_start, 32), :]
            for c in range(0, height, chunk):
                new = stencil(f, first, 8 + c, chunk)
                for v in range(2):
                    for a in range(2):
                        second[f, v, a, 8 + c : 8 + c + chunk, :] = new[v][a]
        for f in range(fields):
            for c in range(0, strip_rows, chunk):
                new = stencil(f, second, 16 + c, chunk)
                for v in range(2):
                    inner_out[j, f, v, c : c + chunk, 0:LANES] = new[v][0]
                    inner_out[j, f, v, c : c + chunk, LANES : LANES + half] = new[v][1][:, :half]
        return 0

    lax.fori_loop(0, slot_count, one, 0)


def gaps(i):
    return jnp.minimum(i, SPAN - 1 - i)


def settle_kernel(
    fields, strip_rows, strip_cols, rows, slot_count, moves, touching,
    plan, rates, inner, side_in, row_in, partial, zone_self, *refs,
):
    count = len(moves) - 1
    zone_gots = refs[:count]
    nest_out, parent_out = refs[count : count + 2]
    zone, turned, sides, strips, side_new, mixed, rows_mixed, rows_new, whole, done = refs[count + 2 :]
    planes = 2 * fields
    rim = planes * BWP
    both = STEPS * rim
    own = slot_count * both
    half = strip_cols - LANES
    height = strip_rows + 16
    tile_at, tiles = lax.axis_index("tile"), lax.axis_size("tile")
    nest_at = lax.axis_index("nest")
    lev_at = lax.axis_index("lev")
    lane = lane_iota()
    first_lane, last_lane = lane == 0, lane == LANES - 1

    below = jnp.zeros((rim, LANES), jnp.float32)
    above = jnp.zeros((rim, LANES), jnp.float32)
    for i, k in enumerate(moves[1:]):
        if k in touching:
            other = lax.bitwise_xor(tile_at, k)
            edge = zone_gots[i][own : own + rim, :]
            below = below + jnp.where(other == tile_at - 1, edge, 0.0)
            above = above + jnp.where(other == tile_at + 1, edge, 0.0)
    for p in range(planes):
        f, v = p // 2, p % 2
        two = slice(BWP * p, BWP * (p + 1))
        parent_out[f, v] = partial[f, v]
        parent_out[f, v, 0:RING, :] = partial[f, v, 0:RING, :] + below[two]
        parent_out[f, v, rows - RING : rows, :] = partial[f, v, rows - RING : rows, :] + above[two]

    whole_move = [[plan[j * PLAN + 2 + d] for d in range(2)] for j in range(slot_count)]
    last_move = [[plan[j * PLAN + 4 + d] for d in range(2)] for j in range(slot_count)]
    offsets = [[(0, 0) if s == 1 else last_move[j] for s in range(STEPS)] for j in range(slot_count)]
    earlier = [[whole_move[j], last_move[j]] for j in range(slot_count)]

    total = zone_self[0:own, :]
    for got in zone_gots:
        total = total + got[0:own, :]
    zone[...] = jnp.zeros_like(zone)
    zone[0:own, :] = total
    second = row_iota(both) >= rim
    col_base = lev_at * (strip_cols // 3 - 3)
    col_from = lev_at * strip_cols
    gap = (half + LANES) // 2
    owner = jnp.zeros((1, LANES), jnp.int32)
    for f in range(1, fields):
        owner = owner + (lane >= f * SLOT).astype(jnp.int32)
    side_cols = lane - SLOT * owner + jnp.where(lev_at == 0, -8, 2 * strip_cols - 16)
    lane_cols = (
        lane + col_from,
        jnp.where(lane < gap, lane + LANES, lane - LANES) + col_from,
        side_cols,
    )
    for j in range(slot_count):
        block = zone[j * both : (j + 1) * both, :]
        for a in range(3):
            picks = [
                jnp.clip(third(jnp.clip(lane_cols[a] + offsets[j][s][1], 0, SPAN - 1)) - col_base, 0, ZONE_AT - 1)
                for s in range(STEPS)
            ]
            strips[j, a] = jnp.take_along_axis(block, jnp.where(second, picks[1], picks[0]), axis=1)
        picks = [
            jnp.clip(
                third(jnp.clip(lane + (tile_at * strip_rows - 8) + offsets[j][s][0], 0, SPAN - 1))
                - ((strip_rows // 3) * tile_at - 3)
                + ZONE_AT,
                ZONE_AT,
                LANES - 1,
            )
            for s in range(STEPS)
        ]
        turned[j * both : (j + 1) * both, :] = jnp.take_along_axis(
            block, jnp.where(second, picks[1], picks[0]), axis=1
        )
    sides[...] = turned[...].T

    chunk = 16 if height % 16 == 0 else 8
    lats = [rates[f : f + 1, :] for f in range(fields)]
    vers = [rates[fields + f : fields + f + 1, :] for f in range(fields)]
    lat, ver = lats[0], vers[0]
    for f in range(1, fields):
        lat = jnp.where(owner >= f, lats[f], lat)
        ver = jnp.where(owner >= f, vers[f], ver)
    stay = 4.0 * lat + 2.0 * ver
    for s in range(STEPS):
        insides = {}
        for j in range(slot_count):
            by_row, by_col = offsets[j][s]
            was_row, was_col = earlier[j][s]
            col = side_cols + by_col
            col_gap = gaps(col)
            col_kept = gaps(side_cols + was_col)
            depth = jnp.where((col < 3) | ((col >= SPAN // 2) & (col < SPAN - 3)), 0, 1)
            lines, picks = [], []
            for v in range(2):
                picks.append(jnp.minimum(j * both + s * rim + v * BWP + 2 * BWP * owner + depth, own - 1))
                pair_of = []
                for r in range(BWP):
                    n = s * rim + v * BWP + r
                    line = strips[j, 2, n : n + 1, :]
                    for f in range(1, fields):
                        m = n + 2 * BWP * f
                        line = jnp.where(owner >= f, strips[j, 2, m : m + 1, :], line)
                    pair_of.append(line)
                lines.append(pair_of)
            for c in range(0, height, chunk):
                base = row_iota(chunk) + (tile_at * strip_rows - 8 + c)
                i = base + by_row
                distance = jnp.minimum(gaps(i), col_gap)
                kept = jnp.minimum(gaps(base + was_row), col_kept)
                w = jnp.clip(BORDER - distance, 0, BORDER).astype(jnp.float32) * (1.0 / BORDER)
                w = jnp.where(kept >= 0, w, 1.0)
                in_rows = (i < BORDER) | (i >= SPAN - BORDER)
                early = (i < 3) | ((i >= SPAN // 2) & (i < SPAN - 3))
                insides[j, c] = (distance >= 1).astype(jnp.float32)
                for v in range(2):
                    pick = jnp.broadcast_to(picks[v], (chunk, LANES))
                    side = jnp.take_along_axis(sides[c : c + chunk, :], pick, axis=1)
                    strip = jnp.where(early, lines[v][0], lines[v][1])
                    driving = jnp.where(in_rows, strip, side)
                    x = side_in[v, j, c : c + chunk, :] if s == 0 else side_new[v, j, c : c + chunk, :]
                    mixed[v, j, 8 + c : 8 + c + chunk, :] = (1.0 - w) * x + w * driving
        for j in range(slot_count):
            for c in range(0, height, chunk):
                x = [mixed[v, j, 8 + c : 8 + c + chunk, :] for v in range(2)]
                for v in range(2):
                    near = (
                        pltpu.roll(x[v], 1, 1)
                        + pltpu.roll(x[v], LANES - 1, 1)
                        + mixed[v, j, 7 + c : 7 + c + chunk, :]
                        + mixed[v, j, 9 + c : 9 + c + chunk, :]
                    )
                    change = lat * near + ver * x[1 - v] - stay * x[v]
                    side_new[v, j, c : c + chunk, :] = x[v] + insides[j, c] * change

    outer = (tile_at == 0) | (tile_at == tiles - 1)
    window = jnp.where(tile_at == 0, -8, tile_at * strip_rows + strip_rows - 24)
    row_start = pl.multiple_of(jnp.where(tile_at == 0, 0, strip_rows - 16), 8)
    line = row_iota(16)
    line_from = jnp.where(tile_at == 0, 0, 16 - HALO)
    lows = (0, jnp.where(lev_at > 0, half - HALO, LANES))
    highs = (jnp.where(lev_at == 0, HALO, 0), half)
    along = lane_iota(strip_rows)
    near_col = [(along >= lows[a]) & (along < highs[a]) for a in range(2)]
    across = lane_iota(16)
    near_row = [
        (line >= line_from)
        & (line < line_from + HALO)
        & ((across < lows[a]) | (across >= highs[a]))
        for a in range(2)
    ]

    def one(j, _):
        for f in range(fields):
            back = (2 * LANES + jnp.where(lev_at == 0, -8, half - 16) - f * SLOT) % LANES
            for v in range(2):
                near = pltpu.roll(side_new[v, j, 8 : 8 + strip_rows, :], back, 1)
                whole[j, f, v, :, 0:LANES] = jnp.where(near_col[0], near, inner[j, f, v, :, 0:LANES])
                whole[j, f, v, :, LANES : LANES + half] = jnp.where(
                    near_col[1][:, :half], near[:, :half], inner[j, f, v, :, LANES : LANES + half]
                )

        @pl.when(outer)
        def _():
            full, last = plan[j * PLAN + 2], plan[j * PLAN + 4]
            base = row_iota(32) + window
            for s in range(STEPS):
                i = base + (last if s == 0 else 0)
                kept = gaps(base + (full if s == 0 else last)) >= 0
                w = jnp.clip(BORDER - gaps(i), 0, BORDER).astype(jnp.float32) * (1.0 / BORDER)
                w = jnp.where(kept, w, 1.0)
                rest = 1.0 - w
                inside = (gaps(i) >= 1).astype(jnp.float32)
                early = (i < 3) | ((i >= SPAN // 2) & (i < SPAN - 3))
                for f in range(fields):
                    for v in range(2):
                        n = s * rim + (2 * f + v) * BWP
                        for a in range(2):
                            driving = jnp.where(
                                early, strips[j, a, n : n + 1, :], strips[j, a, n + 1 : n + 2, :]
                            )
                            x = row_in[j, f, v, a] if s == 0 else rows_new[f, v, a]
                            rows_mixed[f, v, a, 8:40, :] = rest * x + w * driving
                for f in range(fields):
                    stay = 4.0 * lats[f] + 2.0 * vers[f]
                    value = [[rows_mixed[f, v, a, 8:40, :] for a in range(2)] for v in range(2)]
                    for v in range(2):
                        sideways = beside(value[v], first_lane, last_lane)
                        for a in range(2):
                            near = (
                                sideways[a]
                                + rows_mixed[f, v, a, 7:39, :]
                                + rows_mixed[f, v, a, 9:41, :]
                            )
                            change = (
                                lats[f] * near + vers[f] * value[1 - v][a] - stay * value[v][a]
                            )
                            rows_new[f, v, a] = value[v][a] + inside * change
            for f in range(fields):
                for v in range(2):
                    target = pl.ds(row_start, 16)
                    whole[j, f, v, target, 0:LANES] = jnp.where(
                        near_row[0], rows_new[f, v, 0, 8:24, :], whole[j, f, v, target, 0:LANES]
                    )
                    whole[j, f, v, target, LANES : LANES + half] = jnp.where(
                        near_row[1][:, :half],
                        rows_new[f, v, 1, 8:24, 0:half],
                        whole[j, f, v, target, LANES : LANES + half],
                    )

        pltpu.make_async_copy(whole.at[j], nest_out.at[j], done.at[j]).start()
        return 0

    lax.fori_loop(0, slot_count, one, 0)

    def wait(j, _):
        pltpu.make_async_copy(whole.at[j], nest_out.at[j], done.at[j]).wait()
        return 0

    lax.fori_loop(0, slot_count, wait, 0)


def per_device(parent_field, nest_fields, lateral_rate, vertical_rate, centres, slot_storm):
    fields, _, rows, cols = parent_field.shape
    slot_count, _, _, strip_rows, strip_cols = nest_fields.shape
    storms = slot_storm.shape[0]
    tiles, groups, levs = lax.axis_size("tile"), lax.axis_size("nest"), lax.axis_size("lev")
    planes = 2 * fields
    rim = planes * BWP
    share = storms * STEPS * rim
    own = slot_count * STEPS * rim
    height = strip_rows + 2 * PAD
    half = strip_cols - LANES
    f32 = jnp.float32

    def shaped(*dims):
        return jax.ShapeDtypeStruct(dims, f32)

    pair_list = [(t, t ^ 1) for t in range(tiles) if t ^ 1 < tiles]
    cross_list = [(t, t - 1 if t % 2 == 0 else t + 1) for t in range(1, tiles - 1)]
    centres = jnp.swapaxes(centres, 1, 2)

    send, keep, ring, to_pair, to_cross, plan, rates = pl.pallas_call(
        lambda *refs: strips_kernel(fields, rows, cols, storms, slot_count, strip_rows, *refs),
        in_specs=[HBM_SPEC] * 6,
        out_specs=[VMEM_SPEC] * 5 + [SMEM_SPEC, VMEM_SPEC],
        out_shape=[
            shaped(2 * share + 2 * rim, LANES),
            shaped(2 * share, LANES),
            shaped(planes, cols, LANES),
            shaped(slot_count, 3 * fields * HALO, LANES),
            shaped(slot_count, 3 * fields * HALO, LANES),
            jax.ShapeDtypeStruct((slot_count * PLAN,), jnp.int32),
            shaped(2 * fields, LANES),
        ],
        scratch_shapes=[pltpu.VMEM((planes, 2, rows + 16, LANES), f32)] * 3
        + [pltpu.VMEM((planes, cols + 16, LANES), f32)] * 3
        + [
            pltpu.VMEM((LANES, LANES), f32),
            pltpu.VMEM((2, 24, LANES), f32),
            pltpu.SMEM(centres.shape, jnp.int32),
            pltpu.SMEM(slot_storm.shape, jnp.int32),
            pltpu.SMEM(lateral_rate.shape, f32),
            pltpu.SMEM(vertical_rate.shape, f32),
            pltpu.VMEM(parent_field.shape, f32),
            pltpu.VMEM((slot_count, fields, 2, PAD, strip_cols), f32),
            pltpu.VMEM((slot_count, fields, 2, PAD, strip_cols), f32),
            pltpu.SemaphoreType.DMA((7,)),
        ],
        compiler_params=params(),
        name="strips",
    )(
        *(
            pltpu.with_memory_space_constraint(x, pltpu.HBM)
            for x in (centres, slot_storm, lateral_rate, vertical_rate, parent_field, nest_fields)
        )
    )
    got = lax.ppermute(send, "lev", [(l, l ^ 1) for l in range(levs)])
    pair = lax.ppermute(to_pair, "tile", pair_list)
    cross = lax.ppermute(to_cross, "tile", cross_list)

    kept, *sends = pl.pallas_call(
        lambda *refs: pair_up_kernel(own, share, rim, *refs),
        in_specs=[VMEM_SPEC] * 2,
        out_specs=[VMEM_SPEC] * groups,
        out_shape=[shaped(2 * own, LANES)] + [shaped(2 * own + rim, LANES)] * (groups - 1),
        compiler_params=params(),
        name="pair_up",
    )(keep, got)
    nest_gots = [
        lax.ppermute(x, "nest", [(n, n ^ (i + 1)) for n in range(groups)])
        for i, x in enumerate(sends)
    ]

    def holds(source, dest):
        low = max((strip_rows // 3) * dest - 3, 0)
        high = tiles * rows - FP + min((strip_rows // 3) * (dest + 1) + 3, FP)
        return rows * source - RING < high and rows * (source + 1) + RING > low

    routes = {}
    for k in range(1, tiles):
        pairs = [
            (t, t ^ k)
            for t in range(tiles)
            if t ^ k < tiles and (holds(t, t ^ k) or holds(t ^ k, t) or abs(t - (t ^ k)) == 1)
        ]
        if pairs:
            routes[k] = pairs
    touching = tuple(k for k in routes if any(abs(a - b) == 1 for a, b in routes[k]))
    moves = (0, *routes)
    zone_shapes = [shaped(own + (rim if k in touching else 0), LANES) for k in moves]
    partial, zone_self, *zone_sends = pl.pallas_call(
        lambda *refs: aim_kernel(
            fields, rows, cols, strip_rows, strip_cols, slot_count, moves, share, touching, *refs
        ),
        in_specs=[SMEM_SPEC] + [VMEM_SPEC] * (2 + groups),
        out_specs=[VMEM_SPEC] * (1 + len(moves)),
        out_shape=[shaped(fields, 2, rows, cols), *zone_shapes],
        scratch_shapes=[pltpu.VMEM((2 * own, LANES), f32)],
        compiler_params=params(),
        name="aim",
    )(plan, ring, got, kept, *nest_gots)
    zone_gots = [lax.ppermute(x, "tile", routes[k]) for k, x in zip(moves[1:], zone_sends)]

    bundles = -(-slot_count * planes // 8)
    packed = pl.pallas_call(
        lambda *refs: edge_cols_kernel(fields, strip_rows, slot_count, *refs),
        in_specs=[VMEM_SPEC] * 3 + [ANY_SPEC],
        out_specs=VMEM_SPEC,
        out_shape=shaped(bundles, height, LANES),
        scratch_shapes=[pltpu.VMEM((strip_rows, LANES), f32)],
        compiler_params=params(),
        name="edge_cols",
    )(nest_fields, pair, cross, zone_self)
    packed = lax.ppermute(packed, "lev", [(l, l ^ 1) for l in range(levs)])

    inner, side_in, row_in = pl.pallas_call(
        lambda *refs: advance_kernel(fields, strip_rows, strip_cols, slot_count, *refs),
        in_specs=[SMEM_SPEC] + [VMEM_SPEC] * 5,
        out_specs=[VMEM_SPEC] * 3,
        out_shape=[
            shaped(*nest_fields.shape),
            shaped(2, slot_count, strip_rows + 16, LANES),
            shaped(slot_count, fields, 2, 2, 32, LANES),
        ],
        scratch_shapes=[pltpu.VMEM((fields, 2, 2, strip_rows + 48, LANES), f32)]
        + [pltpu.VMEM((fields, 2, 2, strip_rows + 32, LANES), f32)] * 2,
        compiler_params=params(),
        name="advance",
    )(plan, rates, nest_fields, pair, cross, packed)

    nest_final, parent_final = pl.pallas_call(
        lambda *refs: settle_kernel(
            fields, strip_rows, strip_cols, rows, slot_count, moves, touching, *refs
        ),
        in_specs=[SMEM_SPEC] + [VMEM_SPEC] * (5 + len(moves)),
        out_specs=[ANY_SPEC, VMEM_SPEC],
        out_shape=[shaped(*nest_fields.shape), shaped(*parent_field.shape)],
        scratch_shapes=[
            pltpu.VMEM((LANES, LANES), f32),
            pltpu.VMEM((LANES, LANES), f32),
            pltpu.VMEM((LANES, LANES), f32),
            pltpu.VMEM((slot_count, 3, STEPS * rim, LANES), f32),
            pltpu.VMEM((2, slot_count, strip_rows + 16, LANES), f32),
            pltpu.VMEM((2, slot_count, strip_rows + 32, LANES), f32),
            pltpu.VMEM((fields, 2, 2, 48, LANES), f32),
            pltpu.VMEM((fields, 2, 2, 32, LANES), f32),
            pltpu.VMEM((slot_count, fields, 2, strip_rows, strip_cols), f32),
            pltpu.SemaphoreType.DMA((slot_count,)),
        ],
        compiler_params=params(),
        name="settle",
    )(
        plan, rates, inner, side_in, row_in, partial, zone_self, *zone_gots,
    )
    return (parent_final, nest_final)


def solution(mesh):
    placed = (
        P("member", None, "tile", ("nest", "lev")),
        P(("member", "nest"), None, None, "tile", "lev"),
        P(),
        P(),
        P("member", None, None),
        P("member"),
    )
    return jax.shard_map(
        per_device,
        mesh=mesh,
        in_specs=placed,
        out_specs=(
            P("member", None, "tile", ("nest", "lev")),
            P(("member", "nest"), None, None, "tile", "lev"),
        ),
        check_vma=False,
    )
```

```python
import jax
import jax.numpy as jnp
from jax import lax
from jax.experimental import pallas as pl
from jax.experimental.pallas import tpu as pltpu
from jax.sharding import PartitionSpec as P

FP = 128
BWP = 2
MOVE = 2
STEPS = 2
BORDER = 3 * BWP
SPAN = 3 * FP
HALO = STEPS * (3 * MOVE + 1)
PAD = 16
LANES = 128
PLAN = 8
RING = STEPS
ROW_AT = 32
ZONE_AT = 72
SPLIT = -(FP // 4)
SLOT = 24
VMEM_LIMIT = 40 * 1024 * 1024

SMEM_SPEC = pl.BlockSpec(memory_space=pltpu.SMEM)
VMEM_SPEC = pl.BlockSpec(memory_space=pltpu.VMEM)
HBM_SPEC = pl.BlockSpec(memory_space=pltpu.HBM)
ANY_SPEC = pl.BlockSpec(memory_space=pl.ANY)


def params(**more):
    return pltpu.CompilerParams(vmem_limit_bytes=VMEM_LIMIT, **more)


def lane_iota(rows=1, lanes=LANES):
    return lax.broadcasted_iota(jnp.int32, (rows, lanes), 1)


def row_iota(rows, lanes=LANES):
    return lax.broadcasted_iota(jnp.int32, (rows, lanes), 0)


def beside(x, first_lane, last_lane):
    left = [pltpu.roll(v, 1, 1) for v in x]
    right = [pltpu.roll(v, LANES - 1, 1) for v in x]
    return [
        jnp.where(first_lane, left[1 - a], left[a]) + jnp.where(last_lane, right[1 - a], right[a])
        for a in range(2)
    ]


def third(values):
    return (values * 21846) >> 16


def strips_kernel(
    fields, rows, cols, storms, slot_count,
    centres_in, slots_in, lateral_in, vertical_in, parent_in, nests_in,
    send, keep, ring_out, plan, rates, nests,
    plain0, plain1, plain2, turned0, turned1, turned2, block, gather,
    centres, slots, lateral, vertical, parent, arrived,
):
    sources = (
        (centres_in, centres),
        (slots_in, slots),
        (lateral_in, lateral),
        (vertical_in, vertical),
        (parent_in, parent),
        (nests_in, nests),
    )
    copies = [
        pltpu.make_async_copy(source, target, arrived.at[i])
        for i, (source, target) in enumerate(sources)
    ]
    for copy in copies:
        copy.start()
    planes = 2 * fields
    tile_at, tiles = lax.axis_index("tile"), lax.axis_size("tile")
    lev_at, levs = lax.axis_index("lev"), lax.axis_size("lev")
    col_at = lax.axis_index("nest") * levs + lev_at
    col_blocks = lax.axis_size("nest") * levs
    top = 8
    height = rows + 16
    width = cols + 16

    lane = lane_iota()
    first_lane, last_lane = lane == 0, lane == LANES - 1
    row = tile_at * rows + row_iota(height) - top
    tile_cols = (lane, jnp.where(lane < LANES // 2, lane + LANES, lane - LANES))
    within = [
        (
            (row >= 0) & (row < tiles * rows)
            & (col_at * cols + c >= 0) & (col_at * cols + c < col_blocks * cols)
        ).astype(jnp.float32)
        for c in tile_cols
    ]
    plain0[...] = jnp.zeros_like(plain0)
    turned0[...] = jnp.zeros_like(turned0)
    block[...] = jnp.zeros_like(block)
    for copy in copies[:5]:
        copy.wait()
    for f in range(fields):
        rates[f : f + 1, :] = jnp.full((1, LANES), lateral[f], jnp.float32)
        rates[fields + f : fields + f + 1, :] = jnp.full((1, LANES), vertical[f], jnp.float32)
    for j in range(slot_count):
        storm = slots[lax.axis_index("nest") * slot_count + j]
        at = [[centres[n, d, storm] for d in range(2)] for n in range(STEPS + 1)]
        for d in range(2):
            plan[j * PLAN + d] = at[d + 1][0] - FP // 2
            plan[j * PLAN + 2 + d] = 3 * (at[STEPS][d] - at[0][d])
            plan[j * PLAN + 4 + d] = 3 * (at[STEPS][d] - at[STEPS - 1][d])
    for p in range(planes):
        plain0[p, 0, top : top + rows, :] = parent[p // 2, p % 2]
        block[ROW_AT : ROW_AT + rows, :] = parent[p // 2, p % 2]
        turned0[p, top : top + cols, :] = block[...].T

    inner = slice(1, height - 1)

    def plain_step(source, target, mask):
        for f in range(fields):
            lat, ver = lateral[f], vertical[f]
            for v in range(2):
                x = [source[2 * f + v, a, inner, :] for a in range(2)]
                sideways = beside(x, first_lane, last_lane)
                for a in range(2):
                    near = (
                        sideways[a]
                        + source[2 * f + v, a, 2:height, :]
                        + source[2 * f + v, a, 0 : height - 2, :]
                    )
                    other = source[2 * f + 1 - v, a, inner, :]
                    new = x[a] + lat * (near - 4.0 * x[a]) + ver * (other - 2.0 * x[a])
                    if mask is not None:
                        new = new * mask[a][inner, :]
                    target[2 * f + v, a, inner, :] = new
                    for edge in (0, height - 1):
                        target[2 * f + v, a, edge : edge + 1, :] = jnp.zeros(
                            (1, LANES), jnp.float32
                        )

    plain_step(plain0, plain1, within)
    plain_step(plain1, plain2, None)

    row_t = tile_at * rows + lane_iota() - ROW_AT
    col_t = col_at * cols + row_iota(width) - top
    within_t = (
        (row_t >= 0) & (row_t < tiles * rows) & (col_t >= 0) & (col_t < col_blocks * cols)
    ).astype(jnp.float32)

    def turned_step(source, target, mask):
        for f in range(fields):
            lat, ver = lateral[f], vertical[f]
            for v in range(2):
                x = source[2 * f + v, 1 : width - 1, :]
                near = (
                    source[2 * f + v, 2:width, :]
                    + source[2 * f + v, 0 : width - 2, :]
                    + pltpu.roll(x, 1, 1)
                    + pltpu.roll(x, LANES - 1, 1)
                )
                other = source[2 * f + 1 - v, 1 : width - 1, :]
                new = x + lat * (near - 4.0 * x) + ver * (other - 2.0 * x)
                if mask is not None:
                    new = new * mask[1 : width - 1, :]
                target[2 * f + v, 1 : width - 1, :] = new
                target[2 * f + v, 0:1, :] = jnp.zeros((1, LANES), jnp.float32)
                target[2 * f + v, width - 1 : width, :] = jnp.zeros((1, LANES), jnp.float32)

    turned_step(turned0, turned1, within_t)
    turned_step(turned1, turned2, None)

    share = storms * STEPS * planes * BWP
    for j in range(storms):
        storm = slots[j]
        for s in range(STEPS):
            at = (j * STEPS + s) * planes * BWP
            corner_row = centres[s + 1, 0, storm] - FP // 2 - tile_at * rows
            corner_col = centres[s + 1, 1, storm] - FP // 2 - col_at * cols
            plain = (plain1, plain2)[s]
            turned = (turned1, turned2)[s]
            first = jnp.where(corner_row >= SPLIT, corner_row, corner_row + FP - BWP)
            first = jnp.clip(first + top, 0, height - BWP)
            for p in range(planes):
                for a in range(2):
                    gather[a, BWP * p : BWP * (p + 1), :] = plain[p, a, pl.ds(first, BWP), :]
            shift = (64 * LANES - corner_col) % LANES
            window = [pltpu.roll(gather[a], shift, 1) for a in range(2)]
            place = lane + corner_col
            main = (place >= 0) & (place < cols)
            rim = (place >= -RING) & (place < cols + RING)
            window = jnp.where(main, window[0], jnp.where(rim, window[1], 0.0))[: planes * BWP]
            send[at : at + planes * BWP, :] = window
            keep[at : at + planes * BWP, :] = window
            mine = corner_col + (FP - BWP) * lev_at
            theirs = corner_col + (FP - BWP) * (levs - 1 - lev_at)
            for target, start in ((keep, mine), (send, theirs)):
                start = jnp.clip(start + top, 0, width - BWP)
                for p in range(planes):
                    target[share + at + BWP * p : share + at + BWP * (p + 1), :] = turned[
                        p, pl.ds(start, BWP), :
                    ]
    for p in range(planes):
        send[2 * share + BWP * p : 2 * share + BWP * (p + 1), :] = turned2[p, top - RING : top, :]
        at = 2 * share + planes * BWP + BWP * p
        send[at : at + BWP, :] = turned2[p, top + cols : top + cols + RING, :]
        ring_out[p] = turned2[p, top : top + cols, :]
    copies[5].wait()


def pair_up_kernel(own, share, rim, keep, got, kept, *sends):
    nest_at = lax.axis_index("nest")
    lev_at = lax.axis_index("lev")
    for k in range(len(sends) + 1):
        group = lax.bitwise_xor(nest_at, k)
        target = kept if k == 0 else sends[k - 1]
        for part in range(2):
            rows = pl.ds(pl.multiple_of(part * share + group * own, 8), own)
            target[part * own : (part + 1) * own, :] = keep[rows, :] + got[rows, :]
        if k > 0:
            west = got[2 * share : 2 * share + rim, :]
            east = got[2 * share + rim : 2 * share + 2 * rim, :]
            target[2 * own : 2 * own + rim, :] = jnp.where(lev_at == 0, east, west)


def aim_kernel(
    fields, rows, cols, strip_rows, strip_cols, slot_count, moves, share, touching,
    plan, ring, first_got, kept, *refs,
):
    crossing = lax.axis_size("nest") - 1
    nest_gots, rest = refs[:crossing], refs[crossing:]
    partial, zone_self, zone_sends, total = rest[0], rest[1], rest[2:-1], rest[-1]
    planes = 2 * fields
    rim = planes * BWP
    own = slot_count * STEPS * rim
    tile_at, tiles = lax.axis_index("tile"), lax.axis_size("tile")
    nest_at = lax.axis_index("nest")
    lev_at = lax.axis_index("lev")

    sums = kept[...]
    for got in nest_gots:
        sums = sums + got[0 : 2 * own, :]
    total[...] = sums

    lane = lane_iota()
    col_base = lev_at * (strip_cols // 3 - 3)
    for j in range(slot_count):
        at = j * STEPS * rim
        both = STEPS * rim
        strip = pltpu.roll(total[at : at + both, :], (LANES - col_base) % LANES, 1)
        side = total[own + at : own + at + both, :]
        second = row_iota(both) >= rim
        origins = [plan[j * PLAN + s] - tile_at * rows for s in range(STEPS)]
        for k in moves:
            dest = lax.bitwise_xor(tile_at, k)
            parts = []
            for s in range(STEPS):
                south = origins[s] >= SPLIT
                wanted = ((dest == 0) & south) | ((dest == tiles - 1) & jnp.logical_not(south))
                offset = ROW_AT + origins[s] + (strip_rows // 3) * dest - 3 - ZONE_AT
                source = lane + offset
                fits = (source >= ROW_AT - RING) & (source < ROW_AT + rows + RING)
                turned = pltpu.roll(side, (64 * LANES - offset) % LANES, 1)
                turned = jnp.where(fits, turned, 0.0)
                parts.append(
                    jnp.where(lane < ZONE_AT, strip * wanted.astype(jnp.float32), turned)
                )
            target = zone_self if k == 0 else zone_sends[moves.index(k) - 1]
            target[at : at + both, :] = jnp.where(second, parts[1], parts[0])

    from_west = first_got[2 * share + rim : 2 * share + 2 * rim, :]
    from_east = first_got[2 * share : 2 * share + rim, :]
    far_west = jnp.zeros((rim, LANES), jnp.float32)
    far_east = jnp.zeros((rim, LANES), jnp.float32)
    for i, got in enumerate(nest_gots):
        other = lax.bitwise_xor(nest_at, i + 1)
        edge = got[2 * own : 2 * own + rim, :]
        far_west = far_west + jnp.where(other == nest_at - 1, edge, 0.0)
        far_east = far_east + jnp.where(other == nest_at + 1, edge, 0.0)
    from_west = jnp.where(lev_at == 0, far_west, from_west)
    from_east = jnp.where(lev_at == 0, from_east, far_east)
    for p in range(planes):
        two = slice(BWP * p, BWP * (p + 1))
        total[0:cols, :] = ring[p]
        total[0:RING, :] = total[0:RING, :] + from_west[two]
        total[cols - RING : cols, :] = total[cols - RING : cols, :] + from_east[two]
        total[0:LANES, :] = total[0:cols, :].T
        partial[p // 2, p % 2] = total[ROW_AT : ROW_AT + rows, :]
        below = total[ROW_AT - RING : ROW_AT, :]
        above = total[ROW_AT + rows : ROW_AT + rows + RING, :]
        for i, k in enumerate(moves[1:]):
            if k in touching:
                dest = lax.bitwise_xor(tile_at, k)
                zone_sends[i][own + BWP * p : own + BWP * (p + 1), :] = jnp.where(
                    dest > tile_at, above, below
                )


def edge_cols_kernel(fields, slot_count, nests, after, packed, wide):
    del after
    west_most = lax.axis_index("lev") == 0
    planes = 2 * fields
    half = nests.shape[4] - LANES
    wide[...] = jnp.zeros_like(wide)
    lane = lane_iota()
    for q in range(slot_count * planes):
        j, f, v = q // planes, (q % planes) // 2, q % 2
        spot = (q % 8) * 16
        wide[q % 8, :, 0:half] = nests[j, f, v, :, LANES : LANES + half]
        cells = jnp.where(west_most, wide[q % 8], nests[j, f, v, :, 0:LANES])
        shift = jnp.where(west_most, spot + 2 * LANES - (half - HALO), spot + 2 * LANES) % LANES
        cells = pltpu.roll(cells, shift, 1)
        row = cells if q % 8 == 0 else jnp.where(lane >= spot, cells, row)
        if q % 8 == 7 or q == slot_count * planes - 1:
            packed[q // 8] = row


def edge_rows_kernel(fields, strip_rows, slot_count, nests, packed, after, to_pair, to_cross):
    del after
    even = lax.rem(lax.axis_index("tile"), 2) == 0
    half = nests.shape[4] - LANES
    lows, highs, tail = slice(0, HALO), slice(strip_rows - HALO, strip_rows), slice(LANES, LANES + half)

    def put(at, low, high):
        to_pair[at : at + HALO, :] = jnp.where(even, high, low)
        to_cross[at : at + HALO, :] = jnp.where(even, low, high)

    for j in range(slot_count):
        for f in range(fields):
            at = (3 * fields * j + 2 * f) * HALO
            for v in range(2):
                put(at + v * HALO, nests[j, f, v, lows, 0:LANES], nests[j, f, v, highs, 0:LANES])
            at = (3 * fields * j + 2 * fields + f) * HALO
            put(
                at,
                jnp.concatenate([nests[j, f, v, lows, tail] for v in range(2)], 1),
                jnp.concatenate([nests[j, f, v, highs, tail] for v in range(2)], 1),
            )
    for g in range(packed.shape[0]):
        at = (3 * fields * slot_count + g) * HALO
        put(at, packed[g, lows, :], packed[g, highs, :])


def advance_kernel(
    fields, strip_rows, strip_cols, slot_count,
    plan, rates, nests, pair, cross, packed,
    inner_out, side_out, row_out, cells, first, second,
):
    planes = 2 * fields
    half = strip_cols - LANES
    room = PAD + 8
    height = strip_rows + 16
    tile_at, tiles = lax.axis_index("tile"), lax.axis_size("tile")
    nest_at = lax.axis_index("nest")
    lev_at = lax.axis_index("lev")
    even = lax.rem(tile_at, 2) == 0
    lane = lane_iota()
    first_lane, last_lane = lane == 0, lane == LANES - 1
    chunk = 16 if height % 16 == 0 and strip_rows % 16 == 0 else 8
    row_start = pl.multiple_of(jnp.where(tile_at == 0, 0, strip_rows - 16), 8)
    west_lanes = lane < jnp.where(lev_at == 0, LANES // 2, 0)

    cells[...] = jnp.zeros_like(cells)

    lats = [rates[f : f + 1, :] for f in range(fields)]
    vers = [rates[fields + f : fields + f + 1, :] for f in range(fields)]
    stays = [1.0 - 4.0 * lats[f] - 2.0 * vers[f] for f in range(fields)]

    def stencil(f, source, at, size):
        x = [[source[f, v, a, at : at + size, :] for a in range(2)] for v in range(2)]
        new = [[None] * 2, [None] * 2]
        for v in range(2):
            sideways = beside(x[v], first_lane, last_lane)
            for a in range(2):
                near = (
                    sideways[a]
                    + source[f, v, a, at - 1 : at + size - 1, :]
                    + source[f, v, a, at + 1 : at + size + 1, :]
                )
                new[v][a] = stays[f] * x[v][a] + lats[f] * near + vers[f] * x[1 - v][a]
        return new

    def one(j, _):
        down, right = plan[j * PLAN + 2], plan[j * PLAN + 3]
        shift = (LANES - right) % LANES
        same = (lane + right >= 0) & (lane + right < LANES)
        start = room - 8 + down
        goal = jnp.where(lev_at == 0, half, LANES - HALO)
        in_goal = (lane >= goal) & (lane < goal + HALO)
        for f in range(fields):
            for v in range(2):
                cells[f, v, 0, room : room + strip_rows, :] = nests[j, f, v, :, 0:LANES]
                cells[f, v, 1, room : room + strip_rows, 0:half] = nests[j, f, v, :, LANES : LANES + half]
                n = j * planes + 2 * f + v
                goal_shift = (goal - lax.rem(n, 8) * 16 + 2 * LANES) % LANES
                ends = []
                for got in (pair, cross):
                    main = got[pl.ds((3 * fields * j + 2 * f + v) * HALO, HALO), :]
                    tail = got[pl.ds((3 * fields * j + planes + f) * HALO, HALO), :]
                    if v == 1:
                        tail = pltpu.roll(tail, LANES - half, 1)
                    corner = got[pl.ds((3 * fields * slot_count + lax.div(n, 8)) * HALO, HALO), :]
                    corner = jnp.where(in_goal, pltpu.roll(corner, goal_shift, 1), 0.0)
                    ends.append((main, jnp.where(lane < half, tail, corner)))
                for a in range(2):
                    cells[f, v, a, room - HALO : room, :] = jnp.where(even, ends[1][a], ends[0][a])
                    cells[f, v, a, room + strip_rows : room + strip_rows + HALO, :] = jnp.where(
                        even, ends[0][a], ends[1][a]
                    )
                got = jnp.where(in_goal, pltpu.roll(packed[lax.div(n, 8)], goal_shift, 1), 0.0)
                cells[f, v, 1, room : room + strip_rows, half:LANES] = got[:, half:LANES]

        sides = [None, None]
        for f in range(fields):
            for v in range(2):
                both = [
                    pltpu.roll(cells[f, v, a, pl.ds(start, height), :], shift, 1) for a in range(2)
                ]
                both = [jnp.where(same, both[a], both[1 - a]) for a in range(2)]
                for a in range(2):
                    first[f, v, a, 8 : 8 + height, :] = both[a]
                near = jnp.where(west_lanes, both[0], both[1])
                turn = jnp.where(lev_at == 0, 8, LANES + 16 - half) + f * SLOT
                near = pltpu.roll(near, turn % LANES, 1)
                sides[v] = near if f == 0 else jnp.where(lane >= f * SLOT, near, sides[v])
        for v in range(2):
            side_out[v, j] = sides[v]
        for f in range(fields):
            for v in range(2):
                for a in range(2):
                    row_out[j, f, v, a] = first[f, v, a, pl.ds(8 + row_start, 32), :]
            for c in range(0, height, chunk):
                new = stencil(f, first, 8 + c, chunk)
                for v in range(2):
                    for a in range(2):
                        second[f, v, a, 8 + c : 8 + c + chunk, :] = new[v][a]
        for f in range(fields):
            for c in range(0, strip_rows, chunk):
                new = stencil(f, second, 16 + c, chunk)
                for v in range(2):
                    inner_out[j, f, v, c : c + chunk, 0:LANES] = new[v][0]
                    inner_out[j, f, v, c : c + chunk, LANES : LANES + half] = new[v][1][:, :half]
        return 0

    lax.fori_loop(0, slot_count, one, 0)


def gaps(i):
    return jnp.minimum(i, SPAN - 1 - i)


def settle_kernel(
    fields, strip_rows, strip_cols, rows, slot_count, moves, touching,
    plan, rates, inner, side_in, row_in, partial, zone_self, *refs,
):
    count = len(moves) - 1
    zone_gots = refs[:count]
    nest_out, parent_out = refs[count : count + 2]
    zone, turned, sides, strips, side_new, mixed, rows_mixed, rows_new, whole, done = refs[count + 2 :]
    planes = 2 * fields
    rim = planes * BWP
    both = STEPS * rim
    own = slot_count * both
    half = strip_cols - LANES
    height = strip_rows + 16
    tile_at, tiles = lax.axis_index("tile"), lax.axis_size("tile")
    nest_at = lax.axis_index("nest")
    lev_at = lax.axis_index("lev")
    lane = lane_iota()
    first_lane, last_lane = lane == 0, lane == LANES - 1

    below = jnp.zeros((rim, LANES), jnp.float32)
    above = jnp.zeros((rim, LANES), jnp.float32)
    for i, k in enumerate(moves[1:]):
        if k in touching:
            other = lax.bitwise_xor(tile_at, k)
            edge = zone_gots[i][own : own + rim, :]
            below = below + jnp.where(other == tile_at - 1, edge, 0.0)
            above = above + jnp.where(other == tile_at + 1, edge, 0.0)
    for p in range(planes):
        f, v = p // 2, p % 2
        two = slice(BWP * p, BWP * (p + 1))
        parent_out[f, v] = partial[f, v]
        parent_out[f, v, 0:RING, :] = partial[f, v, 0:RING, :] + below[two]
        parent_out[f, v, rows - RING : rows, :] = partial[f, v, rows - RING : rows, :] + above[two]

    whole_move = [[plan[j * PLAN + 2 + d] for d in range(2)] for j in range(slot_count)]
    last_move = [[plan[j * PLAN + 4 + d] for d in range(2)] for j in range(slot_count)]
    offsets = [[(0, 0) if s == 1 else last_move[j] for s in range(STEPS)] for j in range(slot_count)]
    earlier = [[whole_move[j], last_move[j]] for j in range(slot_count)]

    total = zone_self[0:own, :]
    for got in zone_gots:
        total = total + got[0:own, :]
    zone[...] = jnp.zeros_like(zone)
    zone[0:own, :] = total
    second = row_iota(both) >= rim
    col_base = lev_at * (strip_cols // 3 - 3)
    col_from = lev_at * strip_cols
    gap = (half + LANES) // 2
    owner = jnp.zeros((1, LANES), jnp.int32)
    for f in range(1, fields):
        owner = owner + (lane >= f * SLOT).astype(jnp.int32)
    side_cols = lane - SLOT * owner + jnp.where(lev_at == 0, -8, 2 * strip_cols - 16)
    lane_cols = (
        lane + col_from,
        jnp.where(lane < gap, lane + LANES, lane - LANES) + col_from,
        side_cols,
    )
    for j in range(slot_count):
        block = zone[j * both : (j + 1) * both, :]
        for a in range(3):
            picks = [
                jnp.clip(third(jnp.clip(lane_cols[a] + offsets[j][s][1], 0, SPAN - 1)) - col_base, 0, ZONE_AT - 1)
                for s in range(STEPS)
            ]
            strips[j, a] = jnp.take_along_axis(block, jnp.where(second, picks[1], picks[0]), axis=1)
        picks = [
            jnp.clip(
                third(jnp.clip(lane + (tile_at * strip_rows - 8) + offsets[j][s][0], 0, SPAN - 1))
                - ((strip_rows // 3) * tile_at - 3)
                + ZONE_AT,
                ZONE_AT,
                LANES - 1,
            )
            for s in range(STEPS)
        ]
        turned[j * both : (j + 1) * both, :] = jnp.take_along_axis(
            block, jnp.where(second, picks[1], picks[0]), axis=1
        )
    sides[...] = turned[...].T

    chunk = 16 if height % 16 == 0 else 8
    lats = [rates[f : f + 1, :] for f in range(fields)]
    vers = [rates[fields + f : fields + f + 1, :] for f in range(fields)]
    lat, ver = lats[0], vers[0]
    for f in range(1, fields):
        lat = jnp.where(owner >= f, lats[f], lat)
        ver = jnp.where(owner >= f, vers[f], ver)
    stay = 4.0 * lat + 2.0 * ver
    for s in range(STEPS):
        insides = {}
        for j in range(slot_count):
            by_row, by_col = offsets[j][s]
            was_row, was_col = earlier[j][s]
            col = side_cols + by_col
            col_gap = gaps(col)
            col_kept = gaps(side_cols + was_col)
            depth = jnp.where((col < 3) | ((col >= SPAN // 2) & (col < SPAN - 3)), 0, 1)
            lines, picks = [], []
            for v in range(2):
                picks.append(jnp.minimum(j * both + s * rim + v * BWP + 2 * BWP * owner + depth, own - 1))
                pair_of = []
                for r in range(BWP):
                    n = s * rim + v * BWP + r
                    line = strips[j, 2, n : n + 1, :]
                    for f in range(1, fields):
                        m = n + 2 * BWP * f
                        line = jnp.where(owner >= f, strips[j, 2, m : m + 1, :], line)
                    pair_of.append(line)
                lines.append(pair_of)
            for c in range(0, height, chunk):
                base = row_iota(chunk) + (tile_at * strip_rows - 8 + c)
                i = base + by_row
                distance = jnp.minimum(gaps(i), col_gap)
                kept = jnp.minimum(gaps(base + was_row), col_kept)
                w = jnp.clip(BORDER - distance, 0, BORDER).astype(jnp.float32) * (1.0 / BORDER)
                w = jnp.where(kept >= 0, w, 1.0)
                in_rows = (i < BORDER) | (i >= SPAN - BORDER)
                early = (i < 3) | ((i >= SPAN // 2) & (i < SPAN - 3))
                insides[j, c] = (distance >= 1).astype(jnp.float32)
                for v in range(2):
                    pick = jnp.broadcast_to(picks[v], (chunk, LANES))
                    side = jnp.take_along_axis(sides[c : c + chunk, :], pick, axis=1)
                    strip = jnp.where(early, lines[v][0], lines[v][1])
                    driving = jnp.where(in_rows, strip, side)
                    x = side_in[v, j, c : c + chunk, :] if s == 0 else side_new[v, j, c : c + chunk, :]
                    mixed[v, j, 8 + c : 8 + c + chunk, :] = (1.0 - w) * x + w * driving
        for j in range(slot_count):
            for c in range(0, height, chunk):
                x = [mixed[v, j, 8 + c : 8 + c + chunk, :] for v in range(2)]
                for v in range(2):
                    near = (
                        pltpu.roll(x[v], 1, 1)
                        + pltpu.roll(x[v], LANES - 1, 1)
                        + mixed[v, j, 7 + c : 7 + c + chunk, :]
                        + mixed[v, j, 9 + c : 9 + c + chunk, :]
                    )
                    change = lat * near + ver * x[1 - v] - stay * x[v]
                    side_new[v, j, c : c + chunk, :] = x[v] + insides[j, c] * change

    outer = (tile_at == 0) | (tile_at == tiles - 1)
    window = jnp.where(tile_at == 0, -8, tile_at * strip_rows + strip_rows - 24)
    row_start = pl.multiple_of(jnp.where(tile_at == 0, 0, strip_rows - 16), 8)
    line = row_iota(16)
    line_from = jnp.where(tile_at == 0, 0, 16 - HALO)
    lows = (0, jnp.where(lev_at > 0, half - HALO, LANES))
    highs = (jnp.where(lev_at == 0, HALO, 0), half)
    along = lane_iota(strip_rows)
    near_col = [(along >= lows[a]) & (along < highs[a]) for a in range(2)]
    across = lane_iota(16)
    near_row = [
        (line >= line_from)
        & (line < line_from + HALO)
        & ((across < lows[a]) | (across >= highs[a]))
        for a in range(2)
    ]

    def one(j, _):
        for f in range(fields):
            back = (2 * LANES + jnp.where(lev_at == 0, -8, half - 16) - f * SLOT) % LANES
            for v in range(2):
                near = pltpu.roll(side_new[v, j, 8 : 8 + strip_rows, :], back, 1)
                whole[j, f, v, :, 0:LANES] = jnp.where(near_col[0], near, inner[j, f, v, :, 0:LANES])
                whole[j, f, v, :, LANES : LANES + half] = jnp.where(
                    near_col[1][:, :half], near[:, :half], inner[j, f, v, :, LANES : LANES + half]
                )

        @pl.when(outer)
        def _():
            full, last = plan[j * PLAN + 2], plan[j * PLAN + 4]
            base = row_iota(32) + window
            for s in range(STEPS):
                i = base + (last if s == 0 else 0)
                kept = gaps(base + (full if s == 0 else last)) >= 0
                w = jnp.clip(BORDER - gaps(i), 0, BORDER).astype(jnp.float32) * (1.0 / BORDER)
                w = jnp.where(kept, w, 1.0)
                rest = 1.0 - w
                inside = (gaps(i) >= 1).astype(jnp.float32)
                early = (i < 3) | ((i >= SPAN // 2) & (i < SPAN - 3))
                for f in range(fields):
                    for v in range(2):
                        n = s * rim + (2 * f + v) * BWP
                        for a in range(2):
                            driving = jnp.where(
                                early, strips[j, a, n : n + 1, :], strips[j, a, n + 1 : n + 2, :]
                            )
                            x = row_in[j, f, v, a] if s == 0 else rows_new[f, v, a]
                            rows_mixed[f, v, a, 8:40, :] = rest * x + w * driving
                for f in range(fields):
                    stay = 4.0 * lats[f] + 2.0 * vers[f]
                    value = [[rows_mixed[f, v, a, 8:40, :] for a in range(2)] for v in range(2)]
                    for v in range(2):
                        sideways = beside(value[v], first_lane, last_lane)
                        for a in range(2):
                            near = (
                                sideways[a]
                                + rows_mixed[f, v, a, 7:39, :]
                                + rows_mixed[f, v, a, 9:41, :]
                            )
                            change = (
                                lats[f] * near + vers[f] * value[1 - v][a] - stay * value[v][a]
                            )
                            rows_new[f, v, a] = value[v][a] + inside * change
            for f in range(fields):
                for v in range(2):
                    target = pl.ds(row_start, 16)
                    whole[j, f, v, target, 0:LANES] = jnp.where(
                        near_row[0], rows_new[f, v, 0, 8:24, :], whole[j, f, v, target, 0:LANES]
                    )
                    whole[j, f, v, target, LANES : LANES + half] = jnp.where(
                        near_row[1][:, :half],
                        rows_new[f, v, 1, 8:24, 0:half],
                        whole[j, f, v, target, LANES : LANES + half],
                    )

        pltpu.make_async_copy(whole.at[j], nest_out.at[j], done.at[j]).start()
        return 0

    lax.fori_loop(0, slot_count, one, 0)

    def wait(j, _):
        pltpu.make_async_copy(whole.at[j], nest_out.at[j], done.at[j]).wait()
        return 0

    lax.fori_loop(0, slot_count, wait, 0)


def per_device(parent_field, nest_fields, lateral_rate, vertical_rate, centres, slot_storm):
    fields, _, rows, cols = parent_field.shape
    slot_count, _, _, strip_rows, strip_cols = nest_fields.shape
    storms = slot_storm.shape[0]
    tiles, groups, levs = lax.axis_size("tile"), lax.axis_size("nest"), lax.axis_size("lev")
    planes = 2 * fields
    rim = planes * BWP
    share = storms * STEPS * rim
    own = slot_count * STEPS * rim
    height = strip_rows + 2 * PAD
    half = strip_cols - LANES
    f32 = jnp.float32

    def shaped(*dims):
        return jax.ShapeDtypeStruct(dims, f32)

    pair_list = [(t, t ^ 1) for t in range(tiles) if t ^ 1 < tiles]
    cross_list = [(t, t - 1 if t % 2 == 0 else t + 1) for t in range(1, tiles - 1)]
    centres = jnp.swapaxes(centres, 1, 2)

    send, keep, ring, plan, rates, nests = pl.pallas_call(
        lambda *refs: strips_kernel(fields, rows, cols, storms, slot_count, *refs),
        in_specs=[HBM_SPEC] * 6,
        out_specs=[VMEM_SPEC] * 3 + [SMEM_SPEC] + [VMEM_SPEC] * 2,
        out_shape=[
            shaped(2 * share + 2 * rim, LANES),
            shaped(2 * share, LANES),
            shaped(planes, cols, LANES),
            jax.ShapeDtypeStruct((slot_count * PLAN,), jnp.int32),
            shaped(2 * fields, LANES),
            shaped(*nest_fields.shape),
        ],
        scratch_shapes=[pltpu.VMEM((planes, 2, rows + 16, LANES), f32)] * 3
        + [pltpu.VMEM((planes, cols + 16, LANES), f32)] * 3
        + [
            pltpu.VMEM((LANES, LANES), f32),
            pltpu.VMEM((2, 24, LANES), f32),
            pltpu.SMEM(centres.shape, jnp.int32),
            pltpu.SMEM(slot_storm.shape, jnp.int32),
            pltpu.SMEM(lateral_rate.shape, f32),
            pltpu.SMEM(vertical_rate.shape, f32),
            pltpu.VMEM(parent_field.shape, f32),
            pltpu.SemaphoreType.DMA((6,)),
        ],
        compiler_params=params(),
        name="strips",
    )(
        *(
            pltpu.with_memory_space_constraint(x, pltpu.HBM)
            for x in (centres, slot_storm, lateral_rate, vertical_rate, parent_field, nest_fields)
        )
    )
    got = lax.ppermute(send, "lev", [(l, l ^ 1) for l in range(levs)])

    bundles = -(-slot_count * planes // 8)
    packed = pl.pallas_call(
        lambda *refs: edge_cols_kernel(fields, slot_count, *refs),
        in_specs=[VMEM_SPEC, ANY_SPEC],
        out_specs=VMEM_SPEC,
        out_shape=shaped(bundles, strip_rows, LANES),
        scratch_shapes=[pltpu.VMEM((8, strip_rows, LANES), f32)],
        compiler_params=params(),
        name="edge_cols",
    )(nests, keep)
    packed = lax.ppermute(packed, "lev", [(l, l ^ 1) for l in range(levs)])

    kept, *sends = pl.pallas_call(
        lambda *refs: pair_up_kernel(own, share, rim, *refs),
        in_specs=[VMEM_SPEC] * 2,
        out_specs=[VMEM_SPEC] * groups,
        out_shape=[shaped(2 * own, LANES)] + [shaped(2 * own + rim, LANES)] * (groups - 1),
        compiler_params=params(),
        name="pair_up",
    )(keep, got)
    nest_gots = [
        lax.ppermute(x, "nest", [(n, n ^ (i + 1)) for n in range(groups)])
        for i, x in enumerate(sends)
    ]

    edge_lines = (3 * fields * slot_count + bundles) * HALO
    to_pair, to_cross = pl.pallas_call(
        lambda *refs: edge_rows_kernel(fields, strip_rows, slot_count, *refs),
        in_specs=[VMEM_SPEC] * 2 + [ANY_SPEC],
        out_specs=[VMEM_SPEC] * 2,
        out_shape=[shaped(edge_lines, LANES)] * 2,
        compiler_params=params(),
        name="edge_rows",
    )(nests, packed, kept)
    pair = lax.ppermute(to_pair, "tile", pair_list)
    cross = lax.ppermute(to_cross, "tile", cross_list)

    def holds(source, dest):
        low = max((strip_rows // 3) * dest - 3, 0)
        high = tiles * rows - FP + min((strip_rows // 3) * (dest + 1) + 3, FP)
        return rows * source - RING < high and rows * (source + 1) + RING > low

    routes = {}
    for k in range(1, tiles):
        pairs = [
            (t, t ^ k)
            for t in range(tiles)
            if t ^ k < tiles and (holds(t, t ^ k) or holds(t ^ k, t) or abs(t - (t ^ k)) == 1)
        ]
        if pairs:
            routes[k] = pairs
    touching = tuple(k for k in routes if any(abs(a - b) == 1 for a, b in routes[k]))
    moves = (0, *routes)
    zone_shapes = [
        shaped(own + (rim if k in touching else rim + 8 if k > 0 else 0), LANES) for k in moves
    ]
    partial, zone_self, *zone_sends = pl.pallas_call(
        lambda *refs: aim_kernel(
            fields, rows, cols, strip_rows, strip_cols, slot_count, moves, share, touching, *refs
        ),
        in_specs=[SMEM_SPEC] + [VMEM_SPEC] * (2 + groups),
        out_specs=[VMEM_SPEC] * (1 + len(moves)),
        out_shape=[shaped(fields, 2, rows, cols), *zone_shapes],
        scratch_shapes=[pltpu.VMEM((2 * own, LANES), f32)],
        compiler_params=params(),
        name="aim",
    )(plan, ring, got, kept, *nest_gots)
    zone_gots = [lax.ppermute(x, "tile", routes[k]) for k, x in zip(moves[1:], zone_sends)]

    inner, side_in, row_in = pl.pallas_call(
        lambda *refs: advance_kernel(fields, strip_rows, strip_cols, slot_count, *refs),
        in_specs=[SMEM_SPEC] + [VMEM_SPEC] * 5,
        out_specs=[VMEM_SPEC] * 3,
        out_shape=[
            shaped(*nest_fields.shape),
            shaped(2, slot_count, strip_rows + 16, LANES),
            shaped(slot_count, fields, 2, 2, 32, LANES),
        ],
        scratch_shapes=[pltpu.VMEM((fields, 2, 2, strip_rows + 48, LANES), f32)]
        + [pltpu.VMEM((fields, 2, 2, strip_rows + 32, LANES), f32)] * 2,
        compiler_params=params(),
        name="advance",
    )(plan, rates, nests, pair, cross, packed)

    nest_final, parent_final = pl.pallas_call(
        lambda *refs: settle_kernel(
            fields, strip_rows, strip_cols, rows, slot_count, moves, touching, *refs
        ),
        in_specs=[SMEM_SPEC] + [VMEM_SPEC] * (5 + len(moves)),
        out_specs=[ANY_SPEC, VMEM_SPEC],
        out_shape=[shaped(*nest_fields.shape), shaped(*parent_field.shape)],
        scratch_shapes=[
            pltpu.VMEM((LANES, LANES), f32),
            pltpu.VMEM((LANES, LANES), f32),
            pltpu.VMEM((LANES, LANES), f32),
            pltpu.VMEM((slot_count, 3, STEPS * rim, LANES), f32),
            pltpu.VMEM((2, slot_count, strip_rows + 16, LANES), f32),
            pltpu.VMEM((2, slot_count, strip_rows + 32, LANES), f32),
            pltpu.VMEM((fields, 2, 2, 48, LANES), f32),
            pltpu.VMEM((fields, 2, 2, 32, LANES), f32),
            pltpu.VMEM((slot_count, fields, 2, strip_rows, strip_cols), f32),
            pltpu.SemaphoreType.DMA((slot_count,)),
        ],
        compiler_params=params(),
        name="settle",
    )(
        plan, rates, inner, side_in, row_in, partial, zone_self, *zone_gots,
    )
    return (parent_final, nest_final)


def solution(mesh):
    placed = (
        P("member", None, "tile", ("nest", "lev")),
        P(("member", "nest"), None, None, "tile", "lev"),
        P(),
        P(),
        P("member", None, None),
        P("member"),
    )
    return jax.shard_map(
        per_device,
        mesh=mesh,
        in_specs=placed,
        out_specs=(
            P("member", None, "tile", ("nest", "lev")),
            P(("member", "nest"), None, None, "tile", "lev"),
        ),
        check_vma=False,
    )
```

```python
import jax
import jax.numpy as jnp
from jax import lax
from jax.experimental import pallas as pl
from jax.experimental.pallas import tpu as pltpu
from jax.sharding import PartitionSpec as P

FP = 128
BWP = 2
MOVE = 2
STEPS = 2
BORDER = 3 * BWP
SPAN = 3 * FP
HALO = STEPS * (3 * MOVE + 1)
PAD = 16
LANES = 128
FRAME = 32
PLAN = 8
RING = STEPS
ROW_AT = 32
ZONE_AT = 72
SPLIT = -(FP // 4)
SLOT = 24
VMEM_LIMIT = 40 * 1024 * 1024

SMEM_SPEC = pl.BlockSpec(memory_space=pltpu.SMEM)
VMEM_SPEC = pl.BlockSpec(memory_space=pltpu.VMEM)
HBM_SPEC = pl.BlockSpec(memory_space=pltpu.HBM)
ANY_SPEC = pl.BlockSpec(memory_space=pl.ANY)


def params(**more):
    return pltpu.CompilerParams(vmem_limit_bytes=VMEM_LIMIT, **more)


def lane_iota(rows=1, lanes=LANES):
    return lax.broadcasted_iota(jnp.int32, (rows, lanes), 1)


def row_iota(rows, lanes=LANES):
    return lax.broadcasted_iota(jnp.int32, (rows, lanes), 0)


def beside(x, first_lane, last_lane):
    left = [pltpu.roll(v, 1, 1) for v in x]
    right = [pltpu.roll(v, LANES - 1, 1) for v in x]
    return [
        jnp.where(first_lane, left[1 - a], left[a]) + jnp.where(last_lane, right[1 - a], right[a])
        for a in range(2)
    ]


def third(values):
    return (values * 21846) >> 16


def strips_kernel(
    fields, rows, cols, storms, slot_count,
    centres_in, slots_in, lateral_in, vertical_in, parent_in, nests_in,
    send, keep, ring_out, plan, rates, nests,
    plain0, plain1, plain2, turned0, turned1, turned2, block, gather,
    centres, slots, lateral, vertical, parent, arrived,
):
    sources = (
        (centres_in, centres),
        (slots_in, slots),
        (lateral_in, lateral),
        (vertical_in, vertical),
        (parent_in, parent),
        (nests_in, nests),
    )
    copies = [
        pltpu.make_async_copy(source, target, arrived.at[i])
        for i, (source, target) in enumerate(sources)
    ]
    for copy in copies:
        copy.start()
    planes = 2 * fields
    tile_at, tiles = lax.axis_index("tile"), lax.axis_size("tile")
    lev_at, levs = lax.axis_index("lev"), lax.axis_size("lev")
    col_at = lax.axis_index("nest") * levs + lev_at
    col_blocks = lax.axis_size("nest") * levs
    top = 8
    height = rows + 16
    width = cols + 16

    lane = lane_iota()
    first_lane, last_lane = lane == 0, lane == LANES - 1
    row = tile_at * rows + row_iota(height) - top
    tile_cols = (lane, jnp.where(lane < LANES // 2, lane + LANES, lane - LANES))
    within = [
        (
            (row >= 0) & (row < tiles * rows)
            & (col_at * cols + c >= 0) & (col_at * cols + c < col_blocks * cols)
        ).astype(jnp.float32)
        for c in tile_cols
    ]
    plain0[...] = jnp.zeros_like(plain0)
    turned0[...] = jnp.zeros_like(turned0)
    block[...] = jnp.zeros_like(block)
    for copy in copies[:5]:
        copy.wait()
    for f in range(fields):
        rates[f : f + 1, :] = jnp.full((1, LANES), lateral[f], jnp.float32)
        rates[fields + f : fields + f + 1, :] = jnp.full((1, LANES), vertical[f], jnp.float32)
    for j in range(slot_count):
        storm = slots[lax.axis_index("nest") * slot_count + j]
        at = [[centres[n, d, storm] for d in range(2)] for n in range(STEPS + 1)]
        for d in range(2):
            plan[j * PLAN + d] = at[d + 1][0] - FP // 2
            plan[j * PLAN + 2 + d] = 3 * (at[STEPS][d] - at[0][d])
            plan[j * PLAN + 4 + d] = 3 * (at[STEPS][d] - at[STEPS - 1][d])
    for p in range(planes):
        plain0[p, 0, top : top + rows, :] = parent[p // 2, p % 2]
        block[ROW_AT : ROW_AT + rows, :] = parent[p // 2, p % 2]
        turned0[p, top : top + cols, :] = block[...].T

    inner = slice(1, height - 1)

    def plain_step(source, target, mask):
        for f in range(fields):
            lat, ver = lateral[f], vertical[f]
            for v in range(2):
                x = [source[2 * f + v, a, inner, :] for a in range(2)]
                sideways = beside(x, first_lane, last_lane)
                for a in range(2):
                    near = (
                        sideways[a]
                        + source[2 * f + v, a, 2:height, :]
                        + source[2 * f + v, a, 0 : height - 2, :]
                    )
                    other = source[2 * f + 1 - v, a, inner, :]
                    new = x[a] + lat * (near - 4.0 * x[a]) + ver * (other - 2.0 * x[a])
                    if mask is not None:
                        new = new * mask[a][inner, :]
                    target[2 * f + v, a, inner, :] = new
                    for edge in (0, height - 1):
                        target[2 * f + v, a, edge : edge + 1, :] = jnp.zeros(
                            (1, LANES), jnp.float32
                        )

    plain_step(plain0, plain1, within)
    plain_step(plain1, plain2, None)

    row_t = tile_at * rows + lane_iota() - ROW_AT
    col_t = col_at * cols + row_iota(width) - top
    within_t = (
        (row_t >= 0) & (row_t < tiles * rows) & (col_t >= 0) & (col_t < col_blocks * cols)
    ).astype(jnp.float32)

    def turned_step(source, target, mask):
        for f in range(fields):
            lat, ver = lateral[f], vertical[f]
            for v in range(2):
                x = source[2 * f + v, 1 : width - 1, :]
                near = (
                    source[2 * f + v, 2:width, :]
                    + source[2 * f + v, 0 : width - 2, :]
                    + pltpu.roll(x, 1, 1)
                    + pltpu.roll(x, LANES - 1, 1)
                )
                other = source[2 * f + 1 - v, 1 : width - 1, :]
                new = x + lat * (near - 4.0 * x) + ver * (other - 2.0 * x)
                if mask is not None:
                    new = new * mask[1 : width - 1, :]
                target[2 * f + v, 1 : width - 1, :] = new
                target[2 * f + v, 0:1, :] = jnp.zeros((1, LANES), jnp.float32)
                target[2 * f + v, width - 1 : width, :] = jnp.zeros((1, LANES), jnp.float32)

    turned_step(turned0, turned1, within_t)
    turned_step(turned1, turned2, None)

    share = storms * STEPS * planes * BWP
    for j in range(storms):
        storm = slots[j]
        for s in range(STEPS):
            at = (j * STEPS + s) * planes * BWP
            corner_row = centres[s + 1, 0, storm] - FP // 2 - tile_at * rows
            corner_col = centres[s + 1, 1, storm] - FP // 2 - col_at * cols
            plain = (plain1, plain2)[s]
            turned = (turned1, turned2)[s]
            first = jnp.where(corner_row >= SPLIT, corner_row, corner_row + FP - BWP)
            first = jnp.clip(first + top, 0, height - BWP)
            for p in range(planes):
                for a in range(2):
                    gather[a, BWP * p : BWP * (p + 1), :] = plain[p, a, pl.ds(first, BWP), :]
            shift = (64 * LANES - corner_col) % LANES
            window = [pltpu.roll(gather[a], shift, 1) for a in range(2)]
            place = lane + corner_col
            main = (place >= 0) & (place < cols)
            rim = (place >= -RING) & (place < cols + RING)
            window = jnp.where(main, window[0], jnp.where(rim, window[1], 0.0))[: planes * BWP]
            send[at : at + planes * BWP, :] = window
            keep[at : at + planes * BWP, :] = window
            mine = corner_col + (FP - BWP) * lev_at
            theirs = corner_col + (FP - BWP) * (levs - 1 - lev_at)
            for target, start in ((keep, mine), (send, theirs)):
                start = jnp.clip(start + top, 0, width - BWP)
                for p in range(planes):
                    target[share + at + BWP * p : share + at + BWP * (p + 1), :] = turned[
                        p, pl.ds(start, BWP), :
                    ]
    for p in range(planes):
        send[2 * share + BWP * p : 2 * share + BWP * (p + 1), :] = turned2[p, top - RING : top, :]
        at = 2 * share + planes * BWP + BWP * p
        send[at : at + BWP, :] = turned2[p, top + cols : top + cols + RING, :]
        ring_out[p] = turned2[p, top : top + cols, :]
    copies[5].wait()


def pair_up_kernel(own, share, rim, keep, got, kept, *sends):
    nest_at = lax.axis_index("nest")
    lev_at = lax.axis_index("lev")
    for k in range(len(sends) + 1):
        group = lax.bitwise_xor(nest_at, k)
        target = kept if k == 0 else sends[k - 1]
        for part in range(2):
            rows = pl.ds(pl.multiple_of(part * share + group * own, 8), own)
            target[part * own : (part + 1) * own, :] = keep[rows, :] + got[rows, :]
        if k > 0:
            west = got[2 * share : 2 * share + rim, :]
            east = got[2 * share + rim : 2 * share + 2 * rim, :]
            target[2 * own : 2 * own + rim, :] = jnp.where(lev_at == 0, east, west)


def aim_kernel(
    fields, rows, cols, strip_rows, strip_cols, slot_count, moves, share, touching,
    plan, ring, first_got, kept, *refs,
):
    crossing = lax.axis_size("nest") - 1
    nest_gots, rest = refs[:crossing], refs[crossing + 1 :]
    partial, zone_self, zone_sends, total = rest[0], rest[1], rest[2:-1], rest[-1]
    planes = 2 * fields
    rim = planes * BWP
    own = slot_count * STEPS * rim
    tile_at, tiles = lax.axis_index("tile"), lax.axis_size("tile")
    nest_at = lax.axis_index("nest")
    lev_at = lax.axis_index("lev")

    sums = kept[...]
    for got in nest_gots:
        sums = sums + got[0 : 2 * own, :]
    total[...] = sums

    lane = lane_iota()
    col_base = lev_at * (strip_cols // 3 - 3)
    for j in range(slot_count):
        at = j * STEPS * rim
        both = STEPS * rim
        strip = pltpu.roll(total[at : at + both, :], (LANES - col_base) % LANES, 1)
        side = total[own + at : own + at + both, :]
        second = row_iota(both) >= rim
        origins = [plan[j * PLAN + s] - tile_at * rows for s in range(STEPS)]
        for k in moves:
            dest = lax.bitwise_xor(tile_at, k)
            parts = []
            for s in range(STEPS):
                south = origins[s] >= SPLIT
                wanted = ((dest == 0) & south) | ((dest == tiles - 1) & jnp.logical_not(south))
                offset = ROW_AT + origins[s] + (strip_rows // 3) * dest - 3 - ZONE_AT
                source = lane + offset
                fits = (source >= ROW_AT - RING) & (source < ROW_AT + rows + RING)
                turned = pltpu.roll(side, (64 * LANES - offset) % LANES, 1)
                turned = jnp.where(fits, turned, 0.0)
                parts.append(
                    jnp.where(lane < ZONE_AT, strip * wanted.astype(jnp.float32), turned)
                )
            target = zone_self if k == 0 else zone_sends[moves.index(k) - 1]
            target[at : at + both, :] = jnp.where(second, parts[1], parts[0])

    from_west = first_got[2 * share + rim : 2 * share + 2 * rim, :]
    from_east = first_got[2 * share : 2 * share + rim, :]
    far_west = jnp.zeros((rim, LANES), jnp.float32)
    far_east = jnp.zeros((rim, LANES), jnp.float32)
    for i, got in enumerate(nest_gots):
        other = lax.bitwise_xor(nest_at, i + 1)
        edge = got[2 * own : 2 * own + rim, :]
        far_west = far_west + jnp.where(other == nest_at - 1, edge, 0.0)
        far_east = far_east + jnp.where(other == nest_at + 1, edge, 0.0)
    from_west = jnp.where(lev_at == 0, far_west, from_west)
    from_east = jnp.where(lev_at == 0, from_east, far_east)
    for p in range(planes):
        two = slice(BWP * p, BWP * (p + 1))
        total[0:cols, :] = ring[p]
        total[0:RING, :] = total[0:RING, :] + from_west[two]
        total[cols - RING : cols, :] = total[cols - RING : cols, :] + from_east[two]
        total[0:LANES, :] = total[0:cols, :].T
        partial[p // 2, p % 2] = total[ROW_AT : ROW_AT + rows, :]
        below = total[ROW_AT - RING : ROW_AT, :]
        above = total[ROW_AT + rows : ROW_AT + rows + RING, :]
        for i, k in enumerate(moves[1:]):
            if k in touching:
                dest = lax.bitwise_xor(tile_at, k)
                zone_sends[i][own + BWP * p : own + BWP * (p + 1), :] = jnp.where(
                    dest > tile_at, above, below
                )


def edge_cols_kernel(fields, slot_count, nests, after, packed, wide):
    del after
    west_most = lax.axis_index("lev") == 0
    planes = 2 * fields
    half = nests.shape[4] - LANES
    wide[...] = jnp.zeros_like(wide)
    lane = lane_iota()
    for q in range(slot_count * planes):
        j, f, v = q // planes, (q % planes) // 2, q % 2
        spot = (q % 8) * 16
        wide[q % 8, :, 0:half] = nests[j, f, v, :, LANES : LANES + half]
        cells = jnp.where(west_most, wide[q % 8], nests[j, f, v, :, 0:LANES])
        shift = jnp.where(west_most, spot + 2 * LANES - (half - HALO), spot + 2 * LANES) % LANES
        cells = pltpu.roll(cells, shift, 1)
        row = cells if q % 8 == 0 else jnp.where(lane >= spot, cells, row)
        if q % 8 == 7 or q == slot_count * planes - 1:
            packed[q // 8] = row


def edge_rows_kernel(fields, strip_rows, slot_count, nests, packed, after, to_pair, to_cross):
    del after
    even = lax.rem(lax.axis_index("tile"), 2) == 0
    half = nests.shape[4] - LANES
    lows, highs, tail = slice(0, HALO), slice(strip_rows - HALO, strip_rows), slice(LANES, LANES + half)

    def put(at, low, high):
        to_pair[at : at + HALO, :] = jnp.where(even, high, low)
        to_cross[at : at + HALO, :] = jnp.where(even, low, high)

    for j in range(slot_count):
        for f in range(fields):
            at = (3 * fields * j + 2 * f) * HALO
            for v in range(2):
                put(at + v * HALO, nests[j, f, v, lows, 0:LANES], nests[j, f, v, highs, 0:LANES])
            at = (3 * fields * j + 2 * fields + f) * HALO
            put(
                at,
                jnp.concatenate([nests[j, f, v, lows, tail] for v in range(2)], 1),
                jnp.concatenate([nests[j, f, v, highs, tail] for v in range(2)], 1),
            )
    for g in range(packed.shape[0]):
        at = (3 * fields * slot_count + g) * HALO
        put(at, packed[g, lows, :], packed[g, highs, :])


def shift_kernel(fields, strip_rows, strip_cols, slot_count, plan, nests, packed, moved, cells):
    planes = 2 * fields
    half = strip_cols - LANES
    room = PAD + 8
    height = strip_rows + 16
    lane = lane_iota()
    goal = jnp.where(lax.axis_index("lev") == 0, half, LANES - HALO)
    in_goal = (lane >= goal) & (lane < goal + HALO)
    cells[...] = jnp.zeros_like(cells)

    def one(j, _):
        down, right = plan[j * PLAN + 2], plan[j * PLAN + 3]
        shift = (LANES - right) % LANES
        same = (lane + right >= 0) & (lane + right < LANES)
        start = room - 8 + down
        for f in range(fields):
            for v in range(2):
                cells[f, v, 0, room : room + strip_rows, :] = nests[j, f, v, :, 0:LANES]
                cells[f, v, 1, room : room + strip_rows, 0:half] = nests[j, f, v, :, LANES : LANES + half]
                n = j * planes + 2 * f + v
                goal_shift = (goal - lax.rem(n, 8) * 16 + 2 * LANES) % LANES
                got = jnp.where(in_goal, pltpu.roll(packed[lax.div(n, 8)], goal_shift, 1), 0.0)
                cells[f, v, 1, room : room + strip_rows, half:LANES] = got[:, half:LANES]
        for f in range(fields):
            for v in range(2):
                both = [
                    pltpu.roll(cells[f, v, a, pl.ds(start, height), :], shift, 1) for a in range(2)
                ]
                for a in range(2):
                    moved[j, f, v, a] = jnp.where(same, both[a], both[1 - a])
        return 0

    lax.fori_loop(0, slot_count, one, 0)


def advance_kernel(
    fields, strip_rows, strip_cols, slot_count,
    plan, rates, moved, pair, cross,
    inner_out, side_out, row_out, first, second,
):
    planes = 2 * fields
    half = strip_cols - LANES
    height = strip_rows + 16
    tile_at = lax.axis_index("tile")
    lev_at = lax.axis_index("lev")
    even = lax.rem(tile_at, 2) == 0
    lane = lane_iota()
    first_lane, last_lane = lane == 0, lane == LANES - 1
    chunk = 16 if height % 16 == 0 and strip_rows % 16 == 0 else 8
    row_start = pl.multiple_of(jnp.where(tile_at == 0, 0, strip_rows - 16), 8)
    west_lanes = lane < jnp.where(lev_at == 0, LANES // 2, 0)
    goal = jnp.where(lev_at == 0, half, LANES - HALO)
    in_goal = (lane >= goal) & (lane < goal + HALO)

    lats = [rates[f : f + 1, :] for f in range(fields)]
    vers = [rates[fields + f : fields + f + 1, :] for f in range(fields)]
    stays = [1.0 - 4.0 * lats[f] - 2.0 * vers[f] for f in range(fields)]

    def stencil(f, source, at, size):
        x = [[source[f, v, a, at : at + size, :] for a in range(2)] for v in range(2)]
        new = [[None] * 2, [None] * 2]
        for v in range(2):
            sideways = beside(x[v], first_lane, last_lane)
            for a in range(2):
                near = (
                    sideways[a]
                    + source[f, v, a, at - 1 : at + size - 1, :]
                    + source[f, v, a, at + 1 : at + size + 1, :]
                )
                new[v][a] = stays[f] * x[v][a] + lats[f] * near + vers[f] * x[1 - v][a]
        return new

    def one(j, _):
        down, right = plan[j * PLAN + 2], plan[j * PLAN + 3]
        shift = (LANES - right) % LANES
        same = (lane + right >= 0) & (lane + right < LANES)
        for f in range(fields):
            for v in range(2):
                n = j * planes + 2 * f + v
                goal_shift = (goal - lax.rem(n, 8) * 16 + 2 * LANES) % LANES
                ends = []
                for got in (pair, cross):
                    main = got[pl.ds((3 * fields * j + 2 * f + v) * HALO, HALO), :]
                    tail = got[pl.ds((3 * fields * j + planes + f) * HALO, HALO), :]
                    if v == 1:
                        tail = pltpu.roll(tail, LANES - half, 1)
                    corner = got[pl.ds((3 * fields * slot_count + lax.div(n, 8)) * HALO, HALO), :]
                    corner = jnp.where(in_goal, pltpu.roll(corner, goal_shift, 1), 0.0)
                    tail = jnp.where(lane < half, tail, corner)
                    turned = [pltpu.roll(main, shift, 1), pltpu.roll(tail, shift, 1)]
                    ends.append([jnp.where(same, turned[a], turned[1 - a]) for a in range(2)])
                for a in range(2):
                    first[f, v, a, FRAME - 8 : FRAME - 8 + height, :] = moved[j, f, v, a]
                    low = jnp.where(even, ends[1][a], ends[0][a])
                    high = jnp.where(even, ends[0][a], ends[1][a])
                    first[f, v, a, pl.ds(FRAME - HALO - down, HALO), :] = low
                    first[f, v, a, pl.ds(FRAME + strip_rows - down, HALO), :] = high

        sides = [None, None]
        for f in range(fields):
            for v in range(2):
                both = [first[f, v, a, FRAME - 8 : FRAME - 8 + height, :] for a in range(2)]
                near = jnp.where(west_lanes, both[0], both[1])
                turn = jnp.where(lev_at == 0, 8, LANES + 16 - half) + f * SLOT
                near = pltpu.roll(near, turn % LANES, 1)
                sides[v] = near if f == 0 else jnp.where(lane >= f * SLOT, near, sides[v])
        for v in range(2):
            side_out[v, j] = sides[v]
        for f in range(fields):
            for v in range(2):
                for a in range(2):
                    row_out[j, f, v, a] = first[f, v, a, pl.ds(FRAME - 8 + row_start, 32), :]
            for c in range(0, height, chunk):
                new = stencil(f, first, FRAME - 8 + c, chunk)
                for v in range(2):
                    for a in range(2):
                        second[f, v, a, 8 + c : 8 + c + chunk, :] = new[v][a]
        for f in range(fields):
            for c in range(0, strip_rows, chunk):
                new = stencil(f, second, 16 + c, chunk)
                for v in range(2):
                    inner_out[j, f, v, c : c + chunk, 0:LANES] = new[v][0]
                    inner_out[j, f, v, c : c + chunk, LANES : LANES + half] = new[v][1][:, :half]
        return 0

    lax.fori_loop(0, slot_count, one, 0)


def gaps(i):
    return jnp.minimum(i, SPAN - 1 - i)


def settle_kernel(
    fields, strip_rows, strip_cols, rows, slot_count, moves, touching,
    plan, rates, inner, side_in, row_in, partial, zone_self, *refs,
):
    count = len(moves) - 1
    zone_gots = refs[:count]
    nest_out, parent_out = refs[count : count + 2]
    zone, turned, sides, strips, side_new, mixed, rows_mixed, rows_new, whole, done = refs[count + 2 :]
    planes = 2 * fields
    rim = planes * BWP
    both = STEPS * rim
    own = slot_count * both
    half = strip_cols - LANES
    height = strip_rows + 16
    tile_at, tiles = lax.axis_index("tile"), lax.axis_size("tile")
    nest_at = lax.axis_index("nest")
    lev_at = lax.axis_index("lev")
    lane = lane_iota()
    first_lane, last_lane = lane == 0, lane == LANES - 1

    below = jnp.zeros((rim, LANES), jnp.float32)
    above = jnp.zeros((rim, LANES), jnp.float32)
    for i, k in enumerate(moves[1:]):
        if k in touching:
            other = lax.bitwise_xor(tile_at, k)
            edge = zone_gots[i][own : own + rim, :]
            below = below + jnp.where(other == tile_at - 1, edge, 0.0)
            above = above + jnp.where(other == tile_at + 1, edge, 0.0)
    for p in range(planes):
        f, v = p // 2, p % 2
        two = slice(BWP * p, BWP * (p + 1))
        parent_out[f, v] = partial[f, v]
        parent_out[f, v, 0:RING, :] = partial[f, v, 0:RING, :] + below[two]
        parent_out[f, v, rows - RING : rows, :] = partial[f, v, rows - RING : rows, :] + above[two]

    whole_move = [[plan[j * PLAN + 2 + d] for d in range(2)] for j in range(slot_count)]
    last_move = [[plan[j * PLAN + 4 + d] for d in range(2)] for j in range(slot_count)]
    offsets = [[(0, 0) if s == 1 else last_move[j] for s in range(STEPS)] for j in range(slot_count)]
    earlier = [[whole_move[j], last_move[j]] for j in range(slot_count)]

    total = zone_self[0:own, :]
    for got in zone_gots:
        total = total + got[0:own, :]
    zone[...] = jnp.zeros_like(zone)
    zone[0:own, :] = total
    second = row_iota(both) >= rim
    col_base = lev_at * (strip_cols // 3 - 3)
    col_from = lev_at * strip_cols
    gap = (half + LANES) // 2
    owner = jnp.zeros((1, LANES), jnp.int32)
    for f in range(1, fields):
        owner = owner + (lane >= f * SLOT).astype(jnp.int32)
    side_cols = lane - SLOT * owner + jnp.where(lev_at == 0, -8, 2 * strip_cols - 16)
    lane_cols = (
        lane + col_from,
        jnp.where(lane < gap, lane + LANES, lane - LANES) + col_from,
        side_cols,
    )
    for j in range(slot_count):
        block = zone[j * both : (j + 1) * both, :]
        for a in range(3):
            picks = [
                jnp.clip(third(jnp.clip(lane_cols[a] + offsets[j][s][1], 0, SPAN - 1)) - col_base, 0, ZONE_AT - 1)
                for s in range(STEPS)
            ]
            strips[j, a] = jnp.take_along_axis(block, jnp.where(second, picks[1], picks[0]), axis=1)
        picks = [
            jnp.clip(
                third(jnp.clip(lane + (tile_at * strip_rows - 8) + offsets[j][s][0], 0, SPAN - 1))
                - ((strip_rows // 3) * tile_at - 3)
                + ZONE_AT,
                ZONE_AT,
                LANES - 1,
            )
            for s in range(STEPS)
        ]
        turned[j * both : (j + 1) * both, :] = jnp.take_along_axis(
            block, jnp.where(second, picks[1], picks[0]), axis=1
        )
    sides[...] = turned[...].T

    chunk = 16 if height % 16 == 0 else 8
    lats = [rates[f : f + 1, :] for f in range(fields)]
    vers = [rates[fields + f : fields + f + 1, :] for f in range(fields)]
    lat, ver = lats[0], vers[0]
    for f in range(1, fields):
        lat = jnp.where(owner >= f, lats[f], lat)
        ver = jnp.where(owner >= f, vers[f], ver)
    stay = 4.0 * lat + 2.0 * ver
    for s in range(STEPS):
        insides = {}
        for j in range(slot_count):
            by_row, by_col = offsets[j][s]
            was_row, was_col = earlier[j][s]
            col = side_cols + by_col
            col_gap = gaps(col)
            col_kept = gaps(side_cols + was_col)
            depth = jnp.where((col < 3) | ((col >= SPAN // 2) & (col < SPAN - 3)), 0, 1)
            lines, picks = [], []
            for v in range(2):
                picks.append(jnp.minimum(j * both + s * rim + v * BWP + 2 * BWP * owner + depth, own - 1))
                pair_of = []
                for r in range(BWP):
                    n = s * rim + v * BWP + r
                    line = strips[j, 2, n : n + 1, :]
                    for f in range(1, fields):
                        m = n + 2 * BWP * f
                        line = jnp.where(owner >= f, strips[j, 2, m : m + 1, :], line)
                    pair_of.append(line)
                lines.append(pair_of)
            for c in range(0, height, chunk):
                base = row_iota(chunk) + (tile_at * strip_rows - 8 + c)
                i = base + by_row
                distance = jnp.minimum(gaps(i), col_gap)
                kept = jnp.minimum(gaps(base + was_row), col_kept)
                w = jnp.clip(BORDER - distance, 0, BORDER).astype(jnp.float32) * (1.0 / BORDER)
                w = jnp.where(kept >= 0, w, 1.0)
                in_rows = (i < BORDER) | (i >= SPAN - BORDER)
                early = (i < 3) | ((i >= SPAN // 2) & (i < SPAN - 3))
                insides[j, c] = (distance >= 1).astype(jnp.float32)
                for v in range(2):
                    pick = jnp.broadcast_to(picks[v], (chunk, LANES))
                    side = jnp.take_along_axis(sides[c : c + chunk, :], pick, axis=1)
                    strip = jnp.where(early, lines[v][0], lines[v][1])
                    driving = jnp.where(in_rows, strip, side)
                    x = side_in[v, j, c : c + chunk, :] if s == 0 else side_new[v, j, c : c + chunk, :]
                    mixed[v, j, 8 + c : 8 + c + chunk, :] = (1.0 - w) * x + w * driving
        for j in range(slot_count):
            for c in range(0, height, chunk):
                x = [mixed[v, j, 8 + c : 8 + c + chunk, :] for v in range(2)]
                for v in range(2):
                    near = (
                        pltpu.roll(x[v], 1, 1)
                        + pltpu.roll(x[v], LANES - 1, 1)
                        + mixed[v, j, 7 + c : 7 + c + chunk, :]
                        + mixed[v, j, 9 + c : 9 + c + chunk, :]
                    )
                    change = lat * near + ver * x[1 - v] - stay * x[v]
                    side_new[v, j, c : c + chunk, :] = x[v] + insides[j, c] * change

    outer = (tile_at == 0) | (tile_at == tiles - 1)
    window = jnp.where(tile_at == 0, -8, tile_at * strip_rows + strip_rows - 24)
    row_start = pl.multiple_of(jnp.where(tile_at == 0, 0, strip_rows - 16), 8)
    line = row_iota(16)
    line_from = jnp.where(tile_at == 0, 0, 16 - HALO)
    lows = (0, jnp.where(lev_at > 0, half - HALO, LANES))
    highs = (jnp.where(lev_at == 0, HALO, 0), half)
    along = lane_iota(strip_rows)
    near_col = [(along >= lows[a]) & (along < highs[a]) for a in range(2)]
    across = lane_iota(16)
    near_row = [
        (line >= line_from)
        & (line < line_from + HALO)
        & ((across < lows[a]) | (across >= highs[a]))
        for a in range(2)
    ]

    def one(j, _):
        for f in range(fields):
            back = (2 * LANES + jnp.where(lev_at == 0, -8, half - 16) - f * SLOT) % LANES
            for v in range(2):
                near = pltpu.roll(side_new[v, j, 8 : 8 + strip_rows, :], back, 1)
                whole[j, f, v, :, 0:LANES] = jnp.where(near_col[0], near, inner[j, f, v, :, 0:LANES])
                whole[j, f, v, :, LANES : LANES + half] = jnp.where(
                    near_col[1][:, :half], near[:, :half], inner[j, f, v, :, LANES : LANES + half]
                )

        @pl.when(outer)
        def _():
            full, last = plan[j * PLAN + 2], plan[j * PLAN + 4]
            base = row_iota(32) + window
            for s in range(STEPS):
                i = base + (last if s == 0 else 0)
                kept = gaps(base + (full if s == 0 else last)) >= 0
                w = jnp.clip(BORDER - gaps(i), 0, BORDER).astype(jnp.float32) * (1.0 / BORDER)
                w = jnp.where(kept, w, 1.0)
                rest = 1.0 - w
                inside = (gaps(i) >= 1).astype(jnp.float32)
                early = (i < 3) | ((i >= SPAN // 2) & (i < SPAN - 3))
                for f in range(fields):
                    for v in range(2):
                        n = s * rim + (2 * f + v) * BWP
                        for a in range(2):
                            driving = jnp.where(
                                early, strips[j, a, n : n + 1, :], strips[j, a, n + 1 : n + 2, :]
                            )
                            x = row_in[j, f, v, a] if s == 0 else rows_new[f, v, a]
                            rows_mixed[f, v, a, 8:40, :] = rest * x + w * driving
                for f in range(fields):
                    stay = 4.0 * lats[f] + 2.0 * vers[f]
                    value = [[rows_mixed[f, v, a, 8:40, :] for a in range(2)] for v in range(2)]
                    for v in range(2):
                        sideways = beside(value[v], first_lane, last_lane)
                        for a in range(2):
                            near = (
                                sideways[a]
                                + rows_mixed[f, v, a, 7:39, :]
                                + rows_mixed[f, v, a, 9:41, :]
                            )
                            change = (
                                lats[f] * near + vers[f] * value[1 - v][a] - stay * value[v][a]
                            )
                            rows_new[f, v, a] = value[v][a] + inside * change
            for f in range(fields):
                for v in range(2):
                    target = pl.ds(row_start, 16)
                    whole[j, f, v, target, 0:LANES] = jnp.where(
                        near_row[0], rows_new[f, v, 0, 8:24, :], whole[j, f, v, target, 0:LANES]
                    )
                    whole[j, f, v, target, LANES : LANES + half] = jnp.where(
                        near_row[1][:, :half],
                        rows_new[f, v, 1, 8:24, 0:half],
                        whole[j, f, v, target, LANES : LANES + half],
                    )

        pltpu.make_async_copy(whole.at[j], nest_out.at[j], done.at[j]).start()
        return 0

    lax.fori_loop(0, slot_count, one, 0)

    def wait(j, _):
        pltpu.make_async_copy(whole.at[j], nest_out.at[j], done.at[j]).wait()
        return 0

    lax.fori_loop(0, slot_count, wait, 0)


def per_device(parent_field, nest_fields, lateral_rate, vertical_rate, centres, slot_storm):
    fields, _, rows, cols = parent_field.shape
    slot_count, _, _, strip_rows, strip_cols = nest_fields.shape
    storms = slot_storm.shape[0]
    tiles, groups, levs = lax.axis_size("tile"), lax.axis_size("nest"), lax.axis_size("lev")
    planes = 2 * fields
    rim = planes * BWP
    share = storms * STEPS * rim
    own = slot_count * STEPS * rim
    height = strip_rows + 2 * PAD
    half = strip_cols - LANES
    f32 = jnp.float32

    def shaped(*dims):
        return jax.ShapeDtypeStruct(dims, f32)

    pair_list = [(t, t ^ 1) for t in range(tiles) if t ^ 1 < tiles]
    cross_list = [(t, t - 1 if t % 2 == 0 else t + 1) for t in range(1, tiles - 1)]
    centres = jnp.swapaxes(centres, 1, 2)

    send, keep, ring, plan, rates, nests = pl.pallas_call(
        lambda *refs: strips_kernel(fields, rows, cols, storms, slot_count, *refs),
        in_specs=[HBM_SPEC] * 6,
        out_specs=[VMEM_SPEC] * 3 + [SMEM_SPEC] + [VMEM_SPEC] * 2,
        out_shape=[
            shaped(2 * share + 2 * rim, LANES),
            shaped(2 * share, LANES),
            shaped(planes, cols, LANES),
            jax.ShapeDtypeStruct((slot_count * PLAN,), jnp.int32),
            shaped(2 * fields, LANES),
            shaped(*nest_fields.shape),
        ],
        scratch_shapes=[pltpu.VMEM((planes, 2, rows + 16, LANES), f32)] * 3
        + [pltpu.VMEM((planes, cols + 16, LANES), f32)] * 3
        + [
            pltpu.VMEM((LANES, LANES), f32),
            pltpu.VMEM((2, 24, LANES), f32),
            pltpu.SMEM(centres.shape, jnp.int32),
            pltpu.SMEM(slot_storm.shape, jnp.int32),
            pltpu.SMEM(lateral_rate.shape, f32),
            pltpu.SMEM(vertical_rate.shape, f32),
            pltpu.VMEM(parent_field.shape, f32),
            pltpu.SemaphoreType.DMA((6,)),
        ],
        compiler_params=params(),
        name="strips",
    )(
        *(
            pltpu.with_memory_space_constraint(x, pltpu.HBM)
            for x in (centres, slot_storm, lateral_rate, vertical_rate, parent_field, nest_fields)
        )
    )
    got = lax.ppermute(send, "lev", [(l, l ^ 1) for l in range(levs)])

    bundles = -(-slot_count * planes // 8)
    packed = pl.pallas_call(
        lambda *refs: edge_cols_kernel(fields, slot_count, *refs),
        in_specs=[VMEM_SPEC, ANY_SPEC],
        out_specs=VMEM_SPEC,
        out_shape=shaped(bundles, strip_rows, LANES),
        scratch_shapes=[pltpu.VMEM((8, strip_rows, LANES), f32)],
        compiler_params=params(),
        name="edge_cols",
    )(nests, keep)
    packed = lax.ppermute(packed, "lev", [(l, l ^ 1) for l in range(levs)])

    kept, *sends = pl.pallas_call(
        lambda *refs: pair_up_kernel(own, share, rim, *refs),
        in_specs=[VMEM_SPEC] * 2,
        out_specs=[VMEM_SPEC] * groups,
        out_shape=[shaped(2 * own, LANES)] + [shaped(2 * own + rim, LANES)] * (groups - 1),
        compiler_params=params(),
        name="pair_up",
    )(keep, got)
    nest_gots = [
        lax.ppermute(x, "nest", [(n, n ^ (i + 1)) for n in range(groups)])
        for i, x in enumerate(sends)
    ]

    edge_lines = (3 * fields * slot_count + bundles) * HALO
    to_pair, to_cross = pl.pallas_call(
        lambda *refs: edge_rows_kernel(fields, strip_rows, slot_count, *refs),
        in_specs=[VMEM_SPEC] * 2 + [ANY_SPEC],
        out_specs=[VMEM_SPEC] * 2,
        out_shape=[shaped(edge_lines, LANES)] * 2,
        compiler_params=params(),
        name="edge_rows",
    )(nests, packed, kept)
    pair = lax.ppermute(to_pair, "tile", pair_list)
    cross = lax.ppermute(to_cross, "tile", cross_list)

    moved = pl.pallas_call(
        lambda *refs: shift_kernel(fields, strip_rows, strip_cols, slot_count, *refs),
        in_specs=[SMEM_SPEC] + [VMEM_SPEC] * 2,
        out_specs=VMEM_SPEC,
        out_shape=shaped(slot_count, fields, 2, 2, strip_rows + 16, LANES),
        scratch_shapes=[pltpu.VMEM((fields, 2, 2, strip_rows + 48, LANES), f32)],
        compiler_params=params(),
        cost_estimate=pl.CostEstimate(flops=3_000_000_000, bytes_accessed=10_000_000, transcendentals=0),
        name="shift",
    )(plan, nests, packed)

    def holds(source, dest):
        low = max((strip_rows // 3) * dest - 3, 0)
        high = tiles * rows - FP + min((strip_rows // 3) * (dest + 1) + 3, FP)
        return rows * source - RING < high and rows * (source + 1) + RING > low

    routes = {}
    for k in range(1, tiles):
        pairs = [
            (t, t ^ k)
            for t in range(tiles)
            if t ^ k < tiles and (holds(t, t ^ k) or holds(t ^ k, t) or abs(t - (t ^ k)) == 1)
        ]
        if pairs:
            routes[k] = pairs
    touching = tuple(k for k in routes if any(abs(a - b) == 1 for a, b in routes[k]))
    moves = (0, *routes)
    zone_shapes = [
        shaped(own + (rim if k in touching else rim + 8 if k > 0 else 0), LANES) for k in moves
    ]
    partial, zone_self, *zone_sends = pl.pallas_call(
        lambda *refs: aim_kernel(
            fields, rows, cols, strip_rows, strip_cols, slot_count, moves, share, touching, *refs
        ),
        in_specs=[SMEM_SPEC] + [VMEM_SPEC] * (2 + groups) + [ANY_SPEC],
        out_specs=[VMEM_SPEC] * (1 + len(moves)),
        out_shape=[shaped(fields, 2, rows, cols), *zone_shapes],
        scratch_shapes=[pltpu.VMEM((2 * own, LANES), f32)],
        compiler_params=params(),
        name="aim",
    )(plan, ring, got, kept, *nest_gots, moved)
    zone_gots = [lax.ppermute(x, "tile", routes[k]) for k, x in zip(moves[1:], zone_sends)]

    inner, side_in, row_in = pl.pallas_call(
        lambda *refs: advance_kernel(fields, strip_rows, strip_cols, slot_count, *refs),
        in_specs=[SMEM_SPEC] + [VMEM_SPEC] * 4,
        out_specs=[VMEM_SPEC] * 3,
        out_shape=[
            shaped(*nest_fields.shape),
            shaped(2, slot_count, strip_rows + 16, LANES),
            shaped(slot_count, fields, 2, 2, 32, LANES),
        ],
        scratch_shapes=[
            pltpu.VMEM((fields, 2, 2, strip_rows + 2 * FRAME, LANES), f32),
            pltpu.VMEM((fields, 2, 2, strip_rows + 32, LANES), f32),
        ],
        compiler_params=params(),
        name="advance",
    )(plan, rates, moved, pair, cross)

    nest_final, parent_final = pl.pallas_call(
        lambda *refs: settle_kernel(
            fields, strip_rows, strip_cols, rows, slot_count, moves, touching, *refs
        ),
        in_specs=[SMEM_SPEC] + [VMEM_SPEC] * (5 + len(moves)),
        out_specs=[ANY_SPEC, VMEM_SPEC],
        out_shape=[shaped(*nest_fields.shape), shaped(*parent_field.shape)],
        scratch_shapes=[
            pltpu.VMEM((LANES, LANES), f32),
            pltpu.VMEM((LANES, LANES), f32),
            pltpu.VMEM((LANES, LANES), f32),
            pltpu.VMEM((slot_count, 3, STEPS * rim, LANES), f32),
            pltpu.VMEM((2, slot_count, strip_rows + 16, LANES), f32),
            pltpu.VMEM((2, slot_count, strip_rows + 32, LANES), f32),
            pltpu.VMEM((fields, 2, 2, 48, LANES), f32),
            pltpu.VMEM((fields, 2, 2, 32, LANES), f32),
            pltpu.VMEM((slot_count, fields, 2, strip_rows, strip_cols), f32),
            pltpu.SemaphoreType.DMA((slot_count,)),
        ],
        compiler_params=params(),
        name="settle",
    )(
        plan, rates, inner, side_in, row_in, partial, zone_self, *zone_gots,
    )
    return (parent_final, nest_final)


def solution(mesh):
    placed = (
        P("member", None, "tile", ("nest", "lev")),
        P(("member", "nest"), None, None, "tile", "lev"),
        P(),
        P(),
        P("member", None, None),
        P("member"),
    )
    return jax.shard_map(
        per_device,
        mesh=mesh,
        in_specs=placed,
        out_specs=(
            P("member", None, "tile", ("nest", "lev")),
            P(("member", "nest"), None, None, "tile", "lev"),
        ),
        check_vma=False,
    )
```

```python
import jax
import jax.numpy as jnp
from jax import lax
from jax.experimental import pallas as pl
from jax.experimental.pallas import tpu as pltpu
from jax.sharding import PartitionSpec as P

FP = 128
BWP = 2
MOVE = 2
STEPS = 2
BORDER = 3 * BWP
SPAN = 3 * FP
HALO = STEPS * (3 * MOVE + 1)
PAD = 16
LANES = 128
FRAME = 32
PLAN = 8
RING = STEPS
ROW_AT = 32
ZONE_AT = 72
SPLIT = -(FP // 4)
SLOT = 24
VMEM_LIMIT = 40 * 1024 * 1024

SMEM_SPEC = pl.BlockSpec(memory_space=pltpu.SMEM)
VMEM_SPEC = pl.BlockSpec(memory_space=pltpu.VMEM)
HBM_SPEC = pl.BlockSpec(memory_space=pltpu.HBM)
ANY_SPEC = pl.BlockSpec(memory_space=pl.ANY)


def params(**more):
    return pltpu.CompilerParams(vmem_limit_bytes=VMEM_LIMIT, **more)


def lane_iota(rows=1, lanes=LANES):
    return lax.broadcasted_iota(jnp.int32, (rows, lanes), 1)


def row_iota(rows, lanes=LANES):
    return lax.broadcasted_iota(jnp.int32, (rows, lanes), 0)


def beside(x, first_lane, last_lane):
    left = [pltpu.roll(v, 1, 1) for v in x]
    right = [pltpu.roll(v, LANES - 1, 1) for v in x]
    return [
        jnp.where(first_lane, left[1 - a], left[a]) + jnp.where(last_lane, right[1 - a], right[a])
        for a in range(2)
    ]


def third(values):
    return (values * 21846) >> 16


def strips_kernel(
    fields, rows, cols, storms, slot_count,
    centres_in, slots_in, lateral_in, vertical_in, parent_in, nests_in,
    send, keep, ring_out, plan, rates, nests,
    plain0, plain1, plain2, turned0, turned1, turned2, block, gather,
    centres, slots, lateral, vertical, parent, arrived,
):
    sources = (
        (centres_in, centres),
        (slots_in, slots),
        (lateral_in, lateral),
        (vertical_in, vertical),
        (parent_in, parent),
        (nests_in, nests),
    )
    copies = [
        pltpu.make_async_copy(source, target, arrived.at[i])
        for i, (source, target) in enumerate(sources)
    ]
    for copy in copies:
        copy.start()
    planes = 2 * fields
    tile_at, tiles = lax.axis_index("tile"), lax.axis_size("tile")
    lev_at, levs = lax.axis_index("lev"), lax.axis_size("lev")
    col_at = lax.axis_index("nest") * levs + lev_at
    col_blocks = lax.axis_size("nest") * levs
    top = 8
    height = rows + 16
    width = cols + 16

    lane = lane_iota()
    first_lane, last_lane = lane == 0, lane == LANES - 1
    row = tile_at * rows + row_iota(height) - top
    tile_cols = (lane, jnp.where(lane < LANES // 2, lane + LANES, lane - LANES))
    within = [
        (
            (row >= 0) & (row < tiles * rows)
            & (col_at * cols + c >= 0) & (col_at * cols + c < col_blocks * cols)
        ).astype(jnp.float32)
        for c in tile_cols
    ]
    plain0[...] = jnp.zeros_like(plain0)
    turned0[...] = jnp.zeros_like(turned0)
    block[...] = jnp.zeros_like(block)
    for copy in copies[:5]:
        copy.wait()
    for f in range(fields):
        rates[f : f + 1, :] = jnp.full((1, LANES), lateral[f], jnp.float32)
        rates[fields + f : fields + f + 1, :] = jnp.full((1, LANES), vertical[f], jnp.float32)
    for j in range(slot_count):
        storm = slots[lax.axis_index("nest") * slot_count + j]
        at = [[centres[n, d, storm] for d in range(2)] for n in range(STEPS + 1)]
        for d in range(2):
            plan[j * PLAN + d] = at[d + 1][0] - FP // 2
            plan[j * PLAN + 2 + d] = 3 * (at[STEPS][d] - at[0][d])
            plan[j * PLAN + 4 + d] = 3 * (at[STEPS][d] - at[STEPS - 1][d])
    for p in range(planes):
        plain0[p, 0, top : top + rows, :] = parent[p // 2, p % 2]
        block[ROW_AT : ROW_AT + rows, :] = parent[p // 2, p % 2]
        turned0[p, top : top + cols, :] = block[...].T

    inner = slice(1, height - 1)

    def plain_step(source, target, mask):
        for f in range(fields):
            lat, ver = lateral[f], vertical[f]
            for v in range(2):
                x = [source[2 * f + v, a, inner, :] for a in range(2)]
                sideways = beside(x, first_lane, last_lane)
                for a in range(2):
                    near = (
                        sideways[a]
                        + source[2 * f + v, a, 2:height, :]
                        + source[2 * f + v, a, 0 : height - 2, :]
                    )
                    other = source[2 * f + 1 - v, a, inner, :]
                    new = x[a] + lat * (near - 4.0 * x[a]) + ver * (other - 2.0 * x[a])
                    if mask is not None:
                        new = new * mask[a][inner, :]
                    target[2 * f + v, a, inner, :] = new
                    for edge in (0, height - 1):
                        target[2 * f + v, a, edge : edge + 1, :] = jnp.zeros(
                            (1, LANES), jnp.float32
                        )

    plain_step(plain0, plain1, within)
    plain_step(plain1, plain2, None)

    row_t = tile_at * rows + lane_iota() - ROW_AT
    col_t = col_at * cols + row_iota(width) - top
    within_t = (
        (row_t >= 0) & (row_t < tiles * rows) & (col_t >= 0) & (col_t < col_blocks * cols)
    ).astype(jnp.float32)

    def turned_step(source, target, mask):
        for f in range(fields):
            lat, ver = lateral[f], vertical[f]
            for v in range(2):
                x = source[2 * f + v, 1 : width - 1, :]
                near = (
                    source[2 * f + v, 2:width, :]
                    + source[2 * f + v, 0 : width - 2, :]
                    + pltpu.roll(x, 1, 1)
                    + pltpu.roll(x, LANES - 1, 1)
                )
                other = source[2 * f + 1 - v, 1 : width - 1, :]
                new = x + lat * (near - 4.0 * x) + ver * (other - 2.0 * x)
                if mask is not None:
                    new = new * mask[1 : width - 1, :]
                target[2 * f + v, 1 : width - 1, :] = new
                target[2 * f + v, 0:1, :] = jnp.zeros((1, LANES), jnp.float32)
                target[2 * f + v, width - 1 : width, :] = jnp.zeros((1, LANES), jnp.float32)

    turned_step(turned0, turned1, within_t)
    turned_step(turned1, turned2, None)

    share = storms * STEPS * planes * BWP
    for j in range(storms):
        storm = slots[j]
        for s in range(STEPS):
            at = (j * STEPS + s) * planes * BWP
            corner_row = centres[s + 1, 0, storm] - FP // 2 - tile_at * rows
            corner_col = centres[s + 1, 1, storm] - FP // 2 - col_at * cols
            plain = (plain1, plain2)[s]
            turned = (turned1, turned2)[s]
            first = jnp.where(corner_row >= SPLIT, corner_row, corner_row + FP - BWP)
            first = jnp.clip(first + top, 0, height - BWP)
            for p in range(planes):
                for a in range(2):
                    gather[a, BWP * p : BWP * (p + 1), :] = plain[p, a, pl.ds(first, BWP), :]
            shift = (64 * LANES - corner_col) % LANES
            window = [pltpu.roll(gather[a], shift, 1) for a in range(2)]
            place = lane + corner_col
            main = (place >= 0) & (place < cols)
            rim = (place >= -RING) & (place < cols + RING)
            window = jnp.where(main, window[0], jnp.where(rim, window[1], 0.0))[: planes * BWP]
            send[at : at + planes * BWP, :] = window
            keep[at : at + planes * BWP, :] = window
            mine = corner_col + (FP - BWP) * lev_at
            theirs = corner_col + (FP - BWP) * (levs - 1 - lev_at)
            for target, start in ((keep, mine), (send, theirs)):
                start = jnp.clip(start + top, 0, width - BWP)
                for p in range(planes):
                    target[share + at + BWP * p : share + at + BWP * (p + 1), :] = turned[
                        p, pl.ds(start, BWP), :
                    ]
    for p in range(planes):
        send[2 * share + BWP * p : 2 * share + BWP * (p + 1), :] = turned2[p, top - RING : top, :]
        at = 2 * share + planes * BWP + BWP * p
        send[at : at + BWP, :] = turned2[p, top + cols : top + cols + RING, :]
        ring_out[p] = turned2[p, top : top + cols, :]
    copies[5].wait()


def pair_up_kernel(own, share, rim, keep, got, kept, *sends):
    nest_at = lax.axis_index("nest")
    lev_at = lax.axis_index("lev")
    for k in range(len(sends) + 1):
        group = lax.bitwise_xor(nest_at, k)
        target = kept if k == 0 else sends[k - 1]
        for part in range(2):
            rows = pl.ds(pl.multiple_of(part * share + group * own, 8), own)
            target[part * own : (part + 1) * own, :] = keep[rows, :] + got[rows, :]
        if k > 0:
            west = got[2 * share : 2 * share + rim, :]
            east = got[2 * share + rim : 2 * share + 2 * rim, :]
            target[2 * own : 2 * own + rim, :] = jnp.where(lev_at == 0, east, west)


def aim_kernel(
    fields, rows, cols, strip_rows, strip_cols, slot_count, moves, share, touching,
    plan, ring, first_got, kept, *refs,
):
    crossing = lax.axis_size("nest") - 1
    nest_gots, rest = refs[:crossing], refs[crossing + 1 :]
    partial, zone_self, zone_sends, total = rest[0], rest[1], rest[2:-1], rest[-1]
    planes = 2 * fields
    rim = planes * BWP
    own = slot_count * STEPS * rim
    tile_at, tiles = lax.axis_index("tile"), lax.axis_size("tile")
    nest_at = lax.axis_index("nest")
    lev_at = lax.axis_index("lev")

    sums = kept[...]
    for got in nest_gots:
        sums = sums + got[0 : 2 * own, :]
    total[...] = sums

    lane = lane_iota()
    col_base = lev_at * (strip_cols // 3 - 3)
    for j in range(slot_count):
        at = j * STEPS * rim
        both = STEPS * rim
        strip = pltpu.roll(total[at : at + both, :], (LANES - col_base) % LANES, 1)
        side = total[own + at : own + at + both, :]
        second = row_iota(both) >= rim
        origins = [plan[j * PLAN + s] - tile_at * rows for s in range(STEPS)]
        for k in moves:
            dest = lax.bitwise_xor(tile_at, k)
            parts = []
            for s in range(STEPS):
                south = origins[s] >= SPLIT
                wanted = ((dest == 0) & south) | ((dest == tiles - 1) & jnp.logical_not(south))
                offset = ROW_AT + origins[s] + (strip_rows // 3) * dest - 3 - ZONE_AT
                source = lane + offset
                fits = (source >= ROW_AT - RING) & (source < ROW_AT + rows + RING)
                turned = pltpu.roll(side, (64 * LANES - offset) % LANES, 1)
                turned = jnp.where(fits, turned, 0.0)
                parts.append(
                    jnp.where(lane < ZONE_AT, strip * wanted.astype(jnp.float32), turned)
                )
            target = zone_self if k == 0 else zone_sends[moves.index(k) - 1]
            target[at : at + both, :] = jnp.where(second, parts[1], parts[0])

    from_west = first_got[2 * share + rim : 2 * share + 2 * rim, :]
    from_east = first_got[2 * share : 2 * share + rim, :]
    far_west = jnp.zeros((rim, LANES), jnp.float32)
    far_east = jnp.zeros((rim, LANES), jnp.float32)
    for i, got in enumerate(nest_gots):
        other = lax.bitwise_xor(nest_at, i + 1)
        edge = got[2 * own : 2 * own + rim, :]
        far_west = far_west + jnp.where(other == nest_at - 1, edge, 0.0)
        far_east = far_east + jnp.where(other == nest_at + 1, edge, 0.0)
    from_west = jnp.where(lev_at == 0, far_west, from_west)
    from_east = jnp.where(lev_at == 0, from_east, far_east)
    for p in range(planes):
        two = slice(BWP * p, BWP * (p + 1))
        total[0:cols, :] = ring[p]
        total[0:RING, :] = total[0:RING, :] + from_west[two]
        total[cols - RING : cols, :] = total[cols - RING : cols, :] + from_east[two]
        total[0:LANES, :] = total[0:cols, :].T
        partial[p // 2, p % 2] = total[ROW_AT : ROW_AT + rows, :]
        below = total[ROW_AT - RING : ROW_AT, :]
        above = total[ROW_AT + rows : ROW_AT + rows + RING, :]
        for i, k in enumerate(moves[1:]):
            if k in touching:
                dest = lax.bitwise_xor(tile_at, k)
                zone_sends[i][own + BWP * p : own + BWP * (p + 1), :] = jnp.where(
                    dest > tile_at, above, below
                )


def edge_cols_kernel(fields, slot_count, nests, after, packed, wide):
    del after
    west_most = lax.axis_index("lev") == 0
    planes = 2 * fields
    half = nests.shape[4] - LANES
    wide[...] = jnp.zeros_like(wide)
    lane = lane_iota()
    for q in range(slot_count * planes):
        j, f, v = q // planes, (q % planes) // 2, q % 2
        spot = (q % 8) * 16
        wide[q % 8, :, 0:half] = nests[j, f, v, :, LANES : LANES + half]
        cells = jnp.where(west_most, wide[q % 8], nests[j, f, v, :, 0:LANES])
        shift = jnp.where(west_most, spot + 2 * LANES - (half - HALO), spot + 2 * LANES) % LANES
        cells = pltpu.roll(cells, shift, 1)
        row = cells if q % 8 == 0 else jnp.where(lane >= spot, cells, row)
        if q % 8 == 7 or q == slot_count * planes - 1:
            packed[q // 8] = row


def edge_rows_kernel(fields, strip_rows, slot_count, nests, packed, after, to_pair, to_cross):
    del after
    even = lax.rem(lax.axis_index("tile"), 2) == 0
    half = nests.shape[4] - LANES
    lows, highs, tail = slice(0, HALO), slice(strip_rows - HALO, strip_rows), slice(LANES, LANES + half)

    def put(at, low, high):
        to_pair[at : at + HALO, :] = jnp.where(even, high, low)
        to_cross[at : at + HALO, :] = jnp.where(even, low, high)

    for j in range(slot_count):
        for f in range(fields):
            at = (3 * fields * j + 2 * f) * HALO
            for v in range(2):
                put(at + v * HALO, nests[j, f, v, lows, 0:LANES], nests[j, f, v, highs, 0:LANES])
            at = (3 * fields * j + 2 * fields + f) * HALO
            put(
                at,
                jnp.concatenate([nests[j, f, v, lows, tail] for v in range(2)], 1),
                jnp.concatenate([nests[j, f, v, highs, tail] for v in range(2)], 1),
            )
    for g in range(packed.shape[0]):
        at = (3 * fields * slot_count + g) * HALO
        put(at, packed[g, lows, :], packed[g, highs, :])


def shift_kernel(fields, strip_rows, strip_cols, slot_count, plan, nests, packed, moved, cells):
    planes = 2 * fields
    half = strip_cols - LANES
    room = PAD + 8
    height = strip_rows + 16
    lane = lane_iota()
    goal = jnp.where(lax.axis_index("lev") == 0, half, LANES - HALO)
    in_goal = (lane >= goal) & (lane < goal + HALO)
    cells[...] = jnp.zeros_like(cells)

    def one(j, _):
        down, right = plan[j * PLAN + 2], plan[j * PLAN + 3]
        shift = (LANES - right) % LANES
        same = (lane + right >= 0) & (lane + right < LANES)
        start = room - 8 + down
        for f in range(fields):
            for v in range(2):
                cells[f, v, 0, room : room + strip_rows, :] = nests[j, f, v, :, 0:LANES]
                cells[f, v, 1, room : room + strip_rows, 0:half] = nests[j, f, v, :, LANES : LANES + half]
                n = j * planes + 2 * f + v
                goal_shift = (goal - lax.rem(n, 8) * 16 + 2 * LANES) % LANES
                got = jnp.where(in_goal, pltpu.roll(packed[lax.div(n, 8)], goal_shift, 1), 0.0)
                cells[f, v, 1, room : room + strip_rows, half:LANES] = got[:, half:LANES]
        for f in range(fields):
            for v in range(2):
                both = [
                    pltpu.roll(cells[f, v, a, pl.ds(start, height), :], shift, 1) for a in range(2)
                ]
                for a in range(2):
                    moved[j, f, v, a] = jnp.where(same, both[a], both[1 - a])
        return 0

    lax.fori_loop(0, slot_count, one, 0)


def advance_kernel(
    fields, strip_rows, strip_cols, slot_count,
    plan, rates, moved, pair, cross,
    inner_out, side_out, row_out, first, second,
):
    planes = 2 * fields
    half = strip_cols - LANES
    height = strip_rows + 16
    tile_at = lax.axis_index("tile")
    lev_at = lax.axis_index("lev")
    even = lax.rem(tile_at, 2) == 0
    lane = lane_iota()
    first_lane, last_lane = lane == 0, lane == LANES - 1
    chunk = 16 if height % 16 == 0 and strip_rows % 16 == 0 else 8
    row_start = pl.multiple_of(jnp.where(tile_at == 0, 0, strip_rows - 16), 8)
    outer = (tile_at == 0) | (tile_at == lax.axis_size("tile") - 1)
    goal = jnp.where(lev_at == 0, half, LANES - HALO)
    in_goal = (lane >= goal) & (lane < goal + HALO)

    lats = [rates[f : f + 1, :] for f in range(fields)]
    vers = [rates[fields + f : fields + f + 1, :] for f in range(fields)]
    stays = [1.0 - 4.0 * lats[f] - 2.0 * vers[f] for f in range(fields)]

    def stencil(f, source, at, size):
        x = [[source[f, v, a, at : at + size, :] for a in range(2)] for v in range(2)]
        new = [[None] * 2, [None] * 2]
        for v in range(2):
            sideways = beside(x[v], first_lane, last_lane)
            for a in range(2):
                near = (
                    sideways[a]
                    + source[f, v, a, at - 1 : at + size - 1, :]
                    + source[f, v, a, at + 1 : at + size + 1, :]
                )
                new[v][a] = stays[f] * x[v][a] + lats[f] * near + vers[f] * x[1 - v][a]
        return new

    def one(j, _):
        down, right = plan[j * PLAN + 2], plan[j * PLAN + 3]
        shift = (LANES - right) % LANES
        same = (lane + right >= 0) & (lane + right < LANES)
        for f in range(fields):
            for v in range(2):
                n = j * planes + 2 * f + v
                goal_shift = (goal - lax.rem(n, 8) * 16 + 2 * LANES) % LANES
                ends = []
                for got in (pair, cross):
                    main = got[pl.ds((3 * fields * j + 2 * f + v) * HALO, HALO), :]
                    tail = got[pl.ds((3 * fields * j + planes + f) * HALO, HALO), :]
                    if v == 1:
                        tail = pltpu.roll(tail, LANES - half, 1)
                    corner = got[pl.ds((3 * fields * slot_count + lax.div(n, 8)) * HALO, HALO), :]
                    corner = jnp.where(in_goal, pltpu.roll(corner, goal_shift, 1), 0.0)
                    tail = jnp.where(lane < half, tail, corner)
                    turned = [pltpu.roll(main, shift, 1), pltpu.roll(tail, shift, 1)]
                    ends.append([jnp.where(same, turned[a], turned[1 - a]) for a in range(2)])
                for a in range(2):
                    first[f, v, a, FRAME - 8 : FRAME - 8 + height, :] = moved[j, f, v, a]
                    low = jnp.where(even, ends[1][a], ends[0][a])
                    high = jnp.where(even, ends[0][a], ends[1][a])
                    first[f, v, a, pl.ds(FRAME - HALO - down, HALO), :] = low
                    first[f, v, a, pl.ds(FRAME + strip_rows - down, HALO), :] = high

        for west in (True, False):

            @pl.when(lev_at == 0 if west else lev_at > 0)
            def _(west=west):
                turn = 8 if west else LANES + 16 - half
                for v in range(2):
                    side = None
                    for f in range(fields):
                        near = first[f, v, 1, FRAME - 8 : FRAME - 8 + height, :]
                        if west:
                            low = first[f, v, 0, FRAME - 8 : FRAME - 8 + height, :]
                            near = jnp.where(lane < LANES // 2, low, near)
                        near = pltpu.roll(near, (turn + f * SLOT) % LANES, 1)
                        side = near if f == 0 else jnp.where(lane >= f * SLOT, near, side)
                    side_out[v, j] = side

        @pl.when(outer)
        def _():
            for f in range(fields):
                for v in range(2):
                    for a in range(2):
                        row_out[j, f, v, a] = first[f, v, a, pl.ds(FRAME - 8 + row_start, 32), :]

        for f in range(fields):
            for c in range(0, height, chunk):
                new = stencil(f, first, FRAME - 8 + c, chunk)
                for v in range(2):
                    for a in range(2):
                        second[f, v, a, 8 + c : 8 + c + chunk, :] = new[v][a]
        for f in range(fields):
            for c in range(0, strip_rows, chunk):
                new = stencil(f, second, 16 + c, chunk)
                for v in range(2):
                    inner_out[j, f, v, c : c + chunk, 0:LANES] = new[v][0]
                    inner_out[j, f, v, c : c + chunk, LANES : LANES + half] = new[v][1][:, :half]
        return 0

    lax.fori_loop(0, slot_count, one, 0)


def gaps(i):
    return jnp.minimum(i, SPAN - 1 - i)


def settle_kernel(
    fields, strip_rows, strip_cols, rows, slot_count, moves, touching,
    plan, rates, inner, side_in, row_in, partial, zone_self, *refs,
):
    count = len(moves) - 1
    zone_gots = refs[:count]
    nest_out, parent_out = refs[count : count + 2]
    zone, turned, sides, strips, side_new, mixed, rows_mixed, rows_new, whole, done = refs[count + 2 :]
    planes = 2 * fields
    rim = planes * BWP
    both = STEPS * rim
    own = slot_count * both
    half = strip_cols - LANES
    height = strip_rows + 16
    tile_at, tiles = lax.axis_index("tile"), lax.axis_size("tile")
    nest_at = lax.axis_index("nest")
    lev_at = lax.axis_index("lev")
    lane = lane_iota()
    first_lane, last_lane = lane == 0, lane == LANES - 1

    below = jnp.zeros((rim, LANES), jnp.float32)
    above = jnp.zeros((rim, LANES), jnp.float32)
    for i, k in enumerate(moves[1:]):
        if k in touching:
            other = lax.bitwise_xor(tile_at, k)
            edge = zone_gots[i][own : own + rim, :]
            below = below + jnp.where(other == tile_at - 1, edge, 0.0)
            above = above + jnp.where(other == tile_at + 1, edge, 0.0)
    for p in range(planes):
        f, v = p // 2, p % 2
        two = slice(BWP * p, BWP * (p + 1))
        parent_out[f, v] = partial[f, v]
        parent_out[f, v, 0:RING, :] = partial[f, v, 0:RING, :] + below[two]
        parent_out[f, v, rows - RING : rows, :] = partial[f, v, rows - RING : rows, :] + above[two]

    whole_move = [[plan[j * PLAN + 2 + d] for d in range(2)] for j in range(slot_count)]
    last_move = [[plan[j * PLAN + 4 + d] for d in range(2)] for j in range(slot_count)]
    offsets = [[(0, 0) if s == 1 else last_move[j] for s in range(STEPS)] for j in range(slot_count)]
    earlier = [[whole_move[j], last_move[j]] for j in range(slot_count)]

    total = zone_self[0:own, :]
    for got in zone_gots:
        total = total + got[0:own, :]
    zone[...] = jnp.zeros_like(zone)
    zone[0:own, :] = total
    second = row_iota(both) >= rim
    col_base = lev_at * (strip_cols // 3 - 3)
    col_from = lev_at * strip_cols
    gap = (half + LANES) // 2
    owner = jnp.zeros((1, LANES), jnp.int32)
    for f in range(1, fields):
        owner = owner + (lane >= f * SLOT).astype(jnp.int32)
    side_cols = lane - SLOT * owner + jnp.where(lev_at == 0, -8, 2 * strip_cols - 16)
    lane_cols = (
        lane + col_from,
        jnp.where(lane < gap, lane + LANES, lane - LANES) + col_from,
        side_cols,
    )
    for j in range(slot_count):
        block = zone[j * both : (j + 1) * both, :]
        for a in range(3):
            picks = [
                jnp.clip(third(jnp.clip(lane_cols[a] + offsets[j][s][1], 0, SPAN - 1)) - col_base, 0, ZONE_AT - 1)
                for s in range(STEPS)
            ]
            strips[j, a] = jnp.take_along_axis(block, jnp.where(second, picks[1], picks[0]), axis=1)
        picks = [
            jnp.clip(
                third(jnp.clip(lane + (tile_at * strip_rows - 8) + offsets[j][s][0], 0, SPAN - 1))
                - ((strip_rows // 3) * tile_at - 3)
                + ZONE_AT,
                ZONE_AT,
                LANES - 1,
            )
            for s in range(STEPS)
        ]
        turned[j * both : (j + 1) * both, :] = jnp.take_along_axis(
            block, jnp.where(second, picks[1], picks[0]), axis=1
        )
    sides[...] = turned[...].T

    chunk = 16 if height % 16 == 0 else 8
    lats = [rates[f : f + 1, :] for f in range(fields)]
    vers = [rates[fields + f : fields + f + 1, :] for f in range(fields)]
    lat, ver = lats[0], vers[0]
    for f in range(1, fields):
        lat = jnp.where(owner >= f, lats[f], lat)
        ver = jnp.where(owner >= f, vers[f], ver)
    stay = 4.0 * lat + 2.0 * ver
    for s in range(STEPS):
        insides = {}
        for j in range(slot_count):
            by_row, by_col = offsets[j][s]
            was_row, was_col = earlier[j][s]
            col = side_cols + by_col
            col_gap = gaps(col)
            col_kept = gaps(side_cols + was_col)
            depth = jnp.where((col < 3) | ((col >= SPAN // 2) & (col < SPAN - 3)), 0, 1)
            lines, picks = [], []
            for v in range(2):
                picks.append(jnp.minimum(j * both + s * rim + v * BWP + 2 * BWP * owner + depth, own - 1))
                pair_of = []
                for r in range(BWP):
                    n = s * rim + v * BWP + r
                    line = strips[j, 2, n : n + 1, :]
                    for f in range(1, fields):
                        m = n + 2 * BWP * f
                        line = jnp.where(owner >= f, strips[j, 2, m : m + 1, :], line)
                    pair_of.append(line)
                lines.append(pair_of)
            for c in range(0, height, chunk):
                base = row_iota(chunk) + (tile_at * strip_rows - 8 + c)
                i = base + by_row
                distance = jnp.minimum(gaps(i), col_gap)
                kept = jnp.minimum(gaps(base + was_row), col_kept)
                w = jnp.clip(BORDER - distance, 0, BORDER).astype(jnp.float32) * (1.0 / BORDER)
                w = jnp.where(kept >= 0, w, 1.0)
                in_rows = (i < BORDER) | (i >= SPAN - BORDER)
                early = (i < 3) | ((i >= SPAN // 2) & (i < SPAN - 3))
                insides[j, c] = (distance >= 1).astype(jnp.float32)
                for v in range(2):
                    pick = jnp.broadcast_to(picks[v], (chunk, LANES))
                    side = jnp.take_along_axis(sides[c : c + chunk, :], pick, axis=1)
                    strip = jnp.where(early, lines[v][0], lines[v][1])
                    driving = jnp.where(in_rows, strip, side)
                    x = side_in[v, j, c : c + chunk, :] if s == 0 else side_new[v, j, c : c + chunk, :]
                    mixed[v, j, 8 + c : 8 + c + chunk, :] = (1.0 - w) * x + w * driving
        for j in range(slot_count):
            for c in range(0, height, chunk):
                x = [mixed[v, j, 8 + c : 8 + c + chunk, :] for v in range(2)]
                for v in range(2):
                    near = (
                        pltpu.roll(x[v], 1, 1)
                        + pltpu.roll(x[v], LANES - 1, 1)
                        + mixed[v, j, 7 + c : 7 + c + chunk, :]
                        + mixed[v, j, 9 + c : 9 + c + chunk, :]
                    )
                    change = lat * near + ver * x[1 - v] - stay * x[v]
                    side_new[v, j, c : c + chunk, :] = x[v] + insides[j, c] * change

    outer = (tile_at == 0) | (tile_at == tiles - 1)
    window = jnp.where(tile_at == 0, -8, tile_at * strip_rows + strip_rows - 24)
    row_start = pl.multiple_of(jnp.where(tile_at == 0, 0, strip_rows - 16), 8)
    line = row_iota(16)
    line_from = jnp.where(tile_at == 0, 0, 16 - HALO)
    lows = (0, jnp.where(lev_at > 0, half - HALO, LANES))
    highs = (jnp.where(lev_at == 0, HALO, 0), half)
    across = lane_iota(16)
    near_row = [
        (line >= line_from)
        & (line < line_from + HALO)
        & ((across < lows[a]) | (across >= highs[a]))
        for a in range(2)
    ]

    def one(j, _):
        for west in (True, False):

            @pl.when(lev_at == 0 if west else lev_at > 0)
            def _(west=west):
                for f in range(fields):
                    back = (2 * LANES + (-8 if west else half - 16) - f * SLOT) % LANES
                    for v in range(2):
                        near = pltpu.roll(side_new[v, j, 8 : 8 + strip_rows, :], back, 1)
                        first = inner[j, f, v, :, 0:LANES]
                        second = inner[j, f, v, :, LANES : LANES + half]
                        if west:
                            first = jnp.where(lane < HALO, near, first)
                        else:
                            second = jnp.where(lane[:, :half] >= half - HALO, near[:, :half], second)
                        whole[j, f, v, :, 0:LANES] = first
                        whole[j, f, v, :, LANES : LANES + half] = second

        @pl.when(outer)
        def _():
            full, last = plan[j * PLAN + 2], plan[j * PLAN + 4]
            base = row_iota(32) + window
            for s in range(STEPS):
                i = base + (last if s == 0 else 0)
                kept = gaps(base + (full if s == 0 else last)) >= 0
                w = jnp.clip(BORDER - gaps(i), 0, BORDER).astype(jnp.float32) * (1.0 / BORDER)
                w = jnp.where(kept, w, 1.0)
                rest = 1.0 - w
                inside = (gaps(i) >= 1).astype(jnp.float32)
                early = (i < 3) | ((i >= SPAN // 2) & (i < SPAN - 3))
                for f in range(fields):
                    for v in range(2):
                        n = s * rim + (2 * f + v) * BWP
                        for a in range(2):
                            driving = jnp.where(
                                early, strips[j, a, n : n + 1, :], strips[j, a, n + 1 : n + 2, :]
                            )
                            x = row_in[j, f, v, a] if s == 0 else rows_new[f, v, a]
                            rows_mixed[f, v, a, 8:40, :] = rest * x + w * driving
                for f in range(fields):
                    stay = 4.0 * lats[f] + 2.0 * vers[f]
                    value = [[rows_mixed[f, v, a, 8:40, :] for a in range(2)] for v in range(2)]
                    for v in range(2):
                        sideways = beside(value[v], first_lane, last_lane)
                        for a in range(2):
                            near = (
                                sideways[a]
                                + rows_mixed[f, v, a, 7:39, :]
                                + rows_mixed[f, v, a, 9:41, :]
                            )
                            change = (
                                lats[f] * near + vers[f] * value[1 - v][a] - stay * value[v][a]
                            )
                            rows_new[f, v, a] = value[v][a] + inside * change
            for f in range(fields):
                for v in range(2):
                    target = pl.ds(row_start, 16)
                    whole[j, f, v, target, 0:LANES] = jnp.where(
                        near_row[0], rows_new[f, v, 0, 8:24, :], whole[j, f, v, target, 0:LANES]
                    )
                    whole[j, f, v, target, LANES : LANES + half] = jnp.where(
                        near_row[1][:, :half],
                        rows_new[f, v, 1, 8:24, 0:half],
                        whole[j, f, v, target, LANES : LANES + half],
                    )

        pltpu.make_async_copy(whole.at[j], nest_out.at[j], done.at[j]).start()
        return 0

    lax.fori_loop(0, slot_count, one, 0)

    def wait(j, _):
        pltpu.make_async_copy(whole.at[j], nest_out.at[j], done.at[j]).wait()
        return 0

    lax.fori_loop(0, slot_count, wait, 0)


def per_device(parent_field, nest_fields, lateral_rate, vertical_rate, centres, slot_storm):
    fields, _, rows, cols = parent_field.shape
    slot_count, _, _, strip_rows, strip_cols = nest_fields.shape
    storms = slot_storm.shape[0]
    tiles, groups, levs = lax.axis_size("tile"), lax.axis_size("nest"), lax.axis_size("lev")
    planes = 2 * fields
    rim = planes * BWP
    share = storms * STEPS * rim
    own = slot_count * STEPS * rim
    height = strip_rows + 2 * PAD
    half = strip_cols - LANES
    f32 = jnp.float32

    def shaped(*dims):
        return jax.ShapeDtypeStruct(dims, f32)

    pair_list = [(t, t ^ 1) for t in range(tiles) if t ^ 1 < tiles]
    cross_list = [(t, t - 1 if t % 2 == 0 else t + 1) for t in range(1, tiles - 1)]
    centres = jnp.swapaxes(centres, 1, 2)

    send, keep, ring, plan, rates, nests = pl.pallas_call(
        lambda *refs: strips_kernel(fields, rows, cols, storms, slot_count, *refs),
        in_specs=[HBM_SPEC] * 6,
        out_specs=[VMEM_SPEC] * 3 + [SMEM_SPEC] + [VMEM_SPEC] * 2,
        out_shape=[
            shaped(2 * share + 2 * rim, LANES),
            shaped(2 * share, LANES),
            shaped(planes, cols, LANES),
            jax.ShapeDtypeStruct((slot_count * PLAN,), jnp.int32),
            shaped(2 * fields, LANES),
            shaped(*nest_fields.shape),
        ],
        scratch_shapes=[pltpu.VMEM((planes, 2, rows + 16, LANES), f32)] * 3
        + [pltpu.VMEM((planes, cols + 16, LANES), f32)] * 3
        + [
            pltpu.VMEM((LANES, LANES), f32),
            pltpu.VMEM((2, 24, LANES), f32),
            pltpu.SMEM(centres.shape, jnp.int32),
            pltpu.SMEM(slot_storm.shape, jnp.int32),
            pltpu.SMEM(lateral_rate.shape, f32),
            pltpu.SMEM(vertical_rate.shape, f32),
            pltpu.VMEM(parent_field.shape, f32),
            pltpu.SemaphoreType.DMA((6,)),
        ],
        compiler_params=params(),
        name="strips",
    )(
        *(
            pltpu.with_memory_space_constraint(x, pltpu.HBM)
            for x in (centres, slot_storm, lateral_rate, vertical_rate, parent_field, nest_fields)
        )
    )
    got = lax.ppermute(send, "lev", [(l, l ^ 1) for l in range(levs)])

    bundles = -(-slot_count * planes // 8)
    packed = pl.pallas_call(
        lambda *refs: edge_cols_kernel(fields, slot_count, *refs),
        in_specs=[VMEM_SPEC, ANY_SPEC],
        out_specs=VMEM_SPEC,
        out_shape=shaped(bundles, strip_rows, LANES),
        scratch_shapes=[pltpu.VMEM((8, strip_rows, LANES), f32)],
        compiler_params=params(),
        name="edge_cols",
    )(nests, keep)
    packed = lax.ppermute(packed, "lev", [(l, l ^ 1) for l in range(levs)])

    kept, *sends = pl.pallas_call(
        lambda *refs: pair_up_kernel(own, share, rim, *refs),
        in_specs=[VMEM_SPEC] * 2,
        out_specs=[VMEM_SPEC] * groups,
        out_shape=[shaped(2 * own, LANES)] + [shaped(2 * own + rim, LANES)] * (groups - 1),
        compiler_params=params(),
        name="pair_up",
    )(keep, got)
    nest_gots = [
        lax.ppermute(x, "nest", [(n, n ^ (i + 1)) for n in range(groups)])
        for i, x in enumerate(sends)
    ]

    edge_lines = (3 * fields * slot_count + bundles) * HALO
    to_pair, to_cross = pl.pallas_call(
        lambda *refs: edge_rows_kernel(fields, strip_rows, slot_count, *refs),
        in_specs=[VMEM_SPEC] * 2 + [ANY_SPEC],
        out_specs=[VMEM_SPEC] * 2,
        out_shape=[shaped(edge_lines, LANES)] * 2,
        compiler_params=params(),
        name="edge_rows",
    )(nests, packed, kept)
    pair = lax.ppermute(to_pair, "tile", pair_list)
    cross = lax.ppermute(to_cross, "tile", cross_list)

    moved = pl.pallas_call(
        lambda *refs: shift_kernel(fields, strip_rows, strip_cols, slot_count, *refs),
        in_specs=[SMEM_SPEC] + [VMEM_SPEC] * 2,
        out_specs=VMEM_SPEC,
        out_shape=shaped(slot_count, fields, 2, 2, strip_rows + 16, LANES),
        scratch_shapes=[pltpu.VMEM((fields, 2, 2, strip_rows + 48, LANES), f32)],
        compiler_params=params(),
        cost_estimate=pl.CostEstimate(flops=3_000_000_000, bytes_accessed=10_000_000, transcendentals=0),
        name="shift",
    )(plan, nests, packed)

    def holds(source, dest):
        low = max((strip_rows // 3) * dest - 3, 0)
        high = tiles * rows - FP + min((strip_rows // 3) * (dest + 1) + 3, FP)
        return rows * source - RING < high and rows * (source + 1) + RING > low

    routes = {}
    for k in range(1, tiles):
        pairs = [
            (t, t ^ k)
            for t in range(tiles)
            if t ^ k < tiles and (holds(t, t ^ k) or holds(t ^ k, t) or abs(t - (t ^ k)) == 1)
        ]
        if pairs:
            routes[k] = pairs
    touching = tuple(k for k in routes if any(abs(a - b) == 1 for a, b in routes[k]))
    moves = (0, *routes)
    zone_shapes = [
        shaped(own + (rim if k in touching else rim + 8 if k > 0 else 0), LANES) for k in moves
    ]
    partial, zone_self, *zone_sends = pl.pallas_call(
        lambda *refs: aim_kernel(
            fields, rows, cols, strip_rows, strip_cols, slot_count, moves, share, touching, *refs
        ),
        in_specs=[SMEM_SPEC] + [VMEM_SPEC] * (2 + groups) + [ANY_SPEC],
        out_specs=[VMEM_SPEC] * (1 + len(moves)),
        out_shape=[shaped(fields, 2, rows, cols), *zone_shapes],
        scratch_shapes=[pltpu.VMEM((2 * own, LANES), f32)],
        compiler_params=params(),
        name="aim",
    )(plan, ring, got, kept, *nest_gots, moved)
    zone_gots = [lax.ppermute(x, "tile", routes[k]) for k, x in zip(moves[1:], zone_sends)]

    inner, side_in, row_in = pl.pallas_call(
        lambda *refs: advance_kernel(fields, strip_rows, strip_cols, slot_count, *refs),
        in_specs=[SMEM_SPEC] + [VMEM_SPEC] * 4,
        out_specs=[VMEM_SPEC] * 3,
        out_shape=[
            shaped(*nest_fields.shape),
            shaped(2, slot_count, strip_rows + 16, LANES),
            shaped(slot_count, fields, 2, 2, 32, LANES),
        ],
        scratch_shapes=[
            pltpu.VMEM((fields, 2, 2, strip_rows + 2 * FRAME, LANES), f32),
            pltpu.VMEM((fields, 2, 2, strip_rows + 32, LANES), f32),
        ],
        compiler_params=params(),
        name="advance",
    )(plan, rates, moved, pair, cross)

    nest_final, parent_final = pl.pallas_call(
        lambda *refs: settle_kernel(
            fields, strip_rows, strip_cols, rows, slot_count, moves, touching, *refs
        ),
        in_specs=[SMEM_SPEC] + [VMEM_SPEC] * (5 + len(moves)),
        out_specs=[ANY_SPEC, VMEM_SPEC],
        out_shape=[shaped(*nest_fields.shape), shaped(*parent_field.shape)],
        scratch_shapes=[
            pltpu.VMEM((LANES, LANES), f32),
            pltpu.VMEM((LANES, LANES), f32),
            pltpu.VMEM((LANES, LANES), f32),
            pltpu.VMEM((slot_count, 3, STEPS * rim, LANES), f32),
            pltpu.VMEM((2, slot_count, strip_rows + 16, LANES), f32),
            pltpu.VMEM((2, slot_count, strip_rows + 32, LANES), f32),
            pltpu.VMEM((fields, 2, 2, 48, LANES), f32),
            pltpu.VMEM((fields, 2, 2, 32, LANES), f32),
            pltpu.VMEM((slot_count, fields, 2, strip_rows, strip_cols), f32),
            pltpu.SemaphoreType.DMA((slot_count,)),
        ],
        compiler_params=params(),
        name="settle",
    )(
        plan, rates, inner, side_in, row_in, partial, zone_self, *zone_gots,
    )
    return (parent_final, nest_final)


def solution(mesh):
    placed = (
        P("member", None, "tile", ("nest", "lev")),
        P(("member", "nest"), None, None, "tile", "lev"),
        P(),
        P(),
        P("member", None, None),
        P("member"),
    )
    return jax.shard_map(
        per_device,
        mesh=mesh,
        in_specs=placed,
        out_specs=(
            P("member", None, "tile", ("nest", "lev")),
            P(("member", "nest"), None, None, "tile", "lev"),
        ),
        check_vma=False,
    )
```

```python
import jax
import jax.numpy as jnp
from jax import lax
from jax.experimental import pallas as pl
from jax.experimental.pallas import tpu as pltpu
from jax.sharding import PartitionSpec as P

FP = 128
BWP = 2
MOVE = 2
STEPS = 2
BORDER = 3 * BWP
SPAN = 3 * FP
HALO = STEPS * (3 * MOVE + 1)
PAD = 16
LANES = 128
SLIM = 40
FRAME = 32
PLAN = 8
RING = STEPS
ROW_AT = 32
ZONE_AT = 72
SPLIT = -(FP // 4)
SLOT = 24
VMEM_LIMIT = 40 * 1024 * 1024

SMEM_SPEC = pl.BlockSpec(memory_space=pltpu.SMEM)
VMEM_SPEC = pl.BlockSpec(memory_space=pltpu.VMEM)
HBM_SPEC = pl.BlockSpec(memory_space=pltpu.HBM)
ANY_SPEC = pl.BlockSpec(memory_space=pl.ANY)


def params(**more):
    return pltpu.CompilerParams(vmem_limit_bytes=VMEM_LIMIT, **more)


def lane_iota(rows=1, lanes=LANES):
    return lax.broadcasted_iota(jnp.int32, (rows, lanes), 1)


def row_iota(rows, lanes=LANES):
    return lax.broadcasted_iota(jnp.int32, (rows, lanes), 0)


def beside(x, first_lane, last_lane):
    left = [pltpu.roll(v, 1, 1) for v in x]
    right = [pltpu.roll(v, LANES - 1, 1) for v in x]
    return [
        jnp.where(first_lane, left[1 - a], left[a]) + jnp.where(last_lane, right[1 - a], right[a])
        for a in range(2)
    ]


def third(values):
    return (values * 21846) >> 16


def strips_kernel(
    fields, rows, cols, storms, slot_count,
    centres_in, slots_in, lateral_in, vertical_in, parent_in, nests_in,
    send, keep, ring_out, plan, rates, nests,
    plain0, plain1, plain2, turned0, turned1, turned2, block, gather,
    centres, slots, lateral, vertical, parent, arrived,
):
    sources = (
        (centres_in, centres),
        (slots_in, slots),
        (lateral_in, lateral),
        (vertical_in, vertical),
        (parent_in, parent),
        (nests_in, nests),
    )
    copies = [
        pltpu.make_async_copy(source, target, arrived.at[i])
        for i, (source, target) in enumerate(sources)
    ]
    for copy in copies:
        copy.start()
    planes = 2 * fields
    tile_at, tiles = lax.axis_index("tile"), lax.axis_size("tile")
    lev_at, levs = lax.axis_index("lev"), lax.axis_size("lev")
    col_at = lax.axis_index("nest") * levs + lev_at
    col_blocks = lax.axis_size("nest") * levs
    top = 8
    height = rows + 16
    width = cols + 16

    lane = lane_iota()
    first_lane, last_lane = lane == 0, lane == LANES - 1
    row = tile_at * rows + row_iota(height) - top
    tile_cols = (lane, jnp.where(lane < LANES // 2, lane + LANES, lane - LANES))
    within = [
        (
            (row >= 0) & (row < tiles * rows)
            & (col_at * cols + c >= 0) & (col_at * cols + c < col_blocks * cols)
        ).astype(jnp.float32)
        for c in tile_cols
    ]
    plain0[...] = jnp.zeros_like(plain0)
    turned0[...] = jnp.zeros_like(turned0)
    block[...] = jnp.zeros_like(block)
    for copy in copies[:5]:
        copy.wait()
    for f in range(fields):
        rates[f : f + 1, :] = jnp.full((1, LANES), lateral[f], jnp.float32)
        rates[fields + f : fields + f + 1, :] = jnp.full((1, LANES), vertical[f], jnp.float32)
    for j in range(slot_count):
        storm = slots[lax.axis_index("nest") * slot_count + j]
        at = [[centres[n, d, storm] for d in range(2)] for n in range(STEPS + 1)]
        for d in range(2):
            plan[j * PLAN + d] = at[d + 1][0] - FP // 2
            plan[j * PLAN + 2 + d] = 3 * (at[STEPS][d] - at[0][d])
            plan[j * PLAN + 4 + d] = 3 * (at[STEPS][d] - at[STEPS - 1][d])
    for p in range(planes):
        plain0[p, 0, top : top + rows, :] = parent[p // 2, p % 2]
        block[ROW_AT : ROW_AT + rows, :] = parent[p // 2, p % 2]
        turned0[p, top : top + cols, :] = block[...].T

    inner = slice(1, height - 1)

    def plain_step(source, target, mask):
        for f in range(fields):
            lat, ver = lateral[f], vertical[f]
            for v in range(2):
                x = [source[2 * f + v, a, inner, :] for a in range(2)]
                sideways = beside(x, first_lane, last_lane)
                for a in range(2):
                    near = (
                        sideways[a]
                        + source[2 * f + v, a, 2:height, :]
                        + source[2 * f + v, a, 0 : height - 2, :]
                    )
                    other = source[2 * f + 1 - v, a, inner, :]
                    new = x[a] + lat * (near - 4.0 * x[a]) + ver * (other - 2.0 * x[a])
                    if mask is not None:
                        new = new * mask[a][inner, :]
                    target[2 * f + v, a, inner, :] = new
                    for edge in (0, height - 1):
                        target[2 * f + v, a, edge : edge + 1, :] = jnp.zeros(
                            (1, LANES), jnp.float32
                        )

    plain_step(plain0, plain1, within)
    plain_step(plain1, plain2, None)

    row_t = tile_at * rows + lane_iota() - ROW_AT
    col_t = col_at * cols + row_iota(width) - top
    within_t = (
        (row_t >= 0) & (row_t < tiles * rows) & (col_t >= 0) & (col_t < col_blocks * cols)
    ).astype(jnp.float32)

    def turned_step(source, target, mask):
        for f in range(fields):
            lat, ver = lateral[f], vertical[f]
            for v in range(2):
                x = source[2 * f + v, 1 : width - 1, :]
                near = (
                    source[2 * f + v, 2:width, :]
                    + source[2 * f + v, 0 : width - 2, :]
                    + pltpu.roll(x, 1, 1)
                    + pltpu.roll(x, LANES - 1, 1)
                )
                other = source[2 * f + 1 - v, 1 : width - 1, :]
                new = x + lat * (near - 4.0 * x) + ver * (other - 2.0 * x)
                if mask is not None:
                    new = new * mask[1 : width - 1, :]
                target[2 * f + v, 1 : width - 1, :] = new
                target[2 * f + v, 0:1, :] = jnp.zeros((1, LANES), jnp.float32)
                target[2 * f + v, width - 1 : width, :] = jnp.zeros((1, LANES), jnp.float32)

    turned_step(turned0, turned1, within_t)
    turned_step(turned1, turned2, None)

    share = storms * STEPS * planes * BWP
    for j in range(storms):
        storm = slots[j]
        for s in range(STEPS):
            at = (j * STEPS + s) * planes * BWP
            corner_row = centres[s + 1, 0, storm] - FP // 2 - tile_at * rows
            corner_col = centres[s + 1, 1, storm] - FP // 2 - col_at * cols
            plain = (plain1, plain2)[s]
            turned = (turned1, turned2)[s]
            first = jnp.where(corner_row >= SPLIT, corner_row, corner_row + FP - BWP)
            first = jnp.clip(first + top, 0, height - BWP)
            for p in range(planes):
                for a in range(2):
                    gather[a, BWP * p : BWP * (p + 1), :] = plain[p, a, pl.ds(first, BWP), :]
            shift = (64 * LANES - corner_col) % LANES
            window = [pltpu.roll(gather[a], shift, 1) for a in range(2)]
            place = lane + corner_col
            main = (place >= 0) & (place < cols)
            rim = (place >= -RING) & (place < cols + RING)
            window = jnp.where(main, window[0], jnp.where(rim, window[1], 0.0))[: planes * BWP]
            send[at : at + planes * BWP, :] = window
            keep[at : at + planes * BWP, :] = window
            mine = corner_col + (FP - BWP) * lev_at
            theirs = corner_col + (FP - BWP) * (levs - 1 - lev_at)
            for target, start in ((keep, mine), (send, theirs)):
                start = jnp.clip(start + top, 0, width - BWP)
                for p in range(planes):
                    target[share + at + BWP * p : share + at + BWP * (p + 1), :] = turned[
                        p, pl.ds(start, BWP), :
                    ]
    for p in range(planes):
        send[2 * share + BWP * p : 2 * share + BWP * (p + 1), :] = turned2[p, top - RING : top, :]
        at = 2 * share + planes * BWP + BWP * p
        send[at : at + BWP, :] = turned2[p, top + cols : top + cols + RING, :]
        ring_out[p] = turned2[p, top : top + cols, :]
    copies[5].wait()


def pair_up_kernel(own, share, rim, keep, got, kept, *sends):
    nest_at = lax.axis_index("nest")
    lev_at = lax.axis_index("lev")
    for k in range(len(sends) + 1):
        group = lax.bitwise_xor(nest_at, k)
        target = kept if k == 0 else sends[k - 1]
        for part in range(2):
            rows = pl.ds(pl.multiple_of(part * share + group * own, 8), own)
            target[part * own : (part + 1) * own, :] = keep[rows, :] + got[rows, :]
        if k > 0:
            west = got[2 * share : 2 * share + rim, :]
            east = got[2 * share + rim : 2 * share + 2 * rim, :]
            target[2 * own : 2 * own + rim, :] = jnp.where(lev_at == 0, east, west)


def aim_kernel(
    fields, rows, cols, strip_rows, strip_cols, slot_count, moves, share, touching, slims,
    plan, ring, first_got, kept, *refs,
):
    crossing = lax.axis_size("nest") - 1
    nest_gots, rest = refs[:crossing], refs[crossing + 1 :]
    partial, zone_self, zone_sends, total = rest[0], rest[1], rest[2:-1], rest[-1]
    planes = 2 * fields
    rim = planes * BWP
    own = slot_count * STEPS * rim
    tile_at, tiles = lax.axis_index("tile"), lax.axis_size("tile")
    nest_at = lax.axis_index("nest")
    lev_at = lax.axis_index("lev")

    sums = kept[...]
    for got in nest_gots:
        sums = sums + got[0 : 2 * own, :]
    total[...] = sums

    lane = lane_iota()
    col_base = lev_at * (strip_cols // 3 - 3)
    for j in range(slot_count):
        at = j * STEPS * rim
        both = STEPS * rim
        strip = pltpu.roll(total[at : at + both, :], (LANES - col_base) % LANES, 1)
        side = total[own + at : own + at + both, :]
        second = row_iota(both) >= rim
        origins = [plan[j * PLAN + s] - tile_at * rows for s in range(STEPS)]
        for k in moves:
            dest = lax.bitwise_xor(tile_at, k)
            parts = []
            for s in range(STEPS):
                south = origins[s] >= SPLIT
                wanted = ((dest == 0) & south) | ((dest == tiles - 1) & jnp.logical_not(south))
                at_lane = SLIM * j if k in slims else ZONE_AT
                offset = ROW_AT + origins[s] + (strip_rows // 3) * dest - 3 - at_lane
                source = lane + offset
                fits = (source >= ROW_AT - RING) & (source < ROW_AT + rows + RING)
                turned = pltpu.roll(side, (64 * LANES - offset) % LANES, 1)
                turned = jnp.where(fits, turned, 0.0)
                if k not in slims:
                    turned = jnp.where(lane < ZONE_AT, strip * wanted.astype(jnp.float32), turned)
                parts.append(turned)
            target = zone_self if k == 0 else zone_sends[moves.index(k) - 1]
            value = jnp.where(second, parts[1], parts[0])
            if k not in slims:
                target[at : at + both, :] = value
            elif j == 0:
                target[0:both, :] = value
            else:
                target[0:both, :] = jnp.where(lane >= SLIM * j, value, target[0:both, :])

    from_west = first_got[2 * share + rim : 2 * share + 2 * rim, :]
    from_east = first_got[2 * share : 2 * share + rim, :]
    far_west = jnp.zeros((rim, LANES), jnp.float32)
    far_east = jnp.zeros((rim, LANES), jnp.float32)
    for i, got in enumerate(nest_gots):
        other = lax.bitwise_xor(nest_at, i + 1)
        edge = got[2 * own : 2 * own + rim, :]
        far_west = far_west + jnp.where(other == nest_at - 1, edge, 0.0)
        far_east = far_east + jnp.where(other == nest_at + 1, edge, 0.0)
    from_west = jnp.where(lev_at == 0, far_west, from_west)
    from_east = jnp.where(lev_at == 0, from_east, far_east)
    for p in range(planes):
        two = slice(BWP * p, BWP * (p + 1))
        total[0:cols, :] = ring[p]
        total[0:RING, :] = total[0:RING, :] + from_west[two]
        total[cols - RING : cols, :] = total[cols - RING : cols, :] + from_east[two]
        total[0:LANES, :] = total[0:cols, :].T
        partial[p // 2, p % 2] = total[ROW_AT : ROW_AT + rows, :]
        below = total[ROW_AT - RING : ROW_AT, :]
        above = total[ROW_AT + rows : ROW_AT + rows + RING, :]
        for i, k in enumerate(moves[1:]):
            if k in touching:
                dest = lax.bitwise_xor(tile_at, k)
                start = (STEPS * rim if k in slims else own) + BWP * p
                zone_sends[i][start : start + BWP, :] = jnp.where(
                    dest > tile_at, above, below
                )


def edge_cols_kernel(fields, slot_count, nests, after, packed, wide):
    del after
    west_most = lax.axis_index("lev") == 0
    planes = 2 * fields
    half = nests.shape[4] - LANES
    wide[...] = jnp.zeros_like(wide)
    lane = lane_iota()
    for q in range(slot_count * planes):
        j, f, v = q // planes, (q % planes) // 2, q % 2
        spot = (q % 8) * 16
        wide[q % 8, :, 0:half] = nests[j, f, v, :, LANES : LANES + half]
        cells = jnp.where(west_most, wide[q % 8], nests[j, f, v, :, 0:LANES])
        shift = jnp.where(west_most, spot + 2 * LANES - (half - HALO), spot + 2 * LANES) % LANES
        cells = pltpu.roll(cells, shift, 1)
        row = cells if q % 8 == 0 else jnp.where(lane >= spot, cells, row)
        if q % 8 == 7 or q == slot_count * planes - 1:
            packed[q // 8] = row


def edge_rows_kernel(fields, strip_rows, slot_count, nests, packed, after, to_pair, to_cross):
    del after
    even = lax.rem(lax.axis_index("tile"), 2) == 0
    half = nests.shape[4] - LANES
    lows, highs, tail = slice(0, HALO), slice(strip_rows - HALO, strip_rows), slice(LANES, LANES + half)

    def put(at, low, high):
        to_pair[at : at + HALO, :] = jnp.where(even, high, low)
        to_cross[at : at + HALO, :] = jnp.where(even, low, high)

    for j in range(slot_count):
        for f in range(fields):
            at = (3 * fields * j + 2 * f) * HALO
            for v in range(2):
                put(at + v * HALO, nests[j, f, v, lows, 0:LANES], nests[j, f, v, highs, 0:LANES])
            at = (3 * fields * j + 2 * fields + f) * HALO
            put(
                at,
                jnp.concatenate([nests[j, f, v, lows, tail] for v in range(2)], 1),
                jnp.concatenate([nests[j, f, v, highs, tail] for v in range(2)], 1),
            )
    for g in range(packed.shape[0]):
        at = (3 * fields * slot_count + g) * HALO
        put(at, packed[g, lows, :], packed[g, highs, :])


def shift_kernel(fields, strip_rows, strip_cols, slot_count, plan, nests, packed, moved, cells):
    planes = 2 * fields
    half = strip_cols - LANES
    room = PAD + 8
    height = strip_rows + 16
    lane = lane_iota()
    goal = jnp.where(lax.axis_index("lev") == 0, half, LANES - HALO)
    in_goal = (lane >= goal) & (lane < goal + HALO)
    cells[...] = jnp.zeros_like(cells)

    def one(j, _):
        down, right = plan[j * PLAN + 2], plan[j * PLAN + 3]
        shift = (LANES - right) % LANES
        same = (lane + right >= 0) & (lane + right < LANES)
        start = room - 8 + down
        for f in range(fields):
            for v in range(2):
                cells[f, v, 0, room : room + strip_rows, :] = nests[j, f, v, :, 0:LANES]
                cells[f, v, 1, room : room + strip_rows, 0:half] = nests[j, f, v, :, LANES : LANES + half]
                n = j * planes + 2 * f + v
                goal_shift = (goal - lax.rem(n, 8) * 16 + 2 * LANES) % LANES
                got = jnp.where(in_goal, pltpu.roll(packed[lax.div(n, 8)], goal_shift, 1), 0.0)
                cells[f, v, 1, room : room + strip_rows, half:LANES] = got[:, half:LANES]
        for f in range(fields):
            for v in range(2):
                both = [
                    pltpu.roll(cells[f, v, a, pl.ds(start, height), :], shift, 1) for a in range(2)
                ]
                for a in range(2):
                    moved[j, f, v, a] = jnp.where(same, both[a], both[1 - a])
        return 0

    lax.fori_loop(0, slot_count, one, 0)


def advance_kernel(
    fields, strip_rows, strip_cols, slot_count,
    plan, rates, moved, pair, cross,
    inner_out, side_out, row_out, first, second,
):
    planes = 2 * fields
    half = strip_cols - LANES
    height = strip_rows + 16
    tile_at = lax.axis_index("tile")
    lev_at = lax.axis_index("lev")
    even = lax.rem(tile_at, 2) == 0
    lane = lane_iota()
    first_lane, last_lane = lane == 0, lane == LANES - 1
    chunk = 16 if height % 16 == 0 and strip_rows % 16 == 0 else 8
    row_start = pl.multiple_of(jnp.where(tile_at == 0, 0, strip_rows - 16), 8)
    outer = (tile_at == 0) | (tile_at == lax.axis_size("tile") - 1)
    goal = jnp.where(lev_at == 0, half, LANES - HALO)
    in_goal = (lane >= goal) & (lane < goal + HALO)

    lats = [rates[f : f + 1, :] for f in range(fields)]
    vers = [rates[fields + f : fields + f + 1, :] for f in range(fields)]
    stays = [1.0 - 4.0 * lats[f] - 2.0 * vers[f] for f in range(fields)]

    def stencil(f, source, at, size):
        x = [[source[f, v, a, at : at + size, :] for a in range(2)] for v in range(2)]
        new = [[None] * 2, [None] * 2]
        for v in range(2):
            sideways = beside(x[v], first_lane, last_lane)
            for a in range(2):
                near = (
                    sideways[a]
                    + source[f, v, a, at - 1 : at + size - 1, :]
                    + source[f, v, a, at + 1 : at + size + 1, :]
                )
                new[v][a] = stays[f] * x[v][a] + lats[f] * near + vers[f] * x[1 - v][a]
        return new

    def one(j, _):
        down, right = plan[j * PLAN + 2], plan[j * PLAN + 3]
        shift = (LANES - right) % LANES
        same = (lane + right >= 0) & (lane + right < LANES)
        for f in range(fields):
            for v in range(2):
                n = j * planes + 2 * f + v
                goal_shift = (goal - lax.rem(n, 8) * 16 + 2 * LANES) % LANES
                ends = []
                for got in (pair, cross):
                    main = got[pl.ds((3 * fields * j + 2 * f + v) * HALO, HALO), :]
                    tail = got[pl.ds((3 * fields * j + planes + f) * HALO, HALO), :]
                    if v == 1:
                        tail = pltpu.roll(tail, LANES - half, 1)
                    corner = got[pl.ds((3 * fields * slot_count + lax.div(n, 8)) * HALO, HALO), :]
                    corner = jnp.where(in_goal, pltpu.roll(corner, goal_shift, 1), 0.0)
                    tail = jnp.where(lane < half, tail, corner)
                    turned = [pltpu.roll(main, shift, 1), pltpu.roll(tail, shift, 1)]
                    ends.append([jnp.where(same, turned[a], turned[1 - a]) for a in range(2)])
                for a in range(2):
                    first[f, v, a, FRAME - 8 : FRAME - 8 + height, :] = moved[j, f, v, a]
                    low = jnp.where(even, ends[1][a], ends[0][a])
                    high = jnp.where(even, ends[0][a], ends[1][a])
                    first[f, v, a, pl.ds(FRAME - HALO - down, HALO), :] = low
                    first[f, v, a, pl.ds(FRAME + strip_rows - down, HALO), :] = high

        for west in (True, False):

            @pl.when(lev_at == 0 if west else lev_at > 0)
            def _(west=west):
                turn = 8 if west else LANES + 16 - half
                for v in range(2):
                    side = None
                    for f in range(fields):
                        near = first[f, v, 1, FRAME - 8 : FRAME - 8 + height, :]
                        if west:
                            low = first[f, v, 0, FRAME - 8 : FRAME - 8 + height, :]
                            near = jnp.where(lane < LANES // 2, low, near)
                        near = pltpu.roll(near, (turn + f * SLOT) % LANES, 1)
                        side = near if f == 0 else jnp.where(lane >= f * SLOT, near, side)
                    side_out[v, j] = side

        @pl.when(outer)
        def _():
            for f in range(fields):
                for v in range(2):
                    for a in range(2):
                        row_out[j, f, v, a] = first[f, v, a, pl.ds(FRAME - 8 + row_start, 32), :]

        for f in range(fields):
            for c in range(0, height, chunk):
                new = stencil(f, first, FRAME - 8 + c, chunk)
                for v in range(2):
                    for a in range(2):
                        second[f, v, a, 8 + c : 8 + c + chunk, :] = new[v][a]
        for f in range(fields):
            for c in range(0, strip_rows, chunk):
                new = stencil(f, second, 16 + c, chunk)
                for v in range(2):
                    inner_out[j, f, v, c : c + chunk, 0:LANES] = new[v][0]
                    inner_out[j, f, v, c : c + chunk, LANES : LANES + half] = new[v][1][:, :half]
        return 0

    lax.fori_loop(0, slot_count, one, 0)


def gaps(i):
    return jnp.minimum(i, SPAN - 1 - i)


def settle_kernel(
    fields, strip_rows, strip_cols, rows, slot_count, moves, touching, slims,
    plan, rates, inner, side_in, row_in, partial, zone_self, *refs,
):
    count = len(moves) - 1
    zone_gots = refs[:count]
    nest_out, parent_out = refs[count : count + 2]
    zone, turned, sides, strips, side_new, mixed, rows_mixed, rows_new, whole, done = refs[count + 2 :]
    planes = 2 * fields
    rim = planes * BWP
    both = STEPS * rim
    own = slot_count * both
    half = strip_cols - LANES
    height = strip_rows + 16
    tile_at, tiles = lax.axis_index("tile"), lax.axis_size("tile")
    nest_at = lax.axis_index("nest")
    lev_at = lax.axis_index("lev")
    lane = lane_iota()
    first_lane, last_lane = lane == 0, lane == LANES - 1

    below = jnp.zeros((rim, LANES), jnp.float32)
    above = jnp.zeros((rim, LANES), jnp.float32)
    for i, k in enumerate(moves[1:]):
        if k in touching:
            other = lax.bitwise_xor(tile_at, k)
            start = both if k in slims else own
            edge = zone_gots[i][start : start + rim, :]
            below = below + jnp.where(other == tile_at - 1, edge, 0.0)
            above = above + jnp.where(other == tile_at + 1, edge, 0.0)
    for p in range(planes):
        f, v = p // 2, p % 2
        two = slice(BWP * p, BWP * (p + 1))
        parent_out[f, v] = partial[f, v]
        parent_out[f, v, 0:RING, :] = partial[f, v, 0:RING, :] + below[two]
        parent_out[f, v, rows - RING : rows, :] = partial[f, v, rows - RING : rows, :] + above[two]

    whole_move = [[plan[j * PLAN + 2 + d] for d in range(2)] for j in range(slot_count)]
    last_move = [[plan[j * PLAN + 4 + d] for d in range(2)] for j in range(slot_count)]
    offsets = [[(0, 0) if s == 1 else last_move[j] for s in range(STEPS)] for j in range(slot_count)]
    earlier = [[whole_move[j], last_move[j]] for j in range(slot_count)]

    total = zone_self[0:own, :]
    for k, got in zip(moves[1:], zone_gots):
        if k not in slims:
            total = total + got[0:own, :]
    zone[...] = jnp.zeros_like(zone)
    zone[0:own, :] = total
    for k, got in zip(moves[1:], zone_gots):
        if k in slims:
            for j in range(slot_count):
                part = pltpu.roll(got[0:both, :], (LANES + ZONE_AT - SLIM * j) % LANES, 1)
                part = jnp.where((lane >= ZONE_AT) & (lane < ZONE_AT + SLIM), part, 0.0)
                zone[j * both : (j + 1) * both, :] = zone[j * both : (j + 1) * both, :] + part
    second = row_iota(both) >= rim
    col_base = lev_at * (strip_cols // 3 - 3)
    col_from = lev_at * strip_cols
    gap = (half + LANES) // 2
    owner = jnp.zeros((1, LANES), jnp.int32)
    for f in range(1, fields):
        owner = owner + (lane >= f * SLOT).astype(jnp.int32)
    side_cols = lane - SLOT * owner + jnp.where(lev_at == 0, -8, 2 * strip_cols - 16)
    lane_cols = (
        lane + col_from,
        jnp.where(lane < gap, lane + LANES, lane - LANES) + col_from,
        side_cols,
    )
    for j in range(slot_count):
        block = zone[j * both : (j + 1) * both, :]
        for a in range(3):
            picks = [
                jnp.clip(third(jnp.clip(lane_cols[a] + offsets[j][s][1], 0, SPAN - 1)) - col_base, 0, ZONE_AT - 1)
                for s in range(STEPS)
            ]
            strips[j, a] = jnp.take_along_axis(block, jnp.where(second, picks[1], picks[0]), axis=1)
        picks = [
            jnp.clip(
                third(jnp.clip(lane + (tile_at * strip_rows - 8) + offsets[j][s][0], 0, SPAN - 1))
                - ((strip_rows // 3) * tile_at - 3)
                + ZONE_AT,
                ZONE_AT,
                LANES - 1,
            )
            for s in range(STEPS)
        ]
        turned[j * both : (j + 1) * both, :] = jnp.take_along_axis(
            block, jnp.where(second, picks[1], picks[0]), axis=1
        )
    sides[...] = turned[...].T

    chunk = 16 if height % 16 == 0 else 8
    lats = [rates[f : f + 1, :] for f in range(fields)]
    vers = [rates[fields + f : fields + f + 1, :] for f in range(fields)]
    lat, ver = lats[0], vers[0]
    for f in range(1, fields):
        lat = jnp.where(owner >= f, lats[f], lat)
        ver = jnp.where(owner >= f, vers[f], ver)
    stay = 4.0 * lat + 2.0 * ver
    for s in range(STEPS):
        insides = {}
        for j in range(slot_count):
            by_row, by_col = offsets[j][s]
            was_row, was_col = earlier[j][s]
            col = side_cols + by_col
            col_gap = gaps(col)
            col_kept = gaps(side_cols + was_col)
            depth = jnp.where((col < 3) | ((col >= SPAN // 2) & (col < SPAN - 3)), 0, 1)
            lines, picks = [], []
            for v in range(2):
                picks.append(jnp.minimum(j * both + s * rim + v * BWP + 2 * BWP * owner + depth, own - 1))
                pair_of = []
                for r in range(BWP):
                    n = s * rim + v * BWP + r
                    line = strips[j, 2, n : n + 1, :]
                    for f in range(1, fields):
                        m = n + 2 * BWP * f
                        line = jnp.where(owner >= f, strips[j, 2, m : m + 1, :], line)
                    pair_of.append(line)
                lines.append(pair_of)
            for c in range(0, height, chunk):
                base = row_iota(chunk) + (tile_at * strip_rows - 8 + c)
                i = base + by_row
                distance = jnp.minimum(gaps(i), col_gap)
                kept = jnp.minimum(gaps(base + was_row), col_kept)
                w = jnp.clip(BORDER - distance, 0, BORDER).astype(jnp.float32) * (1.0 / BORDER)
                w = jnp.where(kept >= 0, w, 1.0)
                in_rows = (i < BORDER) | (i >= SPAN - BORDER)
                early = (i < 3) | ((i >= SPAN // 2) & (i < SPAN - 3))
                insides[j, c] = (distance >= 1).astype(jnp.float32)
                for v in range(2):
                    pick = jnp.broadcast_to(picks[v], (chunk, LANES))
                    side = jnp.take_along_axis(sides[c : c + chunk, :], pick, axis=1)
                    strip = jnp.where(early, lines[v][0], lines[v][1])
                    driving = jnp.where(in_rows, strip, side)
                    x = side_in[v, j, c : c + chunk, :] if s == 0 else side_new[v, j, c : c + chunk, :]
                    mixed[v, j, 8 + c : 8 + c + chunk, :] = (1.0 - w) * x + w * driving
        for j in range(slot_count):
            for c in range(0, height, chunk):
                x = [mixed[v, j, 8 + c : 8 + c + chunk, :] for v in range(2)]
                for v in range(2):
                    near = (
                        pltpu.roll(x[v], 1, 1)
                        + pltpu.roll(x[v], LANES - 1, 1)
                        + mixed[v, j, 7 + c : 7 + c + chunk, :]
                        + mixed[v, j, 9 + c : 9 + c + chunk, :]
                    )
                    change = lat * near + ver * x[1 - v] - stay * x[v]
                    side_new[v, j, c : c + chunk, :] = x[v] + insides[j, c] * change

    outer = (tile_at == 0) | (tile_at == tiles - 1)
    window = jnp.where(tile_at == 0, -8, tile_at * strip_rows + strip_rows - 24)
    row_start = pl.multiple_of(jnp.where(tile_at == 0, 0, strip_rows - 16), 8)
    line = row_iota(16)
    line_from = jnp.where(tile_at == 0, 0, 16 - HALO)
    lows = (0, jnp.where(lev_at > 0, half - HALO, LANES))
    highs = (jnp.where(lev_at == 0, HALO, 0), half)
    across = lane_iota(16)
    near_row = [
        (line >= line_from)
        & (line < line_from + HALO)
        & ((across < lows[a]) | (across >= highs[a]))
        for a in range(2)
    ]

    def one(j, _):
        for west in (True, False):

            @pl.when(lev_at == 0 if west else lev_at > 0)
            def _(west=west):
                for f in range(fields):
                    back = (2 * LANES + (-8 if west else half - 16) - f * SLOT) % LANES
                    for v in range(2):
                        near = pltpu.roll(side_new[v, j, 8 : 8 + strip_rows, :], back, 1)
                        first = inner[j, f, v, :, 0:LANES]
                        second = inner[j, f, v, :, LANES : LANES + half]
                        if west:
                            first = jnp.where(lane < HALO, near, first)
                        else:
                            second = jnp.where(lane[:, :half] >= half - HALO, near[:, :half], second)
                        whole[j, f, v, :, 0:LANES] = first
                        whole[j, f, v, :, LANES : LANES + half] = second

        @pl.when(outer)
        def _():
            full, last = plan[j * PLAN + 2], plan[j * PLAN + 4]
            base = row_iota(32) + window
            for s in range(STEPS):
                i = base + (last if s == 0 else 0)
                kept = gaps(base + (full if s == 0 else last)) >= 0
                w = jnp.clip(BORDER - gaps(i), 0, BORDER).astype(jnp.float32) * (1.0 / BORDER)
                w = jnp.where(kept, w, 1.0)
                rest = 1.0 - w
                inside = (gaps(i) >= 1).astype(jnp.float32)
                early = (i < 3) | ((i >= SPAN // 2) & (i < SPAN - 3))
                for f in range(fields):
                    for v in range(2):
                        n = s * rim + (2 * f + v) * BWP
                        for a in range(2):
                            driving = jnp.where(
                                early, strips[j, a, n : n + 1, :], strips[j, a, n + 1 : n + 2, :]
                            )
                            x = row_in[j, f, v, a] if s == 0 else rows_new[f, v, a]
                            rows_mixed[f, v, a, 8:40, :] = rest * x + w * driving
                for f in range(fields):
                    stay = 4.0 * lats[f] + 2.0 * vers[f]
                    value = [[rows_mixed[f, v, a, 8:40, :] for a in range(2)] for v in range(2)]
                    for v in range(2):
                        sideways = beside(value[v], first_lane, last_lane)
                        for a in range(2):
                            near = (
                                sideways[a]
                                + rows_mixed[f, v, a, 7:39, :]
                                + rows_mixed[f, v, a, 9:41, :]
                            )
                            change = (
                                lats[f] * near + vers[f] * value[1 - v][a] - stay * value[v][a]
                            )
                            rows_new[f, v, a] = value[v][a] + inside * change
            for f in range(fields):
                for v in range(2):
                    target = pl.ds(row_start, 16)
                    whole[j, f, v, target, 0:LANES] = jnp.where(
                        near_row[0], rows_new[f, v, 0, 8:24, :], whole[j, f, v, target, 0:LANES]
                    )
                    whole[j, f, v, target, LANES : LANES + half] = jnp.where(
                        near_row[1][:, :half],
                        rows_new[f, v, 1, 8:24, 0:half],
                        whole[j, f, v, target, LANES : LANES + half],
                    )

        pltpu.make_async_copy(whole.at[j], nest_out.at[j], done.at[j]).start()
        return 0

    lax.fori_loop(0, slot_count, one, 0)

    def wait(j, _):
        pltpu.make_async_copy(whole.at[j], nest_out.at[j], done.at[j]).wait()
        return 0

    lax.fori_loop(0, slot_count, wait, 0)


def per_device(parent_field, nest_fields, lateral_rate, vertical_rate, centres, slot_storm):
    fields, _, rows, cols = parent_field.shape
    slot_count, _, _, strip_rows, strip_cols = nest_fields.shape
    storms = slot_storm.shape[0]
    tiles, groups, levs = lax.axis_size("tile"), lax.axis_size("nest"), lax.axis_size("lev")
    planes = 2 * fields
    rim = planes * BWP
    share = storms * STEPS * rim
    own = slot_count * STEPS * rim
    height = strip_rows + 2 * PAD
    half = strip_cols - LANES
    f32 = jnp.float32

    def shaped(*dims):
        return jax.ShapeDtypeStruct(dims, f32)

    pair_list = [(t, t ^ 1) for t in range(tiles) if t ^ 1 < tiles]
    cross_list = [(t, t - 1 if t % 2 == 0 else t + 1) for t in range(1, tiles - 1)]
    centres = jnp.swapaxes(centres, 1, 2)

    send, keep, ring, plan, rates, nests = pl.pallas_call(
        lambda *refs: strips_kernel(fields, rows, cols, storms, slot_count, *refs),
        in_specs=[HBM_SPEC] * 6,
        out_specs=[VMEM_SPEC] * 3 + [SMEM_SPEC] + [VMEM_SPEC] * 2,
        out_shape=[
            shaped(2 * share + 2 * rim, LANES),
            shaped(2 * share, LANES),
            shaped(planes, cols, LANES),
            jax.ShapeDtypeStruct((slot_count * PLAN,), jnp.int32),
            shaped(2 * fields, LANES),
            shaped(*nest_fields.shape),
        ],
        scratch_shapes=[pltpu.VMEM((planes, 2, rows + 16, LANES), f32)] * 3
        + [pltpu.VMEM((planes, cols + 16, LANES), f32)] * 3
        + [
            pltpu.VMEM((LANES, LANES), f32),
            pltpu.VMEM((2, 24, LANES), f32),
            pltpu.SMEM(centres.shape, jnp.int32),
            pltpu.SMEM(slot_storm.shape, jnp.int32),
            pltpu.SMEM(lateral_rate.shape, f32),
            pltpu.SMEM(vertical_rate.shape, f32),
            pltpu.VMEM(parent_field.shape, f32),
            pltpu.SemaphoreType.DMA((6,)),
        ],
        compiler_params=params(),
        name="strips",
    )(
        *(
            pltpu.with_memory_space_constraint(x, pltpu.HBM)
            for x in (centres, slot_storm, lateral_rate, vertical_rate, parent_field, nest_fields)
        )
    )
    got = lax.ppermute(send, "lev", [(l, l ^ 1) for l in range(levs)])

    bundles = -(-slot_count * planes // 8)
    packed = pl.pallas_call(
        lambda *refs: edge_cols_kernel(fields, slot_count, *refs),
        in_specs=[VMEM_SPEC, ANY_SPEC],
        out_specs=VMEM_SPEC,
        out_shape=shaped(bundles, strip_rows, LANES),
        scratch_shapes=[pltpu.VMEM((8, strip_rows, LANES), f32)],
        compiler_params=params(),
        name="edge_cols",
    )(nests, keep)
    packed = lax.ppermute(packed, "lev", [(l, l ^ 1) for l in range(levs)])

    kept, *sends = pl.pallas_call(
        lambda *refs: pair_up_kernel(own, share, rim, *refs),
        in_specs=[VMEM_SPEC] * 2,
        out_specs=[VMEM_SPEC] * groups,
        out_shape=[shaped(2 * own, LANES)] + [shaped(2 * own + rim, LANES)] * (groups - 1),
        compiler_params=params(),
        name="pair_up",
    )(keep, got)
    nest_gots = [
        lax.ppermute(x, "nest", [(n, n ^ (i + 1)) for n in range(groups)])
        for i, x in enumerate(sends)
    ]

    edge_lines = (3 * fields * slot_count + bundles) * HALO
    to_pair, to_cross = pl.pallas_call(
        lambda *refs: edge_rows_kernel(fields, strip_rows, slot_count, *refs),
        in_specs=[VMEM_SPEC] * 2 + [ANY_SPEC],
        out_specs=[VMEM_SPEC] * 2,
        out_shape=[shaped(edge_lines, LANES)] * 2,
        compiler_params=params(),
        name="edge_rows",
    )(nests, packed, kept)
    pair = lax.ppermute(to_pair, "tile", pair_list)
    cross = lax.ppermute(to_cross, "tile", cross_list)

    moved = pl.pallas_call(
        lambda *refs: shift_kernel(fields, strip_rows, strip_cols, slot_count, *refs),
        in_specs=[SMEM_SPEC] + [VMEM_SPEC] * 2,
        out_specs=VMEM_SPEC,
        out_shape=shaped(slot_count, fields, 2, 2, strip_rows + 16, LANES),
        scratch_shapes=[pltpu.VMEM((fields, 2, 2, strip_rows + 48, LANES), f32)],
        compiler_params=params(),
        cost_estimate=pl.CostEstimate(flops=3_000_000_000, bytes_accessed=10_000_000, transcendentals=0),
        name="shift",
    )(plan, nests, packed)

    def holds(source, dest):
        low = max((strip_rows // 3) * dest - 3, 0)
        high = tiles * rows - FP + min((strip_rows // 3) * (dest + 1) + 3, FP)
        return rows * source - RING < high and rows * (source + 1) + RING > low

    routes = {}
    for k in range(1, tiles):
        pairs = [
            (t, t ^ k)
            for t in range(tiles)
            if t ^ k < tiles and (holds(t, t ^ k) or holds(t ^ k, t) or abs(t - (t ^ k)) == 1)
        ]
        if pairs:
            routes[k] = pairs
    touching = tuple(k for k in routes if any(abs(a - b) == 1 for a, b in routes[k]))
    moves = (0, *routes)
    fits = slot_count * SLIM <= LANES and strip_rows // 3 + 6 <= SLIM
    slims = tuple(
        k for k in routes if fits and not any(b in (0, tiles - 1) for _, b in routes[k])
    )

    def message(k):
        if k == 0:
            return own
        if k not in touching:
            return own + rim + 8
        return (STEPS * rim if k in slims else own) + rim

    zone_shapes = [shaped(message(k), LANES) for k in moves]
    partial, zone_self, *zone_sends = pl.pallas_call(
        lambda *refs: aim_kernel(
            fields, rows, cols, strip_rows, strip_cols, slot_count, moves, share, touching, slims, *refs
        ),
        in_specs=[SMEM_SPEC] + [VMEM_SPEC] * (2 + groups) + [ANY_SPEC],
        out_specs=[VMEM_SPEC] * (1 + len(moves)),
        out_shape=[shaped(fields, 2, rows, cols), *zone_shapes],
        scratch_shapes=[pltpu.VMEM((2 * own, LANES), f32)],
        compiler_params=params(),
        name="aim",
    )(plan, ring, got, kept, *nest_gots, moved)
    zone_gots = [lax.ppermute(x, "tile", routes[k]) for k, x in zip(moves[1:], zone_sends)]

    inner, side_in, row_in = pl.pallas_call(
        lambda *refs: advance_kernel(fields, strip_rows, strip_cols, slot_count, *refs),
        in_specs=[SMEM_SPEC] + [VMEM_SPEC] * 4,
        out_specs=[VMEM_SPEC] * 3,
        out_shape=[
            shaped(*nest_fields.shape),
            shaped(2, slot_count, strip_rows + 16, LANES),
            shaped(slot_count, fields, 2, 2, 32, LANES),
        ],
        scratch_shapes=[
            pltpu.VMEM((fields, 2, 2, strip_rows + 2 * FRAME, LANES), f32),
            pltpu.VMEM((fields, 2, 2, strip_rows + 32, LANES), f32),
        ],
        compiler_params=params(),
        name="advance",
    )(plan, rates, moved, pair, cross)

    nest_final, parent_final = pl.pallas_call(
        lambda *refs: settle_kernel(
            fields, strip_rows, strip_cols, rows, slot_count, moves, touching, slims, *refs
        ),
        in_specs=[SMEM_SPEC] + [VMEM_SPEC] * (5 + len(moves)),
        out_specs=[ANY_SPEC, VMEM_SPEC],
        out_shape=[shaped(*nest_fields.shape), shaped(*parent_field.shape)],
        scratch_shapes=[
            pltpu.VMEM((LANES, LANES), f32),
            pltpu.VMEM((LANES, LANES), f32),
            pltpu.VMEM((LANES, LANES), f32),
            pltpu.VMEM((slot_count, 3, STEPS * rim, LANES), f32),
            pltpu.VMEM((2, slot_count, strip_rows + 16, LANES), f32),
            pltpu.VMEM((2, slot_count, strip_rows + 32, LANES), f32),
            pltpu.VMEM((fields, 2, 2, 48, LANES), f32),
            pltpu.VMEM((fields, 2, 2, 32, LANES), f32),
            pltpu.VMEM((slot_count, fields, 2, strip_rows, strip_cols), f32),
            pltpu.SemaphoreType.DMA((slot_count,)),
        ],
        compiler_params=params(),
        name="settle",
    )(
        plan, rates, inner, side_in, row_in, partial, zone_self, *zone_gots,
    )
    return (parent_final, nest_final)


def solution(mesh):
    placed = (
        P("member", None, "tile", ("nest", "lev")),
        P(("member", "nest"), None, None, "tile", "lev"),
        P(),
        P(),
        P("member", None, None),
        P("member"),
    )
    return jax.shard_map(
        per_device,
        mesh=mesh,
        in_specs=placed,
        out_specs=(
            P("member", None, "tile", ("nest", "lev")),
            P(("member", "nest"), None, None, "tile", "lev"),
        ),
        check_vma=False,
    )
```

```python
import jax
import jax.numpy as jnp
from jax import lax
from jax.experimental import pallas as pl
from jax.experimental.pallas import tpu as pltpu
from jax.sharding import PartitionSpec as P

FP = 128
BWP = 2
MOVE = 2
STEPS = 2
BORDER = 3 * BWP
SPAN = 3 * FP
HALO = STEPS * (3 * MOVE + 1)
PAD = 16
LANES = 128
SLIM = 40
FRAME = 32
PLAN = 8
RING = STEPS
ROW_AT = 32
ZONE_AT = 72
SPLIT = -(FP // 4)
SLOT = 24
VMEM_LIMIT = 40 * 1024 * 1024

SMEM_SPEC = pl.BlockSpec(memory_space=pltpu.SMEM)
VMEM_SPEC = pl.BlockSpec(memory_space=pltpu.VMEM)
HBM_SPEC = pl.BlockSpec(memory_space=pltpu.HBM)
ANY_SPEC = pl.BlockSpec(memory_space=pl.ANY)


def params(**more):
    return pltpu.CompilerParams(vmem_limit_bytes=VMEM_LIMIT, **more)


def lane_iota(rows=1, lanes=LANES):
    return lax.broadcasted_iota(jnp.int32, (rows, lanes), 1)


def row_iota(rows, lanes=LANES):
    return lax.broadcasted_iota(jnp.int32, (rows, lanes), 0)


def beside(x, first_lane, last_lane):
    left = [pltpu.roll(v, 1, 1) for v in x]
    right = [pltpu.roll(v, LANES - 1, 1) for v in x]
    return [
        jnp.where(first_lane, left[1 - a], left[a]) + jnp.where(last_lane, right[1 - a], right[a])
        for a in range(2)
    ]


def third(values):
    return (values * 21846) >> 16


def strips_kernel(
    fields, rows, cols, storms, slot_count,
    centres_in, slots_in, lateral_in, vertical_in, parent_in, nests_in,
    send, keep, ring_out, plan, rates, nests,
    plain0, plain1, plain2, turned0, turned1, turned2, block, gather,
    centres, slots, lateral, vertical, parent, arrived,
):
    sources = (
        (centres_in, centres),
        (slots_in, slots),
        (lateral_in, lateral),
        (vertical_in, vertical),
        (parent_in, parent),
        (nests_in, nests),
    )
    copies = [
        pltpu.make_async_copy(source, target, arrived.at[i])
        for i, (source, target) in enumerate(sources)
    ]
    for copy in copies:
        copy.start()
    planes = 2 * fields
    tile_at, tiles = lax.axis_index("tile"), lax.axis_size("tile")
    lev_at, levs = lax.axis_index("lev"), lax.axis_size("lev")
    col_at = lax.axis_index("nest") * levs + lev_at
    col_blocks = lax.axis_size("nest") * levs
    top = 8
    height = rows + 16
    width = cols + 16

    lane = lane_iota()
    first_lane, last_lane = lane == 0, lane == LANES - 1
    row = tile_at * rows + row_iota(height) - top
    tile_cols = (lane, jnp.where(lane < LANES // 2, lane + LANES, lane - LANES))
    within = [
        (
            (row >= 0) & (row < tiles * rows)
            & (col_at * cols + c >= 0) & (col_at * cols + c < col_blocks * cols)
        ).astype(jnp.float32)
        for c in tile_cols
    ]
    plain0[...] = jnp.zeros_like(plain0)
    turned0[...] = jnp.zeros_like(turned0)
    block[...] = jnp.zeros_like(block)
    for copy in copies[:5]:
        copy.wait()
    for f in range(fields):
        rates[f : f + 1, :] = jnp.full((1, LANES), lateral[f], jnp.float32)
        rates[fields + f : fields + f + 1, :] = jnp.full((1, LANES), vertical[f], jnp.float32)
    for j in range(slot_count):
        storm = slots[lax.axis_index("nest") * slot_count + j]
        at = [[centres[n, d, storm] for d in range(2)] for n in range(STEPS + 1)]
        for d in range(2):
            plan[j * PLAN + d] = at[d + 1][0] - FP // 2
            plan[j * PLAN + 2 + d] = 3 * (at[STEPS][d] - at[0][d])
            plan[j * PLAN + 4 + d] = 3 * (at[STEPS][d] - at[STEPS - 1][d])
    for p in range(planes):
        plain0[p, 0, top : top + rows, :] = parent[p // 2, p % 2]
        block[ROW_AT : ROW_AT + rows, :] = parent[p // 2, p % 2]
        turned0[p, top : top + cols, :] = block[...].T

    inner = slice(1, height - 1)

    def plain_step(source, target, mask):
        for f in range(fields):
            lat, ver = lateral[f], vertical[f]
            for v in range(2):
                x = [source[2 * f + v, a, inner, :] for a in range(2)]
                sideways = beside(x, first_lane, last_lane)
                for a in range(2):
                    near = (
                        sideways[a]
                        + source[2 * f + v, a, 2:height, :]
                        + source[2 * f + v, a, 0 : height - 2, :]
                    )
                    other = source[2 * f + 1 - v, a, inner, :]
                    new = x[a] + lat * (near - 4.0 * x[a]) + ver * (other - 2.0 * x[a])
                    if mask is not None:
                        new = new * mask[a][inner, :]
                    target[2 * f + v, a, inner, :] = new
                    for edge in (0, height - 1):
                        target[2 * f + v, a, edge : edge + 1, :] = jnp.zeros(
                            (1, LANES), jnp.float32
                        )

    plain_step(plain0, plain1, within)
    plain_step(plain1, plain2, None)

    row_t = tile_at * rows + lane_iota() - ROW_AT
    col_t = col_at * cols + row_iota(width) - top
    within_t = (
        (row_t >= 0) & (row_t < tiles * rows) & (col_t >= 0) & (col_t < col_blocks * cols)
    ).astype(jnp.float32)

    def turned_step(source, target, mask):
        for f in range(fields):
            lat, ver = lateral[f], vertical[f]
            for v in range(2):
                x = source[2 * f + v, 1 : width - 1, :]
                near = (
                    source[2 * f + v, 2:width, :]
                    + source[2 * f + v, 0 : width - 2, :]
                    + pltpu.roll(x, 1, 1)
                    + pltpu.roll(x, LANES - 1, 1)
                )
                other = source[2 * f + 1 - v, 1 : width - 1, :]
                new = x + lat * (near - 4.0 * x) + ver * (other - 2.0 * x)
                if mask is not None:
                    new = new * mask[1 : width - 1, :]
                target[2 * f + v, 1 : width - 1, :] = new
                target[2 * f + v, 0:1, :] = jnp.zeros((1, LANES), jnp.float32)
                target[2 * f + v, width - 1 : width, :] = jnp.zeros((1, LANES), jnp.float32)

    turned_step(turned0, turned1, within_t)
    turned_step(turned1, turned2, None)

    share = storms * STEPS * planes * BWP
    for j in range(storms):
        storm = slots[j]
        for s in range(STEPS):
            at = (j * STEPS + s) * planes * BWP
            corner_row = centres[s + 1, 0, storm] - FP // 2 - tile_at * rows
            corner_col = centres[s + 1, 1, storm] - FP // 2 - col_at * cols
            plain = (plain1, plain2)[s]
            turned = (turned1, turned2)[s]
            first = jnp.where(corner_row >= SPLIT, corner_row, corner_row + FP - BWP)
            first = jnp.clip(first + top, 0, height - BWP)
            for p in range(planes):
                for a in range(2):
                    gather[a, BWP * p : BWP * (p + 1), :] = plain[p, a, pl.ds(first, BWP), :]
            shift = (64 * LANES - corner_col) % LANES
            window = [pltpu.roll(gather[a], shift, 1) for a in range(2)]
            place = lane + corner_col
            main = (place >= 0) & (place < cols)
            rim = (place >= -RING) & (place < cols + RING)
            window = jnp.where(main, window[0], jnp.where(rim, window[1], 0.0))[: planes * BWP]
            send[at : at + planes * BWP, :] = window
            keep[at : at + planes * BWP, :] = window
            mine = corner_col + (FP - BWP) * lev_at
            theirs = corner_col + (FP - BWP) * (levs - 1 - lev_at)
            for target, start in ((keep, mine), (send, theirs)):
                start = jnp.clip(start + top, 0, width - BWP)
                for p in range(planes):
                    target[share + at + BWP * p : share + at + BWP * (p + 1), :] = turned[
                        p, pl.ds(start, BWP), :
                    ]
    for p in range(planes):
        send[2 * share + BWP * p : 2 * share + BWP * (p + 1), :] = turned2[p, top - RING : top, :]
        at = 2 * share + planes * BWP + BWP * p
        send[at : at + BWP, :] = turned2[p, top + cols : top + cols + RING, :]
        ring_out[p] = turned2[p, top : top + cols, :]
    copies[5].wait()


def pair_up_kernel(own, share, rim, keep, got, kept, *sends):
    nest_at = lax.axis_index("nest")
    lev_at = lax.axis_index("lev")
    for k in range(len(sends) + 1):
        group = lax.bitwise_xor(nest_at, k)
        target = kept if k == 0 else sends[k - 1]
        for part in range(2):
            rows = pl.ds(pl.multiple_of(part * share + group * own, 8), own)
            target[part * own : (part + 1) * own, :] = keep[rows, :] + got[rows, :]
        if k > 0:
            west = got[2 * share : 2 * share + rim, :]
            east = got[2 * share + rim : 2 * share + 2 * rim, :]
            target[2 * own : 2 * own + rim, :] = jnp.where(lev_at == 0, east, west)


def aim_kernel(
    fields, rows, cols, strip_rows, strip_cols, slot_count, moves, share, touching, slims,
    plan, ring, first_got, kept, *refs,
):
    crossing = lax.axis_size("nest") - 1
    nest_gots, rest = refs[:crossing], refs[crossing + 1 :]
    partial, zone_self, zone_sends, total = rest[0], rest[1], rest[2:-1], rest[-1]
    planes = 2 * fields
    rim = planes * BWP
    own = slot_count * STEPS * rim
    tile_at, tiles = lax.axis_index("tile"), lax.axis_size("tile")
    nest_at = lax.axis_index("nest")
    lev_at = lax.axis_index("lev")

    sums = kept[...]
    for got in nest_gots:
        sums = sums + got[0 : 2 * own, :]
    total[...] = sums

    lane = lane_iota()
    col_base = lev_at * (strip_cols // 3 - 3)
    for j in range(slot_count):
        at = j * STEPS * rim
        both = STEPS * rim
        strip = pltpu.roll(total[at : at + both, :], (LANES - col_base) % LANES, 1)
        side = total[own + at : own + at + both, :]
        second = row_iota(both) >= rim
        origins = [plan[j * PLAN + s] - tile_at * rows for s in range(STEPS)]
        for k in moves:
            dest = lax.bitwise_xor(tile_at, k)
            parts = []
            for s in range(STEPS):
                south = origins[s] >= SPLIT
                wanted = ((dest == 0) & south) | ((dest == tiles - 1) & jnp.logical_not(south))
                at_lane = SLIM * j if k in slims else ZONE_AT
                offset = ROW_AT + origins[s] + (strip_rows // 3) * dest - 3 - at_lane
                source = lane + offset
                fits = (source >= ROW_AT - RING) & (source < ROW_AT + rows + RING)
                turned = pltpu.roll(side, (64 * LANES - offset) % LANES, 1)
                turned = jnp.where(fits, turned, 0.0)
                if k not in slims:
                    turned = jnp.where(lane < ZONE_AT, strip * wanted.astype(jnp.float32), turned)
                parts.append(turned)
            target = zone_self if k == 0 else zone_sends[moves.index(k) - 1]
            value = jnp.where(second, parts[1], parts[0])
            if k not in slims:
                target[at : at + both, :] = value
            elif j == 0:
                target[0:both, :] = value
            else:
                target[0:both, :] = jnp.where(lane >= SLIM * j, value, target[0:both, :])

    from_west = first_got[2 * share + rim : 2 * share + 2 * rim, :]
    from_east = first_got[2 * share : 2 * share + rim, :]
    far_west = jnp.zeros((rim, LANES), jnp.float32)
    far_east = jnp.zeros((rim, LANES), jnp.float32)
    for i, got in enumerate(nest_gots):
        other = lax.bitwise_xor(nest_at, i + 1)
        edge = got[2 * own : 2 * own + rim, :]
        far_west = far_west + jnp.where(other == nest_at - 1, edge, 0.0)
        far_east = far_east + jnp.where(other == nest_at + 1, edge, 0.0)
    from_west = jnp.where(lev_at == 0, far_west, from_west)
    from_east = jnp.where(lev_at == 0, from_east, far_east)
    for p in range(planes):
        two = slice(BWP * p, BWP * (p + 1))
        total[0:cols, :] = ring[p]
        total[0:RING, :] = total[0:RING, :] + from_west[two]
        total[cols - RING : cols, :] = total[cols - RING : cols, :] + from_east[two]
        total[0:LANES, :] = total[0:cols, :].T
        partial[p // 2, p % 2] = total[ROW_AT : ROW_AT + rows, :]
        below = total[ROW_AT - RING : ROW_AT, :]
        above = total[ROW_AT + rows : ROW_AT + rows + RING, :]
        for i, k in enumerate(moves[1:]):
            if k in touching:
                dest = lax.bitwise_xor(tile_at, k)
                start = (STEPS * rim if k in slims else own) + BWP * p
                zone_sends[i][start : start + BWP, :] = jnp.where(
                    dest > tile_at, above, below
                )


def edge_cols_kernel(fields, slot_count, nests, after, packed, wide):
    del after
    west_most = lax.axis_index("lev") == 0
    planes = 2 * fields
    half = nests.shape[4] - LANES
    wide[...] = jnp.zeros_like(wide)
    lane = lane_iota()
    for west in (True, False):

        @pl.when(west_most if west else jnp.logical_not(west_most))
        def _(west=west):
            row = None
            for q in range(slot_count * planes):
                j, f, v = q // planes, (q % planes) // 2, q % 2
                spot = (q % 8) * 16
                if west:
                    wide[q % 8, :, 0:half] = nests[j, f, v, :, LANES : LANES + half]
                    cells = wide[q % 8]
                else:
                    cells = nests[j, f, v, :, 0:LANES]
                turn = (spot + (2 * LANES - (half - HALO) if west else 0)) % LANES
                cells = pltpu.roll(cells, turn, 1) if turn else cells
                row = cells if q % 8 == 0 else jnp.where(lane >= spot, cells, row)
                if q % 8 == 7 or q == slot_count * planes - 1:
                    packed[q // 8] = row


def edge_rows_kernel(fields, strip_rows, slot_count, nests, packed, after, to_pair, to_cross):
    del after
    even = lax.rem(lax.axis_index("tile"), 2) == 0
    half = nests.shape[4] - LANES
    lows, highs, tail = slice(0, HALO), slice(strip_rows - HALO, strip_rows), slice(LANES, LANES + half)

    def put(at, low, high):
        to_pair[at : at + HALO, :] = jnp.where(even, high, low)
        to_cross[at : at + HALO, :] = jnp.where(even, low, high)

    for j in range(slot_count):
        for f in range(fields):
            at = (3 * fields * j + 2 * f) * HALO
            for v in range(2):
                put(at + v * HALO, nests[j, f, v, lows, 0:LANES], nests[j, f, v, highs, 0:LANES])
            at = (3 * fields * j + 2 * fields + f) * HALO
            put(
                at,
                jnp.concatenate([nests[j, f, v, lows, tail] for v in range(2)], 1),
                jnp.concatenate([nests[j, f, v, highs, tail] for v in range(2)], 1),
            )
    for g in range(packed.shape[0]):
        at = (3 * fields * slot_count + g) * HALO
        put(at, packed[g, lows, :], packed[g, highs, :])


def shift_kernel(fields, strip_rows, strip_cols, slot_count, plan, nests, packed, moved, cells):
    planes = 2 * fields
    half = strip_cols - LANES
    room = PAD + 8
    height = strip_rows + 16
    lane = lane_iota()
    goal = jnp.where(lax.axis_index("lev") == 0, half, LANES - HALO)
    in_goal = (lane >= goal) & (lane < goal + HALO)
    cells[...] = jnp.zeros_like(cells)

    def one(j, _):
        down, right = plan[j * PLAN + 2], plan[j * PLAN + 3]
        shift = (LANES - right) % LANES
        same = (lane + right >= 0) & (lane + right < LANES)
        start = room - 8 + down
        for f in range(fields):
            for v in range(2):
                cells[f, v, 0, room : room + strip_rows, :] = nests[j, f, v, :, 0:LANES]
                cells[f, v, 1, room : room + strip_rows, 0:half] = nests[j, f, v, :, LANES : LANES + half]
                n = j * planes + 2 * f + v
                goal_shift = (goal - lax.rem(n, 8) * 16 + 2 * LANES) % LANES
                got = jnp.where(in_goal, pltpu.roll(packed[lax.div(n, 8)], goal_shift, 1), 0.0)
                cells[f, v, 1, room : room + strip_rows, half:LANES] = got[:, half:LANES]
        for f in range(fields):
            for v in range(2):
                both = [
                    pltpu.roll(cells[f, v, a, pl.ds(start, height), :], shift, 1) for a in range(2)
                ]
                for a in range(2):
                    moved[j, f, v, a] = jnp.where(same, both[a], both[1 - a])
        return 0

    lax.fori_loop(0, slot_count, one, 0)


def advance_kernel(
    fields, strip_rows, strip_cols, slot_count,
    plan, rates, moved, pair, cross,
    inner_out, side_out, row_out, first, second,
):
    planes = 2 * fields
    half = strip_cols - LANES
    height = strip_rows + 16
    tile_at = lax.axis_index("tile")
    lev_at = lax.axis_index("lev")
    even = lax.rem(tile_at, 2) == 0
    lane = lane_iota()
    first_lane, last_lane = lane == 0, lane == LANES - 1
    chunk = 16 if height % 16 == 0 and strip_rows % 16 == 0 else 8
    row_start = pl.multiple_of(jnp.where(tile_at == 0, 0, strip_rows - 16), 8)
    outer = (tile_at == 0) | (tile_at == lax.axis_size("tile") - 1)
    goal = jnp.where(lev_at == 0, half, LANES - HALO)
    in_goal = (lane >= goal) & (lane < goal + HALO)

    lats = [rates[f : f + 1, :] for f in range(fields)]
    vers = [rates[fields + f : fields + f + 1, :] for f in range(fields)]
    stays = [1.0 - 4.0 * lats[f] - 2.0 * vers[f] for f in range(fields)]

    def stencil(f, source, at, size):
        x = [[source[f, v, a, at : at + size, :] for a in range(2)] for v in range(2)]
        new = [[None] * 2, [None] * 2]
        for v in range(2):
            sideways = beside(x[v], first_lane, last_lane)
            for a in range(2):
                near = (
                    sideways[a]
                    + source[f, v, a, at - 1 : at + size - 1, :]
                    + source[f, v, a, at + 1 : at + size + 1, :]
                )
                new[v][a] = stays[f] * x[v][a] + lats[f] * near + vers[f] * x[1 - v][a]
        return new

    def one(j, _):
        down, right = plan[j * PLAN + 2], plan[j * PLAN + 3]
        shift = (LANES - right) % LANES
        same = (lane + right >= 0) & (lane + right < LANES)
        for f in range(fields):
            for v in range(2):
                n = j * planes + 2 * f + v
                goal_shift = (goal - lax.rem(n, 8) * 16 + 2 * LANES) % LANES
                ends = []
                for got in (pair, cross):
                    main = got[pl.ds((3 * fields * j + 2 * f + v) * HALO, HALO), :]
                    tail = got[pl.ds((3 * fields * j + planes + f) * HALO, HALO), :]
                    if v == 1:
                        tail = pltpu.roll(tail, LANES - half, 1)
                    corner = got[pl.ds((3 * fields * slot_count + lax.div(n, 8)) * HALO, HALO), :]
                    corner = jnp.where(in_goal, pltpu.roll(corner, goal_shift, 1), 0.0)
                    tail = jnp.where(lane < half, tail, corner)
                    turned = [pltpu.roll(main, shift, 1), pltpu.roll(tail, shift, 1)]
                    ends.append([jnp.where(same, turned[a], turned[1 - a]) for a in range(2)])
                for a in range(2):
                    first[f, v, a, FRAME - 8 : FRAME - 8 + height, :] = moved[j, f, v, a]
                    low = jnp.where(even, ends[1][a], ends[0][a])
                    high = jnp.where(even, ends[0][a], ends[1][a])
                    first[f, v, a, pl.ds(FRAME - HALO - down, HALO), :] = low
                    first[f, v, a, pl.ds(FRAME + strip_rows - down, HALO), :] = high

        for west in (True, False):

            @pl.when(lev_at == 0 if west else lev_at > 0)
            def _(west=west):
                turn = 8 if west else LANES + 16 - half
                for v in range(2):
                    side = None
                    for f in range(fields):
                        near = first[f, v, 1, FRAME - 8 : FRAME - 8 + height, :]
                        if west:
                            low = first[f, v, 0, FRAME - 8 : FRAME - 8 + height, :]
                            near = jnp.where(lane < LANES // 2, low, near)
                        near = pltpu.roll(near, (turn + f * SLOT) % LANES, 1)
                        side = near if f == 0 else jnp.where(lane >= f * SLOT, near, side)
                    side_out[v, j] = side

        @pl.when(outer)
        def _():
            for f in range(fields):
                for v in range(2):
                    for a in range(2):
                        row_out[j, f, v, a] = first[f, v, a, pl.ds(FRAME - 8 + row_start, 32), :]

        for f in range(fields):
            for c in range(0, height, chunk):
                new = stencil(f, first, FRAME - 8 + c, chunk)
                for v in range(2):
                    for a in range(2):
                        second[f, v, a, 8 + c : 8 + c + chunk, :] = new[v][a]
        for f in range(fields):
            for c in range(0, strip_rows, chunk):
                new = stencil(f, second, 16 + c, chunk)
                for v in range(2):
                    inner_out[j, f, v, c : c + chunk, 0:LANES] = new[v][0]
                    inner_out[j, f, v, c : c + chunk, LANES : LANES + half] = new[v][1][:, :half]
        return 0

    lax.fori_loop(0, slot_count, one, 0)


def gaps(i):
    return jnp.minimum(i, SPAN - 1 - i)


def settle_kernel(
    fields, strip_rows, strip_cols, rows, slot_count, moves, touching, slims,
    plan, rates, inner, side_in, row_in, partial, zone_self, *refs,
):
    count = len(moves) - 1
    zone_gots = refs[:count]
    nest_out, parent_out = refs[count : count + 2]
    zone, turned, sides, strips, side_new, mixed, rows_mixed, rows_new, whole, done = refs[count + 2 :]
    planes = 2 * fields
    rim = planes * BWP
    both = STEPS * rim
    own = slot_count * both
    half = strip_cols - LANES
    height = strip_rows + 16
    tile_at, tiles = lax.axis_index("tile"), lax.axis_size("tile")
    nest_at = lax.axis_index("nest")
    lev_at = lax.axis_index("lev")
    lane = lane_iota()
    first_lane, last_lane = lane == 0, lane == LANES - 1

    below = jnp.zeros((rim, LANES), jnp.float32)
    above = jnp.zeros((rim, LANES), jnp.float32)
    for i, k in enumerate(moves[1:]):
        if k in touching:
            other = lax.bitwise_xor(tile_at, k)
            start = both if k in slims else own
            edge = zone_gots[i][start : start + rim, :]
            below = below + jnp.where(other == tile_at - 1, edge, 0.0)
            above = above + jnp.where(other == tile_at + 1, edge, 0.0)
    for p in range(planes):
        f, v = p // 2, p % 2
        two = slice(BWP * p, BWP * (p + 1))
        parent_out[f, v] = partial[f, v]
        parent_out[f, v, 0:RING, :] = partial[f, v, 0:RING, :] + below[two]
        parent_out[f, v, rows - RING : rows, :] = partial[f, v, rows - RING : rows, :] + above[two]

    whole_move = [[plan[j * PLAN + 2 + d] for d in range(2)] for j in range(slot_count)]
    last_move = [[plan[j * PLAN + 4 + d] for d in range(2)] for j in range(slot_count)]
    offsets = [[(0, 0) if s == 1 else last_move[j] for s in range(STEPS)] for j in range(slot_count)]
    earlier = [[whole_move[j], last_move[j]] for j in range(slot_count)]

    total = zone_self[0:own, :]
    for k, got in zip(moves[1:], zone_gots):
        if k not in slims:
            total = total + got[0:own, :]
    zone[...] = jnp.zeros_like(zone)
    zone[0:own, :] = total
    for k, got in zip(moves[1:], zone_gots):
        if k in slims:
            for j in range(slot_count):
                part = pltpu.roll(got[0:both, :], (LANES + ZONE_AT - SLIM * j) % LANES, 1)
                part = jnp.where((lane >= ZONE_AT) & (lane < ZONE_AT + SLIM), part, 0.0)
                zone[j * both : (j + 1) * both, :] = zone[j * both : (j + 1) * both, :] + part
    second = row_iota(both) >= rim
    col_base = lev_at * (strip_cols // 3 - 3)
    col_from = lev_at * strip_cols
    gap = (half + LANES) // 2
    owner = jnp.zeros((1, LANES), jnp.int32)
    for f in range(1, fields):
        owner = owner + (lane >= f * SLOT).astype(jnp.int32)
    side_cols = lane - SLOT * owner + jnp.where(lev_at == 0, -8, 2 * strip_cols - 16)
    lane_cols = (
        lane + col_from,
        jnp.where(lane < gap, lane + LANES, lane - LANES) + col_from,
        side_cols,
    )
    for j in range(slot_count):
        block = zone[j * both : (j + 1) * both, :]
        for a in range(3):
            picks = [
                jnp.clip(third(jnp.clip(lane_cols[a] + offsets[j][s][1], 0, SPAN - 1)) - col_base, 0, ZONE_AT - 1)
                for s in range(STEPS)
            ]
            strips[j, a] = jnp.take_along_axis(block, jnp.where(second, picks[1], picks[0]), axis=1)
        picks = [
            jnp.clip(
                third(jnp.clip(lane + (tile_at * strip_rows - 8) + offsets[j][s][0], 0, SPAN - 1))
                - ((strip_rows // 3) * tile_at - 3)
                + ZONE_AT,
                ZONE_AT,
                LANES - 1,
            )
            for s in range(STEPS)
        ]
        turned[j * both : (j + 1) * both, :] = jnp.take_along_axis(
            block, jnp.where(second, picks[1], picks[0]), axis=1
        )
    sides[...] = turned[...].T

    chunk = 16 if height % 16 == 0 else 8
    lats = [rates[f : f + 1, :] for f in range(fields)]
    vers = [rates[fields + f : fields + f + 1, :] for f in range(fields)]
    lat, ver = lats[0], vers[0]
    for f in range(1, fields):
        lat = jnp.where(owner >= f, lats[f], lat)
        ver = jnp.where(owner >= f, vers[f], ver)
    stay = 4.0 * lat + 2.0 * ver
    for s in range(STEPS):
        insides = {}
        for j in range(slot_count):
            by_row, by_col = offsets[j][s]
            was_row, was_col = earlier[j][s]
            col = side_cols + by_col
            col_gap = gaps(col)
            col_kept = gaps(side_cols + was_col)
            depth = jnp.where((col < 3) | ((col >= SPAN // 2) & (col < SPAN - 3)), 0, 1)
            lines, picks = [], []
            for v in range(2):
                picks.append(jnp.minimum(j * both + s * rim + v * BWP + 2 * BWP * owner + depth, own - 1))
                pair_of = []
                for r in range(BWP):
                    n = s * rim + v * BWP + r
                    line = strips[j, 2, n : n + 1, :]
                    for f in range(1, fields):
                        m = n + 2 * BWP * f
                        line = jnp.where(owner >= f, strips[j, 2, m : m + 1, :], line)
                    pair_of.append(line)
                lines.append(pair_of)
            for c in range(0, height, chunk):
                base = row_iota(chunk) + (tile_at * strip_rows - 8 + c)
                i = base + by_row
                distance = jnp.minimum(gaps(i), col_gap)
                kept = jnp.minimum(gaps(base + was_row), col_kept)
                w = jnp.clip(BORDER - distance, 0, BORDER).astype(jnp.float32) * (1.0 / BORDER)
                w = jnp.where(kept >= 0, w, 1.0)
                in_rows = (i < BORDER) | (i >= SPAN - BORDER)
                early = (i < 3) | ((i >= SPAN // 2) & (i < SPAN - 3))
                insides[j, c] = (distance >= 1).astype(jnp.float32)
                for v in range(2):
                    pick = jnp.broadcast_to(picks[v], (chunk, LANES))
                    side = jnp.take_along_axis(sides[c : c + chunk, :], pick, axis=1)
                    strip = jnp.where(early, lines[v][0], lines[v][1])
                    driving = jnp.where(in_rows, strip, side)
                    x = side_in[v, j, c : c + chunk, :] if s == 0 else side_new[v, j, c : c + chunk, :]
                    mixed[v, j, 8 + c : 8 + c + chunk, :] = (1.0 - w) * x + w * driving
        for j in range(slot_count):
            for c in range(0, height, chunk):
                x = [mixed[v, j, 8 + c : 8 + c + chunk, :] for v in range(2)]
                for v in range(2):
                    near = (
                        pltpu.roll(x[v], 1, 1)
                        + pltpu.roll(x[v], LANES - 1, 1)
                        + mixed[v, j, 7 + c : 7 + c + chunk, :]
                        + mixed[v, j, 9 + c : 9 + c + chunk, :]
                    )
                    change = lat * near + ver * x[1 - v] - stay * x[v]
                    side_new[v, j, c : c + chunk, :] = x[v] + insides[j, c] * change

    outer = (tile_at == 0) | (tile_at == tiles - 1)
    window = jnp.where(tile_at == 0, -8, tile_at * strip_rows + strip_rows - 24)
    row_start = pl.multiple_of(jnp.where(tile_at == 0, 0, strip_rows - 16), 8)
    line = row_iota(16)
    line_from = jnp.where(tile_at == 0, 0, 16 - HALO)
    lows = (0, jnp.where(lev_at > 0, half - HALO, LANES))
    highs = (jnp.where(lev_at == 0, HALO, 0), half)
    across = lane_iota(16)
    near_row = [
        (line >= line_from)
        & (line < line_from + HALO)
        & ((across < lows[a]) | (across >= highs[a]))
        for a in range(2)
    ]

    def one(j, _):
        for west in (True, False):

            @pl.when(lev_at == 0 if west else lev_at > 0)
            def _(west=west):
                for f in range(fields):
                    back = (2 * LANES + (-8 if west else half - 16) - f * SLOT) % LANES
                    for v in range(2):
                        near = pltpu.roll(side_new[v, j, 8 : 8 + strip_rows, :], back, 1)
                        first = inner[j, f, v, :, 0:LANES]
                        second = inner[j, f, v, :, LANES : LANES + half]
                        if west:
                            first = jnp.where(lane < HALO, near, first)
                        else:
                            second = jnp.where(lane[:, :half] >= half - HALO, near[:, :half], second)
                        whole[j, f, v, :, 0:LANES] = first
                        whole[j, f, v, :, LANES : LANES + half] = second

        @pl.when(outer)
        def _():
            full, last = plan[j * PLAN + 2], plan[j * PLAN + 4]
            base = row_iota(32) + window
            for s in range(STEPS):
                i = base + (last if s == 0 else 0)
                kept = gaps(base + (full if s == 0 else last)) >= 0
                w = jnp.clip(BORDER - gaps(i), 0, BORDER).astype(jnp.float32) * (1.0 / BORDER)
                w = jnp.where(kept, w, 1.0)
                rest = 1.0 - w
                inside = (gaps(i) >= 1).astype(jnp.float32)
                early = (i < 3) | ((i >= SPAN // 2) & (i < SPAN - 3))
                for f in range(fields):
                    for v in range(2):
                        n = s * rim + (2 * f + v) * BWP
                        for a in range(2):
                            driving = jnp.where(
                                early, strips[j, a, n : n + 1, :], strips[j, a, n + 1 : n + 2, :]
                            )
                            x = row_in[j, f, v, a] if s == 0 else rows_new[f, v, a]
                            rows_mixed[f, v, a, 8:40, :] = rest * x + w * driving
                for f in range(fields):
                    stay = 4.0 * lats[f] + 2.0 * vers[f]
                    value = [[rows_mixed[f, v, a, 8:40, :] for a in range(2)] for v in range(2)]
                    for v in range(2):
                        sideways = beside(value[v], first_lane, last_lane)
                        for a in range(2):
                            near = (
                                sideways[a]
                                + rows_mixed[f, v, a, 7:39, :]
                                + rows_mixed[f, v, a, 9:41, :]
                            )
                            change = (
                                lats[f] * near + vers[f] * value[1 - v][a] - stay * value[v][a]
                            )
                            rows_new[f, v, a] = value[v][a] + inside * change
            for f in range(fields):
                for v in range(2):
                    target = pl.ds(row_start, 16)
                    whole[j, f, v, target, 0:LANES] = jnp.where(
                        near_row[0], rows_new[f, v, 0, 8:24, :], whole[j, f, v, target, 0:LANES]
                    )
                    whole[j, f, v, target, LANES : LANES + half] = jnp.where(
                        near_row[1][:, :half],
                        rows_new[f, v, 1, 8:24, 0:half],
                        whole[j, f, v, target, LANES : LANES + half],
                    )

        pltpu.make_async_copy(whole.at[j], nest_out.at[j], done.at[j]).start()
        return 0

    lax.fori_loop(0, slot_count, one, 0)

    def wait(j, _):
        pltpu.make_async_copy(whole.at[j], nest_out.at[j], done.at[j]).wait()
        return 0

    lax.fori_loop(0, slot_count, wait, 0)


def per_device(parent_field, nest_fields, lateral_rate, vertical_rate, centres, slot_storm):
    fields, _, rows, cols = parent_field.shape
    slot_count, _, _, strip_rows, strip_cols = nest_fields.shape
    storms = slot_storm.shape[0]
    tiles, groups, levs = lax.axis_size("tile"), lax.axis_size("nest"), lax.axis_size("lev")
    planes = 2 * fields
    rim = planes * BWP
    share = storms * STEPS * rim
    own = slot_count * STEPS * rim
    height = strip_rows + 2 * PAD
    half = strip_cols - LANES
    f32 = jnp.float32

    def shaped(*dims):
        return jax.ShapeDtypeStruct(dims, f32)

    pair_list = [(t, t ^ 1) for t in range(tiles) if t ^ 1 < tiles]
    cross_list = [(t, t - 1 if t % 2 == 0 else t + 1) for t in range(1, tiles - 1)]
    centres = jnp.swapaxes(centres, 1, 2)

    send, keep, ring, plan, rates, nests = pl.pallas_call(
        lambda *refs: strips_kernel(fields, rows, cols, storms, slot_count, *refs),
        in_specs=[HBM_SPEC] * 6,
        out_specs=[VMEM_SPEC] * 3 + [SMEM_SPEC] + [VMEM_SPEC] * 2,
        out_shape=[
            shaped(2 * share + 2 * rim, LANES),
            shaped(2 * share, LANES),
            shaped(planes, cols, LANES),
            jax.ShapeDtypeStruct((slot_count * PLAN,), jnp.int32),
            shaped(2 * fields, LANES),
            shaped(*nest_fields.shape),
        ],
        scratch_shapes=[pltpu.VMEM((planes, 2, rows + 16, LANES), f32)] * 3
        + [pltpu.VMEM((planes, cols + 16, LANES), f32)] * 3
        + [
            pltpu.VMEM((LANES, LANES), f32),
            pltpu.VMEM((2, 24, LANES), f32),
            pltpu.SMEM(centres.shape, jnp.int32),
            pltpu.SMEM(slot_storm.shape, jnp.int32),
            pltpu.SMEM(lateral_rate.shape, f32),
            pltpu.SMEM(vertical_rate.shape, f32),
            pltpu.VMEM(parent_field.shape, f32),
            pltpu.SemaphoreType.DMA((6,)),
        ],
        compiler_params=params(),
        name="strips",
    )(
        *(
            pltpu.with_memory_space_constraint(x, pltpu.HBM)
            for x in (centres, slot_storm, lateral_rate, vertical_rate, parent_field, nest_fields)
        )
    )
    got = lax.ppermute(send, "lev", [(l, l ^ 1) for l in range(levs)])

    bundles = -(-slot_count * planes // 8)
    packed = pl.pallas_call(
        lambda *refs: edge_cols_kernel(fields, slot_count, *refs),
        in_specs=[VMEM_SPEC, ANY_SPEC],
        out_specs=VMEM_SPEC,
        out_shape=shaped(bundles, strip_rows, LANES),
        scratch_shapes=[pltpu.VMEM((8, strip_rows, LANES), f32)],
        compiler_params=params(),
        name="edge_cols",
    )(nests, keep)
    packed = lax.ppermute(packed, "lev", [(l, l ^ 1) for l in range(levs)])

    kept, *sends = pl.pallas_call(
        lambda *refs: pair_up_kernel(own, share, rim, *refs),
        in_specs=[VMEM_SPEC] * 2,
        out_specs=[VMEM_SPEC] * groups,
        out_shape=[shaped(2 * own, LANES)] + [shaped(2 * own + rim, LANES)] * (groups - 1),
        compiler_params=params(),
        name="pair_up",
    )(keep, got)
    nest_gots = [
        lax.ppermute(x, "nest", [(n, n ^ (i + 1)) for n in range(groups)])
        for i, x in enumerate(sends)
    ]

    edge_lines = (3 * fields * slot_count + bundles) * HALO
    to_pair, to_cross = pl.pallas_call(
        lambda *refs: edge_rows_kernel(fields, strip_rows, slot_count, *refs),
        in_specs=[VMEM_SPEC] * 2 + [ANY_SPEC],
        out_specs=[VMEM_SPEC] * 2,
        out_shape=[shaped(edge_lines, LANES)] * 2,
        compiler_params=params(),
        name="edge_rows",
    )(nests, packed, kept)
    pair = lax.ppermute(to_pair, "tile", pair_list)
    cross = lax.ppermute(to_cross, "tile", cross_list)

    moved = pl.pallas_call(
        lambda *refs: shift_kernel(fields, strip_rows, strip_cols, slot_count, *refs),
        in_specs=[SMEM_SPEC] + [VMEM_SPEC] * 2,
        out_specs=VMEM_SPEC,
        out_shape=shaped(slot_count, fields, 2, 2, strip_rows + 16, LANES),
        scratch_shapes=[pltpu.VMEM((fields, 2, 2, strip_rows + 48, LANES), f32)],
        compiler_params=params(),
        cost_estimate=pl.CostEstimate(flops=3_000_000_000, bytes_accessed=10_000_000, transcendentals=0),
        name="shift",
    )(plan, nests, packed)

    def holds(source, dest):
        low = max((strip_rows // 3) * dest - 3, 0)
        high = tiles * rows - FP + min((strip_rows // 3) * (dest + 1) + 3, FP)
        return rows * source - RING < high and rows * (source + 1) + RING > low

    routes = {}
    for k in range(1, tiles):
        pairs = [
            (t, t ^ k)
            for t in range(tiles)
            if t ^ k < tiles and (holds(t, t ^ k) or holds(t ^ k, t) or abs(t - (t ^ k)) == 1)
        ]
        if pairs:
            routes[k] = pairs
    touching = tuple(k for k in routes if any(abs(a - b) == 1 for a, b in routes[k]))
    moves = (0, *routes)
    fits = slot_count * SLIM <= LANES and strip_rows // 3 + 6 <= SLIM
    slims = tuple(
        k for k in routes if fits and not any(b in (0, tiles - 1) for _, b in routes[k])
    )

    def message(k):
        if k == 0:
            return own
        if k not in touching:
            return own + rim + 8
        return (STEPS * rim if k in slims else own) + rim

    zone_shapes = [shaped(message(k), LANES) for k in moves]
    partial, zone_self, *zone_sends = pl.pallas_call(
        lambda *refs: aim_kernel(
            fields, rows, cols, strip_rows, strip_cols, slot_count, moves, share, touching, slims, *refs
        ),
        in_specs=[SMEM_SPEC] + [VMEM_SPEC] * (2 + groups) + [ANY_SPEC],
        out_specs=[VMEM_SPEC] * (1 + len(moves)),
        out_shape=[shaped(fields, 2, rows, cols), *zone_shapes],
        scratch_shapes=[pltpu.VMEM((2 * own, LANES), f32)],
        compiler_params=params(),
        name="aim",
    )(plan, ring, got, kept, *nest_gots, moved)
    zone_gots = [lax.ppermute(x, "tile", routes[k]) for k, x in zip(moves[1:], zone_sends)]

    inner, side_in, row_in = pl.pallas_call(
        lambda *refs: advance_kernel(fields, strip_rows, strip_cols, slot_count, *refs),
        in_specs=[SMEM_SPEC] + [VMEM_SPEC] * 4,
        out_specs=[VMEM_SPEC] * 3,
        out_shape=[
            shaped(*nest_fields.shape),
            shaped(2, slot_count, strip_rows + 16, LANES),
            shaped(slot_count, fields, 2, 2, 32, LANES),
        ],
        scratch_shapes=[
            pltpu.VMEM((fields, 2, 2, strip_rows + 2 * FRAME, LANES), f32),
            pltpu.VMEM((fields, 2, 2, strip_rows + 32, LANES), f32),
        ],
        compiler_params=params(),
        name="advance",
    )(plan, rates, moved, pair, cross)

    nest_final, parent_final = pl.pallas_call(
        lambda *refs: settle_kernel(
            fields, strip_rows, strip_cols, rows, slot_count, moves, touching, slims, *refs
        ),
        in_specs=[SMEM_SPEC] + [VMEM_SPEC] * (5 + len(moves)),
        out_specs=[ANY_SPEC, VMEM_SPEC],
        out_shape=[shaped(*nest_fields.shape), shaped(*parent_field.shape)],
        scratch_shapes=[
            pltpu.VMEM((LANES, LANES), f32),
            pltpu.VMEM((LANES, LANES), f32),
            pltpu.VMEM((LANES, LANES), f32),
            pltpu.VMEM((slot_count, 3, STEPS * rim, LANES), f32),
            pltpu.VMEM((2, slot_count, strip_rows + 16, LANES), f32),
            pltpu.VMEM((2, slot_count, strip_rows + 32, LANES), f32),
            pltpu.VMEM((fields, 2, 2, 48, LANES), f32),
            pltpu.VMEM((fields, 2, 2, 32, LANES), f32),
            pltpu.VMEM((slot_count, fields, 2, strip_rows, strip_cols), f32),
            pltpu.SemaphoreType.DMA((slot_count,)),
        ],
        compiler_params=params(),
        name="settle",
    )(
        plan, rates, inner, side_in, row_in, partial, zone_self, *zone_gots,
    )
    return (parent_final, nest_final)


def solution(mesh):
    placed = (
        P("member", None, "tile", ("nest", "lev")),
        P(("member", "nest"), None, None, "tile", "lev"),
        P(),
        P(),
        P("member", None, None),
        P("member"),
    )
    return jax.shard_map(
        per_device,
        mesh=mesh,
        in_specs=placed,
        out_specs=(
            P("member", None, "tile", ("nest", "lev")),
            P(("member", "nest"), None, None, "tile", "lev"),
        ),
        check_vma=False,
    )
```
